32 devices in a mesh: dp: 2 (over y), ctx: 4 (over z), mp: 4 (over x, core).
Axes of the slice: x: 2, y: 2, z: 4, core: 2. Of those that a mesh axis runs over, the one named last changes fastest.
Arguments:
- tokens_in: bfloat16 [2, 2, 1024, 2048], P(None, 'dp', 'ctx', 'mp'), may hold values from -6 to 6
- out_grad: bfloat16 [2, 2, 1024, 2048], P(None, 'dp', 'ctx', 'mp'), may hold values from -6 to 6
- segment_ids: int32 [2, 2, 1024], P(None, 'dp', 'ctx'), may hold values from 0 to 18, as said below
- w_query: bfloat16 [2048, 2048], P(('dp', 'ctx'), 'mp'), may hold values from -0.1875 to 0.1875
- w_key: bfloat16 [2048, 2048], P(('dp', 'ctx'), 'mp'), may hold values from -0.1875 to 0.1875
- w_value: bfloat16 [2048, 2048], P(('dp', 'ctx'), 'mp'), may hold values from -0.125 to 0.125
- w_out: bfloat16 [2048, 2048], P('mp', ('dp', 'ctx')), may hold values from -0.5 to 0.5
- w_gate: bfloat16 [2048, 8192], P(('dp', 'ctx'), 'mp'), may hold values from -0.125 to 0.125
- w_up: bfloat16 [2048, 8192], P(('dp', 'ctx'), 'mp'), may hold values from -0.125 to 0.125
- w_down: bfloat16 [8192, 2048], P('mp', ('dp', 'ctx')), may hold values from -0.0625 to 0.0625
Outputs:
- tokens_out: bfloat16 [2, 2, 1024, 2048], P(None, 'dp', 'ctx', 'mp')
- grad_in: float32 [2, 2, 1024, 2048], P(None, 'dp', 'ctx', 'mp')
- grad_w_query: float32 [2048, 2048], P(('dp', 'ctx'), 'mp')
- grad_w_key: float32 [2048, 2048], P(('dp', 'ctx'), 'mp')
- grad_w_value: float32 [2048, 2048], P(('dp', 'ctx'), 'mp')
- grad_w_out: float32 [2048, 2048], P('mp', ('dp', 'ctx'))
- grad_w_gate: float32 [2048, 8192], P(('dp', 'ctx'), 'mp')
- grad_w_up: float32 [2048, 8192], P(('dp', 'ctx'), 'mp')
- grad_w_down: float32 [8192, 2048], P('mp', ('dp', 'ctx'))
The draws below stay inside these ranges and needn't reach their ends.
Inputs may be any that keep to these rules, and one draw needn't show every extreme that they name: `segment_ids`: sequences fall into groups: sequence s of every micro-batch belongs to group s. In each group, one of its 2 sequences over all micro-batches, drawn from the seed, is a single document numbered 1 over all 1024 tokens. Every other sequence holds documents numbered 1, 2, 3 and so on in order, each of 60 to 800 tokens except the last one, which may be cut short, followed by 1 to 128 padding tokens numbered 0. In the first group, the sequence that follows the single-document one (counting micro-batch by micro-batch, cyclically within the group) holds documents of exactly 60 tokens, the last one cut short, and one padding token.
All inputs are finite; a program needn't handle non-finite values.
Results may differ from the reference program's by a relative error of at most 0.018.
Values may be sent and summed in bfloat16 or wider, within the bound.
A program may use at most 256 MiB of HBM per device.

```python
import math
import jax
import jax.numpy as jnp
from jax import lax

D = 2048
H = 16
HD = 128
FF = 8192
SPAN = 256
SEQ_DP = 1
MB = 2
MINDOC = 60
MAXDOC = 800
SEQ = 1024
SEQS = 2


def draw_segment_ids(key, part):
    key = jax.random.fold_in(key, 11)
    key_lengths, key_padding, key_pick = jax.random.split(key, 3)
    sequences = MB * SEQS
    most_docs = SEQ // MINDOC + 1
    group_size = MB * SEQ_DP
    picked = jax.random.randint(key_pick, (SEQS // SEQ_DP,), 0, group_size)
    rows = jnp.arange(sequences, dtype=jnp.int32)
    micro = rows // SEQS
    within = rows % SEQS
    group = within // SEQ_DP
    slot = micro * SEQ_DP + within % SEQ_DP
    single = (slot == picked[group])[:, None]
    is_dense = ((group == 0) & (slot == (picked[0] + 1) % group_size))[:, None]
    lengths = jax.random.randint(key_lengths, (sequences, most_docs), MINDOC, MAXDOC + 1)
    lengths = jnp.where(is_dense, MINDOC, lengths)
    endings = jnp.cumsum(lengths, axis=1)
    places = jnp.arange(SEQ, dtype=jnp.int32)
    numbers = 1 + jnp.sum((places[None, :, None] >= endings[:, None, :]).astype(jnp.int32), axis=2)
    padding = jax.random.randint(key_padding, (sequences, 1), 1, SPAN // 2 + 1)
    padding = jnp.where(is_dense, 1, padding)
    numbers = jnp.where(places[None, :] >= SEQ - padding, 0, numbers)
    numbers = jnp.where(single, 1, numbers)
    return numbers.reshape(MB, SEQS, SEQ).astype(jnp.int32)


def level_of(rng, shape, shards, least, high):
    def one(position, blocks):
        steps = jax.random.uniform(jax.random.fold_in(jax.random.fold_in(rng, 6), position), (blocks,), jnp.float32, least / len(shards), high / len(shards))
        return jnp.repeat(jnp.exp(steps), shape[position] // blocks).reshape((-1,) + (1,) * (len(shape) - position - 1))

    factor_of = one(*shards[0])
    for cut in shards[1:]:
        factor_of = factor_of * one(*cut)
    return factor_of


def scatter_about(key, shape, scale, limit, cuts=(), kind=jnp.bfloat16):
    result = jax.random.normal(key, shape, jnp.float32) * scale
    if len(cuts) > 0:
        result = level_of(key, shape, cuts, -0.22, 0.18) * result
    return jnp.clip(result, min=-limit, max=limit).astype(kind)


def setup_inputs(seed: int = 0) -> dict:
    streams_of = jax.random.split(jax.random.key(seed), 11)
    tokens_in = scatter_about(streams_of[0], (MB, SEQS, SEQ, D), 1.0, 6.0, ((1, 2), (2, 4), (3, 4)))
    out_grad = scatter_about(streams_of[1], (MB, SEQS, SEQ, D), 1.0, 6.0, ((1, 2), (2, 4), (3, 4)))
    segment_ids = draw_segment_ids(jax.random.fold_in(streams_of[10], 71), 0)
    w_query = scatter_about(streams_of[3], (D, H * HD), (D // 2) ** -0.5, 0.1875, ((0, 8), (1, 4)))
    w_key = scatter_about(streams_of[4], (D, H * HD), (D // 2) ** -0.5, 0.1875, ((0, 8), (1, 4)))
    w_value = scatter_about(streams_of[5], (D, H * HD), D ** -0.5, 0.125, ((0, 8), (1, 4)))
    w_out = scatter_about(streams_of[6], (H * HD, D), (H * HD // 16) ** -0.5, 0.5, ((0, 4), (1, 8)))
    w_gate = scatter_about(streams_of[7], (D, FF), D ** -0.5, 0.125, ((0, 8), (1, 4)))
    w_up = scatter_about(streams_of[8], (D, FF), D ** -0.5, 0.125, ((0, 8), (1, 4)))
    w_down = scatter_about(streams_of[9], (FF, D), FF ** -0.5, 0.0625, ((0, 4), (1, 8)))
    return dict(tokens_in=tokens_in, out_grad=out_grad, segment_ids=segment_ids, w_query=w_query, w_key=w_key, w_value=w_value, w_out=w_out, w_gate=w_gate, w_up=w_up, w_down=w_down)


EPSILON = 1e-05
NEG_FILL = -1e+30
PRECISE = lax.Precision.HIGHEST

@jax.custom_vjp
def low(v):
    return lax.optimization_barrier(v.astype(jnp.bfloat16)).astype(jnp.float32)

@jax.custom_vjp
def low_back(v):
    return v

def low_keep(v):
    return (low(v), None)

def low_pass(kept, grad):
    return (grad,)

def back_keep(v):
    return (v, None)

def back_low(kept, grad):
    return (low(grad),)
low.defvjp(low_keep, low_pass)
low_back.defvjp(back_keep, back_low)

def layer_norm(values):
    centred = values - lax.optimization_barrier(jnp.mean(values, axis=-1, keepdims=True))
    return centred * lax.rsqrt(lax.optimization_barrier(jnp.mean(centred * centred, axis=-1, keepdims=True)) + EPSILON)

def doc_positions(segment):
    length = segment.shape[-1]
    places = jnp.arange(length, dtype=jnp.int32)
    opening = jnp.ones(segment.shape[:-1] + (1,), dtype=bool)
    change = jnp.concatenate([opening, segment[..., 1:] != segment[..., :-1]], axis=-1)
    starts = lax.cummax(jnp.where(change, places, jnp.int32(0)), axis=segment.ndim - 1)
    return places - starts

def rope_angles(positions):
    freq_table = jnp.power(10000.0, -2.0 * jnp.arange(HD // 2, dtype=jnp.float32) / HD)
    turned = positions.astype(jnp.float32)[..., None] * freq_table
    return (jnp.cos(turned), jnp.sin(turned))

def rope_turn(values, cosine, sine_part):
    half_size = values.shape[-1] // 2
    leading = values[..., :half_size]
    trailing = values[..., half_size:]
    return jnp.concatenate([leading * cosine - trailing * sine_part, trailing * cosine + leading * sine_part], axis=-1)

def one_sequence(tokens, segment, weights):
    w_query, w_key, w_value, w_out, w_gate, w_up, w_down = weights
    length = tokens.shape[0]
    head_count = w_query.shape[1] // HD
    places = jnp.arange(length, dtype=jnp.int32)
    allowed = (segment[:, None] == segment[None, :]) & (places[None, :] <= places[:, None])
    cosine, sine_part = rope_angles(doc_positions(segment))
    cosine = cosine[:, None, :]
    sine_part = sine_part[:, None, :]
    normed = low(layer_norm(tokens))

    def project(matrix):
        return low_back(jnp.dot(normed, matrix, precision=PRECISE)).reshape(length, head_count, HD)
    queries = low(rope_turn(project(w_query), cosine, sine_part))
    keys_all = low(rope_turn(project(w_key), cosine, sine_part))
    values_all = low(project(w_value))
    scores = jnp.einsum('qhd,khd->hqk', queries, keys_all, precision=PRECISE) * (1.0 / math.sqrt(HD))
    scores = jnp.where(allowed[None], low_back(scores), NEG_FILL)
    soft_weights = low(jax.nn.softmax(scores, axis=-1))
    mixed_heads = jnp.einsum('hqk,khd->qhd', soft_weights, values_all, precision=PRECISE)
    mixed_heads = low(low_back(mixed_heads)).reshape(length, head_count * HD)
    branch = low_back(jnp.dot(mixed_heads, w_out, precision=PRECISE))
    residual = tokens + branch
    normed_two = low(layer_norm(residual))
    gate_lin = low_back(jnp.dot(normed_two, w_gate, precision=PRECISE))
    up_lin = low_back(jnp.dot(normed_two, w_up, precision=PRECISE))
    hidden = low(jax.nn.silu(gate_lin) * up_lin)
    return residual + low_back(jnp.dot(hidden, w_down, precision=PRECISE))

def reference(tokens_in, out_grad, segment_ids, w_query, w_key, w_value, w_out, w_gate, w_up, w_down):
    full_shape = tokens_in.shape
    flat_tokens = tokens_in.astype(jnp.float32).reshape(-1, full_shape[2], full_shape[3])
    flat_segments = segment_ids.reshape(-1, full_shape[2])
    float_weights = tuple((matrix.astype(jnp.float32) for matrix in (w_query, w_key, w_value, w_out, w_gate, w_up, w_down)))

    def forward(tokens, weights):

        def one_step(step_args):
            return one_sequence(step_args[0], step_args[1], weights)
        return lax.map(jax.checkpoint(one_step), (tokens, flat_segments))
    outputs, pullback = jax.vjp(forward, flat_tokens, float_weights)
    cotangent = out_grad.astype(jnp.float32).reshape(flat_tokens.shape)
    grad_tokens, grad_weights = pullback(cotangent)
    return (outputs.reshape(full_shape).astype(jnp.bfloat16), grad_tokens.reshape(full_shape), grad_weights[0], grad_weights[1], grad_weights[2], grad_weights[3], grad_weights[4], grad_weights[5], grad_weights[6])
```

```python
import math

import jax
import jax.numpy as jnp
from jax import lax
from jax.sharding import PartitionSpec as P

HD = 128


EPSILON = 1e-05
NEG_FILL = -1e30


def layer_norm(values):
    centred = values - jnp.mean(values, axis=-1, keepdims=True)
    inverse = lax.rsqrt(jnp.mean(centred * centred, axis=-1, keepdims=True) + EPSILON)
    return (centred * inverse, inverse)


def norm_backward(upstream, normed, inverse):
    plain_mean = jnp.mean(upstream, axis=-1, keepdims=True)
    cross_mean = jnp.mean(upstream * normed, axis=-1, keepdims=True)
    return inverse * (upstream - plain_mean - normed * cross_mean)


def doc_positions(segment):
    length = segment.shape[-1]
    places = jnp.arange(length, dtype=jnp.int32)
    opening = jnp.ones(segment.shape[:-1] + (1,), dtype=bool)
    change = jnp.concatenate([opening, segment[..., 1:] != segment[..., :-1]], axis=-1)
    starts = lax.cummax(jnp.where(change, places, jnp.int32(0)), axis=segment.ndim - 1)
    return places - starts


def rope_angles(positions):
    freq_table = jnp.power(10000.0, -2.0 * jnp.arange(HD // 2, dtype=jnp.float32) / HD)
    turned = positions.astype(jnp.float32)[..., None] * freq_table
    return (jnp.cos(turned), jnp.sin(turned))


def rope_turn(values, cosine, sine_part):
    half_size = values.shape[-1] // 2
    leading = values[..., :half_size]
    trailing = values[..., half_size:]
    return jnp.concatenate(
        [leading * cosine - trailing * sine_part, trailing * cosine + leading * sine_part], axis=-1
    )


def dot_rows(left_mat, right_mat):
    return lax.dot_general(
        left_mat, right_mat, (((1,), (1,)), ((), ())), preferred_element_type=jnp.float32
    )


def dot_cols(left_mat, right_mat):
    return lax.dot_general(
        left_mat, right_mat, (((0,), (0,)), ((), ())), preferred_element_type=jnp.float32
    )


def fetch_weights(w_query, w_key, w_value, w_gate, w_up, w_out, w_down):
    return (
        lax.all_gather(w_query, ("dp", "ctx"), axis=0, tiled=True),
        lax.all_gather(w_key, ("dp", "ctx"), axis=0, tiled=True),
        lax.all_gather(w_value, ("dp", "ctx"), axis=0, tiled=True),
        lax.all_gather(w_gate, ("dp", "ctx"), axis=0, tiled=True),
        lax.all_gather(w_up, ("dp", "ctx"), axis=0, tiled=True),
        lax.all_gather(w_out, ("dp", "ctx"), axis=1, tiled=True),
        lax.all_gather(w_down, ("dp", "ctx"), axis=1, tiled=True),
    )


def per_device_general(
    tokens_in, out_grad, segment_ids, w_query, w_key, w_value, w_out, w_gate, w_up, w_down
):
    micro_count = tokens_in.shape[0]
    seq_local = tokens_in.shape[1]
    span_len = tokens_in.shape[2]
    local_width = tokens_in.shape[3]
    ctx_index = lax.axis_index("ctx")
    model_index = lax.axis_index("mp")
    tokens_all, grads_all = (
        lax.all_gather(tokens_in, "mp", axis=3, tiled=True),
        lax.all_gather(out_grad, "mp", axis=3, tiled=True),
    )
    segments_all = lax.all_gather(segment_ids, "ctx", axis=2, tiled=True)
    feature_width = tokens_all.shape[3]
    seq_length = segments_all.shape[2]
    row_count = seq_local * span_len
    score_scale = 1.0 / math.sqrt(HD)
    positions = doc_positions(segments_all)
    query_places = ctx_index * span_len + jnp.arange(span_len, dtype=jnp.int32)
    key_places = jnp.arange(seq_length, dtype=jnp.int32)
    causal = key_places[None, :] <= query_places[:, None]
    outputs = []
    input_grads = []
    totals = None
    for micro_step in range(micro_count):
        full_weights = fetch_weights(w_query, w_key, w_value, w_gate, w_up, w_out, w_down)
        query_full, key_full, value_full, gate_full, up_full, out_full, down_full = full_weights
        head_count = query_full.shape[1] // HD
        segment_seq = segments_all[micro_step]
        segment_own = lax.dynamic_slice_in_dim(segment_seq, ctx_index * span_len, span_len, 1)
        position_own = lax.dynamic_slice_in_dim(
            positions[micro_step], ctx_index * span_len, span_len, 1
        )
        allowed = (segment_own[:, :, None] == segment_seq[:, None, :]) & causal[None]
        cosine, sine_part = rope_angles(position_own)
        cosine = cosine[:, :, None, :]
        sine_part = sine_part[:, :, None, :]
        inputs = tokens_all[micro_step].astype(jnp.float32)
        normed, inverse_one = layer_norm(inputs)
        normed_low = normed.astype(jnp.bfloat16).reshape(row_count, feature_width)

        def project(matrix):
            product = jnp.dot(normed_low, matrix, preferred_element_type=jnp.float32)
            return product.reshape(seq_local, span_len, head_count, HD)

        query_low = (
            rope_turn(project(query_full), cosine, sine_part)
            .astype(jnp.bfloat16)
            .reshape(seq_local, span_len, head_count * HD)
        )
        key_low = (
            rope_turn(project(key_full), cosine, sine_part)
            .astype(jnp.bfloat16)
            .reshape(seq_local, span_len, head_count * HD)
        )
        value_low = (
            project(value_full).astype(jnp.bfloat16).reshape(seq_local, span_len, head_count * HD)
        )
        key_seq, value_seq = (
            lax.all_gather(key_low, "ctx", axis=1, tiled=True),
            lax.all_gather(value_low, "ctx", axis=1, tiled=True),
        )
        mixed_parts = []
        log_totals = []
        for head_index in range(head_count):
            head_cols = slice(head_index * HD, (head_index + 1) * HD)
            scores = (
                jnp.einsum(
                    "sqd,skd->sqk",
                    query_low[..., head_cols],
                    key_seq[..., head_cols],
                    preferred_element_type=jnp.float32,
                )
                * score_scale
            )
            scores = jnp.where(allowed, scores, NEG_FILL)
            highest = jnp.max(scores, axis=-1, keepdims=True)
            exp_terms = jnp.exp(scores - highest)
            total_exp = jnp.sum(exp_terms, axis=-1, keepdims=True)
            probs_low = (exp_terms / total_exp).astype(jnp.bfloat16)
            mixed_parts.append(
                jnp.einsum(
                    "sqk,skd->sqd",
                    probs_low,
                    value_seq[..., head_cols],
                    preferred_element_type=jnp.float32,
                )
            )
            log_totals.append(highest + jnp.log(total_exp))
        mixed_low = (
            jnp.concatenate(mixed_parts, axis=-1)
            .astype(jnp.bfloat16)
            .reshape(row_count, head_count * HD)
        )
        branch = jnp.dot(mixed_low, out_full, preferred_element_type=jnp.float32)
        branch = lax.psum(branch, "mp")
        residual = inputs + branch.reshape(seq_local, span_len, feature_width)
        normed_two, inverse_two = layer_norm(residual)
        second_low = normed_two.astype(jnp.bfloat16).reshape(row_count, feature_width)
        gate_lin = jnp.dot(second_low, gate_full, preferred_element_type=jnp.float32)
        up_lin = jnp.dot(second_low, up_full, preferred_element_type=jnp.float32)
        sigmoid_gate = jax.nn.sigmoid(gate_lin)
        hidden_low = (gate_lin * sigmoid_gate * up_lin).astype(jnp.bfloat16)
        feed_terms = jnp.dot(hidden_low, down_full, preferred_element_type=jnp.float32).reshape(
            seq_local, span_len, feature_width
        )
        feed_own = lax.psum_scatter(
            feed_terms.astype(jnp.bfloat16), "mp", scatter_dimension=2, tiled=True
        ).astype(jnp.float32)
        residual_own = lax.dynamic_slice_in_dim(residual, model_index * local_width, local_width, 2)
        outputs.append((residual_own + feed_own).astype(jnp.bfloat16))
        back_weights = (
            lax.all_gather(w_query, ("dp", "ctx"), axis=0, tiled=True),
            lax.all_gather(w_key, ("dp", "ctx"), axis=0, tiled=True),
            lax.all_gather(w_value, ("dp", "ctx"), axis=0, tiled=True),
            lax.all_gather(w_gate, ("dp", "ctx"), axis=0, tiled=True),
            lax.all_gather(w_up, ("dp", "ctx"), axis=0, tiled=True),
            lax.all_gather(w_out, ("dp", "ctx"), axis=1, tiled=True),
            lax.all_gather(w_down, ("dp", "ctx"), axis=1, tiled=True),
        )
        key_back, value_back = (
            lax.all_gather(key_low, "ctx", axis=1, tiled=True),
            lax.all_gather(value_low, "ctx", axis=1, tiled=True),
        )
        query_back, key_mat, value_mat, gate_back, up_back, out_back, down_back = back_weights
        grad_low = grads_all[micro_step].reshape(row_count, feature_width)
        grad_float = grads_all[micro_step].astype(jnp.float32)
        hidden_grad = dot_rows(grad_low, down_back)
        gate_grad = (
            hidden_grad * up_lin * sigmoid_gate * (1.0 + gate_lin * (1.0 - sigmoid_gate))
        ).astype(jnp.bfloat16)
        up_grad = (hidden_grad * gate_lin * sigmoid_gate).astype(jnp.bfloat16)
        normed_grad = dot_rows(gate_grad, gate_back) + dot_rows(up_grad, up_back)
        normed_grad = lax.psum(normed_grad, "mp").reshape(seq_local, span_len, feature_width)
        residual_grad = grad_float + norm_backward(normed_grad, normed_two, inverse_two)
        residual_low = residual_grad.astype(jnp.bfloat16).reshape(row_count, feature_width)
        mixed_grad = (
            dot_rows(residual_low, out_back)
            .astype(jnp.bfloat16)
            .reshape(seq_local, span_len, head_count * HD)
        )
        query_parts = []
        key_parts = []
        value_parts = []
        for head_index in range(head_count):
            head_cols = slice(head_index * HD, (head_index + 1) * HD)
            query_head = query_low[..., head_cols]
            key_head = key_back[..., head_cols]
            mixed_head = mixed_grad[..., head_cols]
            scores = (
                jnp.einsum("sqd,skd->sqk", query_head, key_head, preferred_element_type=jnp.float32)
                * score_scale
            )
            scores = jnp.where(allowed, scores, NEG_FILL)
            probs = jnp.exp(scores - log_totals[head_index])
            probs_low = probs.astype(jnp.bfloat16)
            value_parts.append(
                jnp.einsum(
                    "sqk,sqd->skd", probs_low, mixed_head, preferred_element_type=jnp.float32
                )
            )
            probs_grad = jnp.einsum(
                "sqd,skd->sqk",
                mixed_head,
                value_back[..., head_cols],
                preferred_element_type=jnp.float32,
            )
            row_dot = jnp.sum(probs * probs_grad, axis=-1, keepdims=True)
            scores_grad = (probs * (probs_grad - row_dot)).astype(jnp.bfloat16)
            query_parts.append(
                jnp.einsum(
                    "sqk,skd->sqd", scores_grad, key_head, preferred_element_type=jnp.float32
                )
                * score_scale
            )
            key_parts.append(
                jnp.einsum(
                    "sqk,sqd->skd", scores_grad, query_head, preferred_element_type=jnp.float32
                )
                * score_scale
            )
        key_terms = jnp.concatenate(key_parts, axis=-1)
        value_terms = jnp.concatenate(value_parts, axis=-1)
        key_grad_own, value_grad_own = (
            lax.psum_scatter(key_terms, "ctx", scatter_dimension=1, tiled=True),
            lax.psum_scatter(value_terms, "ctx", scatter_dimension=1, tiled=True),
        )
        query_sum = jnp.concatenate(query_parts, axis=-1).reshape(
            seq_local, span_len, head_count, HD
        )
        query_grad = (
            rope_turn(query_sum, cosine, -sine_part)
            .astype(jnp.bfloat16)
            .reshape(row_count, head_count * HD)
        )
        key_grad = (
            rope_turn(key_grad_own.reshape(seq_local, span_len, head_count, HD), cosine, -sine_part)
            .astype(jnp.bfloat16)
            .reshape(row_count, head_count * HD)
        )
        value_grad = value_grad_own.astype(jnp.bfloat16).reshape(row_count, head_count * HD)
        input_terms = (
            dot_rows(query_grad, query_back)
            + dot_rows(key_grad, key_mat)
            + dot_rows(value_grad, value_mat)
        )
        input_sum = (
            lax.psum(input_terms.astype(jnp.bfloat16), "mp")
            .astype(jnp.float32)
            .reshape(seq_local, span_len, feature_width)
        )
        grad_whole = residual_grad + norm_backward(input_sum, normed, inverse_one)
        input_grads.append(
            lax.dynamic_slice_in_dim(grad_whole, model_index * local_width, local_width, 2)
        )
        new_terms = (
            dot_cols(normed_low, query_grad),
            dot_cols(normed_low, key_grad),
            dot_cols(normed_low, value_grad),
            dot_cols(second_low, gate_grad),
            dot_cols(second_low, up_grad),
            dot_cols(mixed_low, residual_low),
            dot_cols(hidden_low, grad_low),
        )
        if totals is None:
            totals = new_terms
        else:
            totals = tuple((older + newer for older, newer in zip(totals, new_terms)))
    grads_total = (
        lax.psum_scatter(
            totals[0].astype(jnp.bfloat16), ("dp", "ctx"), scatter_dimension=0, tiled=True
        ).astype(jnp.float32),
        lax.psum_scatter(
            totals[1].astype(jnp.bfloat16), ("dp", "ctx"), scatter_dimension=0, tiled=True
        ).astype(jnp.float32),
        lax.psum_scatter(
            totals[2].astype(jnp.bfloat16), ("dp", "ctx"), scatter_dimension=0, tiled=True
        ).astype(jnp.float32),
        lax.psum_scatter(
            totals[3].astype(jnp.bfloat16), ("dp", "ctx"), scatter_dimension=0, tiled=True
        ).astype(jnp.float32),
        lax.psum_scatter(
            totals[4].astype(jnp.bfloat16), ("dp", "ctx"), scatter_dimension=0, tiled=True
        ).astype(jnp.float32),
        lax.psum_scatter(
            totals[5].astype(jnp.bfloat16), ("dp", "ctx"), scatter_dimension=1, tiled=True
        ).astype(jnp.float32),
        lax.psum_scatter(
            totals[6].astype(jnp.bfloat16), ("dp", "ctx"), scatter_dimension=1, tiled=True
        ).astype(jnp.float32),
    )
    return (
        jnp.stack(outputs, axis=0),
        jnp.stack(input_grads, axis=0),
        grads_total[0],
        grads_total[1],
        grads_total[2],
        grads_total[5],
        grads_total[3],
        grads_total[4],
        grads_total[6],
    )


def xor_permute(values, axis, size, mask):
    return lax.ppermute(values, axis, [(place, place ^ mask) for place in range(size)])


def pick_blocks(blocks, index):
    stack = jnp.stack(blocks, axis=0)
    return [
        lax.dynamic_index_in_dim(stack, index ^ place, 0, keepdims=False)
        for place in range(len(blocks))
    ]


def token_routes(offset):
    routes = []
    for high in range(2):
        for low in range(2):
            for model in range(4):
                wanted = model ^ offset
                routes.append(
                    ((high * 2 + low) * 4 + model, ((wanted // 2) * 2 + high) * 4 + low * 2 + wanted % 2)
                )
    return routes


def to_rows(values, model_index, quarter):
    span_half = values.shape[2] // 2
    parts = values.reshape(4, span_half, values.shape[3])
    blocks = []
    for offset in range(4):
        part = lax.dynamic_index_in_dim(parts, model_index ^ offset, 0, keepdims=False)
        blocks.append(lax.ppermute(part, ("ctx", "mp"), token_routes(offset)))
    return jnp.concatenate(pick_blocks(blocks, quarter), axis=1)


def from_rows(rows, model_index, quarter):
    row_count, width = rows.shape
    parts = jnp.transpose(rows.reshape(row_count, 4, width // 4), (1, 0, 2))
    blocks = []
    for offset in range(4):
        part = lax.dynamic_index_in_dim(parts, quarter ^ offset, 0, keepdims=False)
        routes = [(target, source) for source, target in token_routes(offset)]
        blocks.append(lax.ppermute(part, ("ctx", "mp"), routes))
    return jnp.concatenate(pick_blocks(blocks, model_index), axis=0).reshape(
        2, 1, 2 * row_count, width // 4
    )


def half_of(values, axis, which):
    size = values.shape[axis] // 2
    return lax.dynamic_slice_in_dim(values, which * size, size, axis)


def fetch_stack(shards, axis, low, home):
    mine = jnp.concatenate([half_of(shard, axis, low) for shard in shards], axis=axis)
    other = jnp.concatenate([half_of(shard, axis, 1 - low) for shard in shards], axis=axis)
    near = [
        mine,
        xor_permute(other, "ctx", 4, 1),
        xor_permute(mine, "ctx", 4, 2),
        xor_permute(other, "ctx", 4, 3),
    ]
    far = [xor_permute(block, "dp", 2, 1) for block in near]
    return jnp.concatenate(pick_blocks(near + far, home), axis=1 - axis)


def return_grads(grad, axis, dp_index, high, low):
    cut = 1 - axis
    sent = half_of(grad, cut, 1 - dp_index).astype(jnp.bfloat16)
    total = half_of(grad, cut, dp_index) + xor_permute(sent, "dp", 2, 1).astype(jnp.float32)
    sent = half_of(total, cut, 1 - high).astype(jnp.bfloat16)
    total = half_of(total, cut, high) + xor_permute(sent, "ctx", 4, 2).astype(jnp.float32)
    sent = half_of(total, cut, 1 - low).astype(jnp.bfloat16)
    mine = half_of(total, cut, low)
    return mine, xor_permute(sent, "ctx", 4, 1).astype(jnp.float32)


def place_halves(mine, other, axis, low):
    first = jnp.where(low == 0, mine, other)
    second = jnp.where(low == 0, other, mine)
    return jnp.concatenate([first, second], axis=axis)


GROUPS = [[(high * 2 + low) * 4 + model for low in range(2) for model in range(4)] for high in range(2)]


def gather_rows(rows):
    return lax.all_gather(rows, ("ctx", "mp"), axis=0, tiled=True, axis_index_groups=GROUPS)


def scatter_rows(terms):
    return lax.psum_scatter(
        terms.astype(jnp.bfloat16),
        ("ctx", "mp"),
        scatter_dimension=0,
        tiled=True,
        axis_index_groups=GROUPS,
    ).astype(jnp.float32)


def per_device_grouped(
    tokens_in, out_grad, segment_ids, w_query, w_key, w_value, w_out, w_gate, w_up, w_down
):
    dp_index = lax.axis_index("dp")
    ctx_index = lax.axis_index("ctx")
    model_index = lax.axis_index("mp")
    high = ctx_index // 2
    low = ctx_index % 2
    quarter = 2 * high + model_index % 2
    home = dp_index * 4 + ctx_index
    score_scale = 1.0 / math.sqrt(HD)
    feature_width = tokens_in.shape[3] * 4

    segments_all = lax.all_gather(segment_ids, "ctx", axis=2, tiled=True)
    segment = lax.dynamic_index_in_dim(segments_all, high, 0, keepdims=False)[0]
    length = segment.shape[0]
    row_count = length // 8

    token_rows = to_rows(tokens_in, model_index, quarter).astype(jnp.float32)
    query_key_value = fetch_stack((w_query, w_key, w_value), 1, low, home)
    out_part = fetch_stack((w_out,), 0, low, home)
    grad_rows = to_rows(out_grad, model_index, quarter)
    gate_part = fetch_stack((w_gate,), 1, low, home)
    up_part = fetch_stack((w_up,), 1, low, home)
    down_part = fetch_stack((w_down,), 0, low, home)

    normed_rows, inverse_one = layer_norm(token_rows)
    normed_low = gather_rows(normed_rows.astype(jnp.bfloat16))

    places = jnp.arange(length, dtype=jnp.int32)
    allowed = (segment[:, None] == segment[None, :]) & (places[None, :] <= places[:, None])
    cosine, sine_part = rope_angles(doc_positions(segment))
    cosine = cosine[:, None, :]
    sine_part = sine_part[:, None, :]

    local_cols = query_key_value.shape[1] // 3
    head_count = local_cols // HD
    projected = jnp.dot(normed_low, query_key_value, preferred_element_type=jnp.float32)

    def turned(values, sine_used):
        return (
            rope_turn(values.reshape(length, head_count, HD), cosine, sine_used)
            .astype(jnp.bfloat16)
            .reshape(length, local_cols)
        )

    query_low = turned(projected[:, :local_cols], sine_part)
    key_low = turned(projected[:, local_cols : 2 * local_cols], sine_part)
    value_low = projected[:, 2 * local_cols :].astype(jnp.bfloat16)
    mixed_parts = []
    log_totals = []
    for head_index in range(head_count):
        cols = slice(head_index * HD, (head_index + 1) * HD)
        scores = dot_rows(query_low[:, cols], key_low[:, cols]) * score_scale
        scores = jnp.where(allowed, scores, NEG_FILL)
        highest = jnp.max(scores, axis=-1, keepdims=True)
        exp_terms = jnp.exp(scores - highest)
        total_exp = jnp.sum(exp_terms, axis=-1, keepdims=True)
        probs_low = (exp_terms / total_exp).astype(jnp.bfloat16)
        mixed_parts.append(
            jnp.dot(probs_low, value_low[:, cols], preferred_element_type=jnp.float32)
        )
        log_totals.append(highest + jnp.log(total_exp))
    mixed_low = jnp.concatenate(mixed_parts, axis=-1).astype(jnp.bfloat16)
    branch = scatter_rows(jnp.dot(mixed_low, out_part, preferred_element_type=jnp.float32))
    residual = token_rows + branch
    normed_two, inverse_two = layer_norm(residual)
    second_low = gather_rows(normed_two.astype(jnp.bfloat16))
    grad_low = gather_rows(grad_rows)
    gate_lin = jnp.dot(second_low, gate_part, preferred_element_type=jnp.float32)
    up_lin = jnp.dot(second_low, up_part, preferred_element_type=jnp.float32)
    sigmoid_gate = jax.nn.sigmoid(gate_lin)
    hidden_low = (gate_lin * sigmoid_gate * up_lin).astype(jnp.bfloat16)
    down_grads = return_grads(dot_cols(hidden_low, grad_low), 0, dp_index, high, low)
    hidden_grad = dot_rows(grad_low, down_part)
    gate_grad = (
        hidden_grad * up_lin * sigmoid_gate * (1.0 + gate_lin * (1.0 - sigmoid_gate))
    ).astype(jnp.bfloat16)
    up_grad = (hidden_grad * gate_lin * sigmoid_gate).astype(jnp.bfloat16)
    normed_grad = scatter_rows(dot_rows(gate_grad, gate_part) + dot_rows(up_grad, up_part))
    gate_grads = return_grads(dot_cols(second_low, gate_grad), 1, dp_index, high, low)
    up_grads = return_grads(dot_cols(second_low, up_grad), 1, dp_index, high, low)
    feed = scatter_rows(jnp.dot(hidden_low, down_part, preferred_element_type=jnp.float32))
    tokens_out = from_rows((residual + feed).astype(jnp.bfloat16), model_index, quarter)
    residual_grad = grad_rows.astype(jnp.float32) + norm_backward(
        normed_grad, normed_two, inverse_two
    )
    residual_low = gather_rows(residual_grad.astype(jnp.bfloat16))
    out_grads = return_grads(dot_cols(mixed_low, residual_low), 0, dp_index, high, low)
    mixed_grad = dot_rows(residual_low, out_part).astype(jnp.bfloat16)
    query_parts = []
    key_parts = []
    value_parts = []
    for head_index in range(head_count):
        cols = slice(head_index * HD, (head_index + 1) * HD)
        query_head = query_low[:, cols]
        key_head = key_low[:, cols]
        mixed_head = mixed_grad[:, cols]
        scores = dot_rows(query_head, key_head) * score_scale
        scores = jnp.where(allowed, scores, NEG_FILL)
        probs = jnp.exp(scores - log_totals[head_index])
        value_parts.append(dot_cols(probs.astype(jnp.bfloat16), mixed_head))
        probs_grad = dot_rows(mixed_head, value_low[:, cols])
        row_dot = jnp.sum(probs * probs_grad, axis=-1, keepdims=True)
        scores_grad = (probs * (probs_grad - row_dot)).astype(jnp.bfloat16)
        query_parts.append(
            jnp.dot(scores_grad, key_head, preferred_element_type=jnp.float32) * score_scale
        )
        key_parts.append(dot_cols(scores_grad, query_head) * score_scale)
    query_grad = turned(jnp.concatenate(query_parts, axis=-1), -sine_part)
    key_grad = turned(jnp.concatenate(key_parts, axis=-1), -sine_part)
    value_grad = jnp.concatenate(value_parts, axis=-1).astype(jnp.bfloat16)
    three_grad = jnp.concatenate([query_grad, key_grad, value_grad], axis=-1)
    input_sum = scatter_rows(dot_rows(three_grad, query_key_value))
    three_grads = return_grads(dot_cols(normed_low, three_grad), 1, dp_index, high, low)
    grad_in_rows = residual_grad + norm_backward(input_sum, normed_rows, inverse_one)
    grad_in = from_rows(grad_in_rows.astype(jnp.bfloat16), model_index, quarter)

    def columns(pair, which):
        cols = slice(which * local_cols, (which + 1) * local_cols)
        return place_halves(pair[0][:, cols], pair[1][:, cols], 1, low)

    return (
        tokens_out,
        grad_in.astype(jnp.float32),
        columns(three_grads, 0),
        columns(three_grads, 1),
        columns(three_grads, 2),
        place_halves(*out_grads, 0, low),
        place_halves(*gate_grads, 1, low),
        place_halves(*up_grads, 1, low),
        place_halves(*down_grads, 0, low),
    )


def solution(mesh):
    in_specs = (
        P(None, "dp", "ctx", "mp"),
        P(None, "dp", "ctx", "mp"),
        P(None, "dp", "ctx"),
        P(("dp", "ctx"), "mp"),
        P(("dp", "ctx"), "mp"),
        P(("dp", "ctx"), "mp"),
        P("mp", ("dp", "ctx")),
        P(("dp", "ctx"), "mp"),
        P(("dp", "ctx"), "mp"),
        P("mp", ("dp", "ctx")),
    )
    out_specs = (
        P(None, "dp", "ctx", "mp"),
        P(None, "dp", "ctx", "mp"),
        P(("dp", "ctx"), "mp"),
        P(("dp", "ctx"), "mp"),
        P(("dp", "ctx"), "mp"),
        P("mp", ("dp", "ctx")),
        P(("dp", "ctx"), "mp"),
        P(("dp", "ctx"), "mp"),
        P("mp", ("dp", "ctx")),
    )
    grouped = mesh.shape["ctx"] == 4 and mesh.shape["mp"] == 4 and mesh.shape["dp"] == 2
    per_device = per_device_grouped if grouped else per_device_general
    return jax.shard_map(
        per_device, mesh=mesh, in_specs=in_specs, out_specs=out_specs, check_vma=False
    )
```

```python
import math

import jax
import jax.numpy as jnp
from jax import lax
from jax.experimental import pallas as pl
from jax.experimental.pallas import tpu as pltpu
from jax.sharding import PartitionSpec as P

HD = 128


EPSILON = 1e-05
NEG_FILL = -1e30


def layer_norm(values):
    centred = values - jnp.mean(values, axis=-1, keepdims=True)
    inverse = lax.rsqrt(jnp.mean(centred * centred, axis=-1, keepdims=True) + EPSILON)
    return (centred * inverse, inverse)


def norm_backward(upstream, normed, inverse):
    plain_mean = jnp.mean(upstream, axis=-1, keepdims=True)
    cross_mean = jnp.mean(upstream * normed, axis=-1, keepdims=True)
    return inverse * (upstream - plain_mean - normed * cross_mean)


def doc_positions(segment):
    length = segment.shape[-1]
    places = jnp.arange(length, dtype=jnp.int32)
    opening = jnp.ones(segment.shape[:-1] + (1,), dtype=bool)
    change = jnp.concatenate([opening, segment[..., 1:] != segment[..., :-1]], axis=-1)
    starts = lax.cummax(jnp.where(change, places, jnp.int32(0)), axis=segment.ndim - 1)
    return places - starts


def rope_angles(positions):
    freq_table = jnp.power(10000.0, -2.0 * jnp.arange(HD // 2, dtype=jnp.float32) / HD)
    turned = positions.astype(jnp.float32)[..., None] * freq_table
    return (jnp.cos(turned), jnp.sin(turned))


def rope_turn(values, cosine, sine_part):
    half_size = values.shape[-1] // 2
    leading = values[..., :half_size]
    trailing = values[..., half_size:]
    return jnp.concatenate(
        [leading * cosine - trailing * sine_part, trailing * cosine + leading * sine_part], axis=-1
    )


def dot_rows(left_mat, right_mat):
    return lax.dot_general(
        left_mat, right_mat, (((1,), (1,)), ((), ())), preferred_element_type=jnp.float32
    )


def dot_cols(left_mat, right_mat):
    return lax.dot_general(
        left_mat, right_mat, (((0,), (0,)), ((), ())), preferred_element_type=jnp.float32
    )


def fetch_weights(w_query, w_key, w_value, w_gate, w_up, w_out, w_down):
    return (
        lax.all_gather(w_query, ("dp", "ctx"), axis=0, tiled=True),
        lax.all_gather(w_key, ("dp", "ctx"), axis=0, tiled=True),
        lax.all_gather(w_value, ("dp", "ctx"), axis=0, tiled=True),
        lax.all_gather(w_gate, ("dp", "ctx"), axis=0, tiled=True),
        lax.all_gather(w_up, ("dp", "ctx"), axis=0, tiled=True),
        lax.all_gather(w_out, ("dp", "ctx"), axis=1, tiled=True),
        lax.all_gather(w_down, ("dp", "ctx"), axis=1, tiled=True),
    )


def per_device_general(
    tokens_in, out_grad, segment_ids, w_query, w_key, w_value, w_out, w_gate, w_up, w_down
):
    micro_count = tokens_in.shape[0]
    seq_local = tokens_in.shape[1]
    span_len = tokens_in.shape[2]
    local_width = tokens_in.shape[3]
    ctx_index = lax.axis_index("ctx")
    model_index = lax.axis_index("mp")
    tokens_all, grads_all = (
        lax.all_gather(tokens_in, "mp", axis=3, tiled=True),
        lax.all_gather(out_grad, "mp", axis=3, tiled=True),
    )
    segments_all = lax.all_gather(segment_ids, "ctx", axis=2, tiled=True)
    feature_width = tokens_all.shape[3]
    seq_length = segments_all.shape[2]
    row_count = seq_local * span_len
    score_scale = 1.0 / math.sqrt(HD)
    positions = doc_positions(segments_all)
    query_places = ctx_index * span_len + jnp.arange(span_len, dtype=jnp.int32)
    key_places = jnp.arange(seq_length, dtype=jnp.int32)
    causal = key_places[None, :] <= query_places[:, None]
    outputs = []
    input_grads = []
    totals = None
    for micro_step in range(micro_count):
        full_weights = fetch_weights(w_query, w_key, w_value, w_gate, w_up, w_out, w_down)
        query_full, key_full, value_full, gate_full, up_full, out_full, down_full = full_weights
        head_count = query_full.shape[1] // HD
        segment_seq = segments_all[micro_step]
        segment_own = lax.dynamic_slice_in_dim(segment_seq, ctx_index * span_len, span_len, 1)
        position_own = lax.dynamic_slice_in_dim(
            positions[micro_step], ctx_index * span_len, span_len, 1
        )
        allowed = (segment_own[:, :, None] == segment_seq[:, None, :]) & causal[None]
        cosine, sine_part = rope_angles(position_own)
        cosine = cosine[:, :, None, :]
        sine_part = sine_part[:, :, None, :]
        inputs = tokens_all[micro_step].astype(jnp.float32)
        normed, inverse_one = layer_norm(inputs)
        normed_low = normed.astype(jnp.bfloat16).reshape(row_count, feature_width)

        def project(matrix):
            product = jnp.dot(normed_low, matrix, preferred_element_type=jnp.float32)
            return product.reshape(seq_local, span_len, head_count, HD)

        query_low = (
            rope_turn(project(query_full), cosine, sine_part)
            .astype(jnp.bfloat16)
            .reshape(seq_local, span_len, head_count * HD)
        )
        key_low = (
            rope_turn(project(key_full), cosine, sine_part)
            .astype(jnp.bfloat16)
            .reshape(seq_local, span_len, head_count * HD)
        )
        value_low = (
            project(value_full).astype(jnp.bfloat16).reshape(seq_local, span_len, head_count * HD)
        )
        key_seq, value_seq = (
            lax.all_gather(key_low, "ctx", axis=1, tiled=True),
            lax.all_gather(value_low, "ctx", axis=1, tiled=True),
        )
        mixed_parts = []
        log_totals = []
        for head_index in range(head_count):
            head_cols = slice(head_index * HD, (head_index + 1) * HD)
            scores = (
                jnp.einsum(
                    "sqd,skd->sqk",
                    query_low[..., head_cols],
                    key_seq[..., head_cols],
                    preferred_element_type=jnp.float32,
                )
                * score_scale
            )
            scores = jnp.where(allowed, scores, NEG_FILL)
            highest = jnp.max(scores, axis=-1, keepdims=True)
            exp_terms = jnp.exp(scores - highest)
            total_exp = jnp.sum(exp_terms, axis=-1, keepdims=True)
            probs_low = (exp_terms / total_exp).astype(jnp.bfloat16)
            mixed_parts.append(
                jnp.einsum(
                    "sqk,skd->sqd",
                    probs_low,
                    value_seq[..., head_cols],
                    preferred_element_type=jnp.float32,
                )
            )
            log_totals.append(highest + jnp.log(total_exp))
        mixed_low = (
            jnp.concatenate(mixed_parts, axis=-1)
            .astype(jnp.bfloat16)
            .reshape(row_count, head_count * HD)
        )
        branch = jnp.dot(mixed_low, out_full, preferred_element_type=jnp.float32)
        branch = lax.psum(branch, "mp")
        residual = inputs + branch.reshape(seq_local, span_len, feature_width)
        normed_two, inverse_two = layer_norm(residual)
        second_low = normed_two.astype(jnp.bfloat16).reshape(row_count, feature_width)
        gate_lin = jnp.dot(second_low, gate_full, preferred_element_type=jnp.float32)
        up_lin = jnp.dot(second_low, up_full, preferred_element_type=jnp.float32)
        sigmoid_gate = jax.nn.sigmoid(gate_lin)
        hidden_low = (gate_lin * sigmoid_gate * up_lin).astype(jnp.bfloat16)
        feed_terms = jnp.dot(hidden_low, down_full, preferred_element_type=jnp.float32).reshape(
            seq_local, span_len, feature_width
        )
        feed_own = lax.psum_scatter(
            feed_terms.astype(jnp.bfloat16), "mp", scatter_dimension=2, tiled=True
        ).astype(jnp.float32)
        residual_own = lax.dynamic_slice_in_dim(residual, model_index * local_width, local_width, 2)
        outputs.append((residual_own + feed_own).astype(jnp.bfloat16))
        back_weights = (
            lax.all_gather(w_query, ("dp", "ctx"), axis=0, tiled=True),
            lax.all_gather(w_key, ("dp", "ctx"), axis=0, tiled=True),
            lax.all_gather(w_value, ("dp", "ctx"), axis=0, tiled=True),
            lax.all_gather(w_gate, ("dp", "ctx"), axis=0, tiled=True),
            lax.all_gather(w_up, ("dp", "ctx"), axis=0, tiled=True),
            lax.all_gather(w_out, ("dp", "ctx"), axis=1, tiled=True),
            lax.all_gather(w_down, ("dp", "ctx"), axis=1, tiled=True),
        )
        key_back, value_back = (
            lax.all_gather(key_low, "ctx", axis=1, tiled=True),
            lax.all_gather(value_low, "ctx", axis=1, tiled=True),
        )
        query_back, key_mat, value_mat, gate_back, up_back, out_back, down_back = back_weights
        grad_low = grads_all[micro_step].reshape(row_count, feature_width)
        grad_float = grads_all[micro_step].astype(jnp.float32)
        hidden_grad = dot_rows(grad_low, down_back)
        gate_grad = (
            hidden_grad * up_lin * sigmoid_gate * (1.0 + gate_lin * (1.0 - sigmoid_gate))
        ).astype(jnp.bfloat16)
        up_grad = (hidden_grad * gate_lin * sigmoid_gate).astype(jnp.bfloat16)
        normed_grad = dot_rows(gate_grad, gate_back) + dot_rows(up_grad, up_back)
        normed_grad = lax.psum(normed_grad, "mp").reshape(seq_local, span_len, feature_width)
        residual_grad = grad_float + norm_backward(normed_grad, normed_two, inverse_two)
        residual_low = residual_grad.astype(jnp.bfloat16).reshape(row_count, feature_width)
        mixed_grad = (
            dot_rows(residual_low, out_back)
            .astype(jnp.bfloat16)
            .reshape(seq_local, span_len, head_count * HD)
        )
        query_parts = []
        key_parts = []
        value_parts = []
        for head_index in range(head_count):
            head_cols = slice(head_index * HD, (head_index + 1) * HD)
            query_head = query_low[..., head_cols]
            key_head = key_back[..., head_cols]
            mixed_head = mixed_grad[..., head_cols]
            scores = (
                jnp.einsum("sqd,skd->sqk", query_head, key_head, preferred_element_type=jnp.float32)
                * score_scale
            )
            scores = jnp.where(allowed, scores, NEG_FILL)
            probs = jnp.exp(scores - log_totals[head_index])
            probs_low = probs.astype(jnp.bfloat16)
            value_parts.append(
                jnp.einsum(
                    "sqk,sqd->skd", probs_low, mixed_head, preferred_element_type=jnp.float32
                )
            )
            probs_grad = jnp.einsum(
                "sqd,skd->sqk",
                mixed_head,
                value_back[..., head_cols],
                preferred_element_type=jnp.float32,
            )
            row_dot = jnp.sum(probs * probs_grad, axis=-1, keepdims=True)
            scores_grad = (probs * (probs_grad - row_dot)).astype(jnp.bfloat16)
            query_parts.append(
                jnp.einsum(
                    "sqk,skd->sqd", scores_grad, key_head, preferred_element_type=jnp.float32
                )
                * score_scale
            )
            key_parts.append(
                jnp.einsum(
                    "sqk,sqd->skd", scores_grad, query_head, preferred_element_type=jnp.float32
                )
                * score_scale
            )
        key_terms = jnp.concatenate(key_parts, axis=-1)
        value_terms = jnp.concatenate(value_parts, axis=-1)
        key_grad_own, value_grad_own = (
            lax.psum_scatter(key_terms, "ctx", scatter_dimension=1, tiled=True),
            lax.psum_scatter(value_terms, "ctx", scatter_dimension=1, tiled=True),
        )
        query_sum = jnp.concatenate(query_parts, axis=-1).reshape(
            seq_local, span_len, head_count, HD
        )
        query_grad = (
            rope_turn(query_sum, cosine, -sine_part)
            .astype(jnp.bfloat16)
            .reshape(row_count, head_count * HD)
        )
        key_grad = (
            rope_turn(key_grad_own.reshape(seq_local, span_len, head_count, HD), cosine, -sine_part)
            .astype(jnp.bfloat16)
            .reshape(row_count, head_count * HD)
        )
        value_grad = value_grad_own.astype(jnp.bfloat16).reshape(row_count, head_count * HD)
        input_terms = (
            dot_rows(query_grad, query_back)
            + dot_rows(key_grad, key_mat)
            + dot_rows(value_grad, value_mat)
        )
        input_sum = (
            lax.psum(input_terms.astype(jnp.bfloat16), "mp")
            .astype(jnp.float32)
            .reshape(seq_local, span_len, feature_width)
        )
        grad_whole = residual_grad + norm_backward(input_sum, normed, inverse_one)
        input_grads.append(
            lax.dynamic_slice_in_dim(grad_whole, model_index * local_width, local_width, 2)
        )
        new_terms = (
            dot_cols(normed_low, query_grad),
            dot_cols(normed_low, key_grad),
            dot_cols(normed_low, value_grad),
            dot_cols(second_low, gate_grad),
            dot_cols(second_low, up_grad),
            dot_cols(mixed_low, residual_low),
            dot_cols(hidden_low, grad_low),
        )
        if totals is None:
            totals = new_terms
        else:
            totals = tuple((older + newer for older, newer in zip(totals, new_terms)))
    grads_total = (
        lax.psum_scatter(
            totals[0].astype(jnp.bfloat16), ("dp", "ctx"), scatter_dimension=0, tiled=True
        ).astype(jnp.float32),
        lax.psum_scatter(
            totals[1].astype(jnp.bfloat16), ("dp", "ctx"), scatter_dimension=0, tiled=True
        ).astype(jnp.float32),
        lax.psum_scatter(
            totals[2].astype(jnp.bfloat16), ("dp", "ctx"), scatter_dimension=0, tiled=True
        ).astype(jnp.float32),
        lax.psum_scatter(
            totals[3].astype(jnp.bfloat16), ("dp", "ctx"), scatter_dimension=0, tiled=True
        ).astype(jnp.float32),
        lax.psum_scatter(
            totals[4].astype(jnp.bfloat16), ("dp", "ctx"), scatter_dimension=0, tiled=True
        ).astype(jnp.float32),
        lax.psum_scatter(
            totals[5].astype(jnp.bfloat16), ("dp", "ctx"), scatter_dimension=1, tiled=True
        ).astype(jnp.float32),
        lax.psum_scatter(
            totals[6].astype(jnp.bfloat16), ("dp", "ctx"), scatter_dimension=1, tiled=True
        ).astype(jnp.float32),
    )
    return (
        jnp.stack(outputs, axis=0),
        jnp.stack(input_grads, axis=0),
        grads_total[0],
        grads_total[1],
        grads_total[2],
        grads_total[5],
        grads_total[3],
        grads_total[4],
        grads_total[6],
    )


MESH = pl.DeviceIdType.MESH
HBM = pl.BlockSpec(memory_space=pl.ANY)
LOW = jnp.bfloat16
FULL = jnp.float32
TILE = 256


def contract(left, right, left_dim, right_dim):
    return lax.dot_general(
        left, right, (((left_dim,), (right_dim,)), ((), ())), preferred_element_type=FULL
    )


def aligned(start, size, unit=None):
    return pl.ds(pl.multiple_of(start, size if unit is None else unit), size)


class Place:
    def __init__(self):
        self.dp = lax.axis_index("dp")
        self.ctx = lax.axis_index("ctx")
        self.mp = lax.axis_index("mp")
        self.high = self.ctx // 2
        self.low = self.ctx % 2
        self.chip = self.mp // 2
        self.core = self.mp % 2
        self.home = self.dp * 4 + self.ctx

    def along(self, mask):
        other = self.ctx + mask - 2 * (self.ctx & mask)
        return (self.dp, other, self.mp)

    def across(self):
        return (1 - self.dp, self.ctx, self.mp)

    def beside_chip(self):
        return (self.dp, self.ctx, (1 - self.chip) * 2 + self.core)

    def beside_core(self):
        return (self.dp, self.ctx, self.chip * 2 + 1 - self.core)

    def shard_rows(self, low, chip, core, size=128):
        return aligned((core * 4 + chip * 2 + low) * 128, size, 128)


class Mover:
    def __init__(self, send, receive, local):
        self.send, self.receive, self.local = send, receive, local
        self.remote_count = 0
        self.local_count = 0

    def to(self, source, target, device):
        slot = self.remote_count
        self.remote_count += 1
        copy = pltpu.make_async_remote_copy(
            src_ref=source,
            dst_ref=target,
            send_sem=self.send.at[slot],
            recv_sem=self.receive.at[slot],
            device_id=device,
            device_id_type=MESH,
        )
        copy.start()
        return copy

    def here(self, source, target):
        slot = self.local_count
        self.local_count += 1
        copy = pltpu.make_async_copy(source, target, self.local.at[slot])
        copy.start()
        return copy


def greet(partners):
    barrier = pltpu.get_barrier_semaphore()
    for partner in partners:
        pl.semaphore_signal(barrier, inc=1, device_id=partner, device_id_type=MESH)
    pl.semaphore_wait(barrier, len(partners))


class GroupGather:
    def __init__(self, place, mover, view, own):
        self.place, self.mover, self.view = place, mover, view
        p = place
        landing = view(p.low, p.chip, p.core)
        self.along = mover.to(own, landing, p.along(1))
        self.chip = mover.to(own, landing, p.beside_chip())
        self.core = mover.to(own, landing, p.beside_core())
        self.sent = [self.along, self.chip, self.core]

    def relay_along(self):
        p = self.place
        self.along.wait_recv()
        piece = self.view(1 - p.low, p.chip, p.core)
        self.corner = self.mover.to(piece, piece, p.beside_chip())
        self.along_core = self.mover.to(piece, piece, p.beside_core())
        self.sent += [self.corner, self.along_core]

    def relay_chip(self):
        p = self.place
        self.chip.wait_recv()
        piece = self.view(p.low, 1 - p.chip, p.core)
        self.chip_core = self.mover.to(piece, piece, p.beside_core())
        self.sent.append(self.chip_core)

    def relay_corner(self):
        p = self.place
        self.corner.wait_recv()
        piece = self.view(1 - p.low, 1 - p.chip, p.core)
        self.corner_core = self.mover.to(piece, piece, p.beside_core())
        self.sent.append(self.corner_core)

    def finish(self):
        for copy in (self.core, self.along_core, self.chip_core, self.corner_core):
            copy.wait_recv()
        for copy in self.sent:
            copy.wait_send()


class GroupScatter:
    def __init__(self, place, mover, buffers, terms):
        self.place, self.mover, self.buffers, self.terms = place, mover, buffers, terms
        self.sent = []

    def half(self, part):
        return pl.ds(part * TILE, TILE)

    def rows(self, chip, core):
        return self.place.shard_rows(0, chip, core, TILE)

    def start_core(self, part):
        p = self.place
        core_send, core_recv = self.buffers[:2]
        chip = 1 - p.chip if part == 0 else p.chip
        core_send[self.half(part), :] = self.terms(self.rows(chip, 1 - p.core)).astype(LOW)
        copy = self.mover.to(
            core_send.at[self.half(part)], core_recv.at[self.half(part)], p.beside_core()
        )
        self.sent.append(copy)
        if part == 0:
            self.core_first = copy
        else:
            self.core_second = copy

    def start_chip(self):
        p = self.place
        core_recv, chip_send, chip_recv = self.buffers[1:4]
        total = self.terms(self.rows(1 - p.chip, p.core))
        self.core_first.wait_recv()
        chip_send[...] = (total + core_recv[self.half(0), :].astype(FULL)).astype(LOW)
        self.chip_copies = []
        for which in (1 - p.low, p.low):
            rows = aligned(which * 128, 128)
            self.chip_copies.append(
                self.mover.to(chip_send.at[rows], chip_recv.at[rows], p.beside_chip())
            )
        self.sent += self.chip_copies

    def start_along(self):
        p = self.place
        core_recv, _, chip_recv, along_send, along_recv, total_ref = self.buffers[1:]
        total = self.terms(self.rows(p.chip, p.core))
        self.core_second.wait_recv()
        total_ref[...] = total + core_recv[self.half(1), :].astype(FULL)
        self.chip_copies[0].wait_recv()
        rows = aligned((1 - p.low) * 128, 128)
        along_send[...] = (total_ref[rows, :] + chip_recv[rows, :].astype(FULL)).astype(LOW)
        self.along = self.mover.to(along_send, along_recv, p.along(1))
        self.sent.append(self.along)

    def result(self):
        p = self.place
        chip_recv, _, along_recv, total_ref = self.buffers[3:]
        self.chip_copies[1].wait_recv()
        rows = aligned(p.low * 128, 128)
        total = total_ref[rows, :] + chip_recv[rows, :].astype(FULL)
        self.along.wait_recv()
        total = total + along_recv[...].astype(FULL)
        for copy in self.sent:
            copy.wait_send()
        return total


def scatter_buffers(width):
    return [
        pltpu.VMEM((2 * TILE, width), LOW),
        pltpu.VMEM((2 * TILE, width), LOW),
        pltpu.VMEM((TILE, width), LOW),
        pltpu.VMEM((TILE, width), LOW),
        pltpu.VMEM((TILE // 2, width), LOW),
        pltpu.VMEM((TILE // 2, width), LOW),
        pltpu.VMEM((TILE, width), FULL),
    ]


class WeightFetch:
    def __init__(self, place, mover, shard, whole, axis, start, size, landing):
        self.place, self.mover = place, mover
        half = shard.shape[axis] // 2
        block = shard.shape[1 - axis]

        def source(which):
            part = aligned(which * half + start, size, 128)
            return shard.at[:, part] if axis == 1 else shard.at[part, :]

        def target(ctx):
            span = aligned((place.dp * 4 + ctx) * block, block, 128)
            part = pl.ds(landing, size)
            return whole.at[span, part] if axis == 1 else whole.at[part, span]

        self.source, self.target = source, target

    def start(self):
        p = self.place
        mine = self.source(p.low)
        other = self.source(1 - p.low)
        spot = self.target(p.ctx)
        self.near = [
            self.mover.to(mine, spot, p.along(2)),
            self.mover.to(other, spot, p.along(3)),
            self.mover.to(other, spot, p.along(1)),
        ]
        self.local = self.mover.here(mine, spot)

    def cross(self):
        p = self.place
        self.far = [self.mover.to(self.source(p.low), self.target(p.ctx), p.across())]
        for copy, mask in ((self.near[2], 1), (self.near[0], 2), (self.near[1], 3)):
            copy.wait_recv()
            block = self.target(p.along(mask)[1])
            self.far.append(self.mover.to(block, block, p.across()))

    def finish(self):
        self.local.wait()
        for copy in self.far:
            copy.wait_recv()

    def drain(self):
        for copy in self.near + self.far:
            copy.wait_send()


def normalise(values):
    centred = values - jnp.mean(values, axis=-1, keepdims=True)
    inverse = lax.rsqrt(jnp.mean(centred * centred, axis=-1, keepdims=True) + EPSILON)
    return centred * inverse, inverse


def allowed_mask(seg_col, seg_row, start, keys):
    rows = seg_col[pl.ds(start, TILE), :][:, :1]
    cols = seg_row[0:1, pl.ds(0, keys)]
    row_place = start + lax.broadcasted_iota(jnp.int32, (TILE, keys), 0)
    col_place = lax.broadcasted_iota(jnp.int32, (TILE, keys), 1)
    return (rows == cols) & (col_place <= row_place)


def turn(values, cosine, sine_part):
    parts = []
    for start in range(0, values.shape[1], HD):
        head = values[:, start : start + HD]
        parts.append(head * cosine + pltpu.roll(head, HD // 2, 1) * sine_part)
    return jnp.concatenate(parts, axis=1)


def attention_kernel(
    tokens_in, out_grad, seg_col_in, seg_row_in, freqs, w_query, w_key, w_value, w_out, w_gate, w_up, w_down,
    qkv_all, out_all, gate_all, up_all, down_all, grads_all, second_all, normed_out,
    query, key, value, mixed, log_total, cosine, sine_part, seg_col, seg_row, residual, inverse_two, kept,
    tokens, qkv_here, out_here, second_rows, core_send, core_recv, chip_send, chip_recv, along_send, along_recv,
    total_ref, send, receive, local,
):
    p = Place()
    mover = Mover(send, receive, local)
    greet([p.along(1), p.along(2), p.along(3), p.across(), p.beside_chip(), p.beside_core()])
    length, width = tokens.shape
    span, feats = tokens_in.shape[2:]
    cols = w_query.shape[1] // 2
    score_scale = 1.0 / math.sqrt(HD)

    def fetch(shard, whole, axis, landing=0, pieces=1):
        size = shard.shape[axis] // 2 // pieces
        return [
            WeightFetch(p, mover, shard, whole, axis, piece * size, size, landing + piece * size)
            for piece in range(pieces)
        ]

    fetch_query = fetch(w_query, qkv_all, 1, 0)
    fetch_key = fetch(w_key, qkv_all, 1, cols)
    fetch_value = fetch(w_value, qkv_all, 1, 2 * cols)
    fetch_out = fetch(w_out, out_all, 0)
    fetch_gate = fetch(w_gate, gate_all, 1, 0, 2)
    fetch_up = fetch(w_up, up_all, 1, 0, 2)
    fetch_down = fetch(w_down, down_all, 0, 0, 2)

    def block_of(whole, ctx, model):
        return whole.at[aligned(ctx * span, span), aligned(model * feats, feats)]

    def own_view(whole):
        return lambda low, chip, core: block_of(whole, p.high * 2 + low, chip * 2 + core)

    def other_view(whole):
        return lambda low, chip, core: block_of(whole, (1 - p.high) * 2 + low, chip * 2 + core)

    seg_copies = []
    for mask in (1, 2, 3):
        goal = p.high if mask == 1 else 1 - p.high
        spot = aligned(p.ctx * span, span)
        seg_copies.append(mover.to(seg_col_in.at[goal], seg_col.at[spot], p.along(mask)))
        seg_copies.append(mover.to(seg_row_in.at[goal], seg_row.at[:, spot], p.along(mask)))
    seg_local = [
        mover.here(seg_col_in.at[p.high], seg_col.at[aligned(p.ctx * span, span)]),
        mover.here(seg_row_in.at[p.high], seg_row.at[:, aligned(p.ctx * span, span)]),
    ]
    here = block_of(tokens, p.ctx, p.mp)
    swap = mover.to(tokens_in.at[1 - p.high, 0], here, p.along(2))
    own_tokens = tokens_in.at[p.high, 0]
    tokens_local = mover.here(own_tokens, here)
    gather_own = GroupGather(p, mover, own_view(tokens), own_tokens)
    for chunk in fetch_query + fetch_key:
        chunk.start()
    for copy in seg_copies:
        copy.wait()
    for copy in seg_local:
        copy.wait()
    for start in range(0, length, TILE):
        rows = pl.ds(start, TILE)
        keys = start + TILE
        allowed = allowed_mask(seg_col, seg_row, start, keys)
        position = jnp.sum(jnp.where(allowed, 1.0, 0.0), axis=1, keepdims=True) - 1.0
        angle = position * freqs[0:1, :]
        cosine[rows, :] = jnp.cos(angle)
        lane = lax.broadcasted_iota(jnp.int32, (TILE, HD), 1)
        sine = jnp.sin(angle)
        sine_part[rows, :] = jnp.where(lane < HD // 2, -sine, sine)
    swap.wait_recv()
    gather_other = GroupGather(
        p, mover, other_view(tokens), block_of(tokens, p.along(2)[1], p.mp)
    )
    fetch_value[0].start()
    gather_own.relay_along()
    gather_own.relay_chip()
    gather_own.relay_corner()
    fetch_query[0].cross()
    gather_other.relay_along()
    gather_other.relay_chip()
    gather_other.relay_corner()
    fetch_out[0].start()
    fetch_key[0].cross()
    tokens_local.wait()
    swap.wait_send()
    gather_own.finish()
    gather_other.finish()
    my_rows = p.shard_rows(p.low, p.chip, p.core)
    kept[...] = tokens[my_rows, :]
    residual[...] = kept[...].astype(FULL)
    for start in range(0, length, 128):
        rows = pl.ds(start, 128)
        tokens[rows, :] = normalise(tokens[rows, :].astype(FULL))[0].astype(LOW)
    normed_copy = mover.here(tokens, normed_out)
    fetch_value[0].cross()
    fetch_gate[0].start()
    for chunk in fetch_query + fetch_key + fetch_value:
        chunk.finish()
    qkv_copy = mover.here(qkv_all, qkv_here)
    qkv_copy.wait()
    for start in range(0, length, TILE):
        rows = pl.ds(start, TILE)
        three = contract(tokens[rows, :], qkv_here[...], 1, 0)
        query[rows, :] = turn(three[:, :cols], cosine[rows, :], sine_part[rows, :]).astype(LOW)
        key[rows, :] = turn(three[:, cols : 2 * cols], cosine[rows, :], sine_part[rows, :]).astype(
            LOW
        )
        value[rows, :] = three[:, 2 * cols :].astype(LOW)

    grads = {}

    def grad_start():
        spot = block_of(grads_all, p.ctx, p.mp)
        own = out_grad.at[p.high, 0]
        grads["swap"] = mover.to(out_grad.at[1 - p.high, 0], spot, p.along(2))
        grads["local"] = mover.here(own, spot)
        grads["own"] = GroupGather(p, mover, own_view(grads_all), own)

    def grad_second():
        grads["swap"].wait_recv()
        grads["other"] = GroupGather(
            p, mover, other_view(grads_all), block_of(grads_all, p.along(2)[1], p.mp)
        )

    pending = [
        fetch_out[0].cross,
        grad_start,
        fetch_gate[1].start,
        grad_second,
        fetch_gate[0].cross,
        lambda: (grads["own"].relay_along(), grads["own"].relay_chip()),
        fetch_up[0].start,
        lambda: (grads["own"].relay_corner(), grads["other"].relay_along()),
        lambda: (grads["other"].relay_chip(), grads["other"].relay_corner()),
        fetch_gate[1].cross,
        fetch_up[1].start,
        fetch_up[0].cross,
        fetch_down[0].start,
        fetch_up[1].cross,
        fetch_down[1].start,
        fetch_down[0].cross,
        fetch_down[1].cross,
    ]

    def pump(count=1):
        for _ in range(min(count, len(pending))):
            pending.pop(0)()

    head_count = cols // HD
    for start in range(0, length, TILE):
        rows = pl.ds(start, TILE)
        keys = start + TILE
        allowed = allowed_mask(seg_col, seg_row, start, keys)
        for head in range(head_count):
            head_cols = pl.ds(head * HD, HD)
            scores = contract(query[rows, head_cols], key[pl.ds(0, keys), head_cols], 1, 1)
            scores = jnp.where(allowed, scores * score_scale, NEG_FILL)
            highest = jnp.max(scores, axis=-1, keepdims=True)
            exp_terms = jnp.exp(scores - highest)
            total_exp = jnp.sum(exp_terms, axis=-1, keepdims=True)
            probs_low = (exp_terms * (1.0 / total_exp)).astype(LOW)
            mixed[rows, head_cols] = contract(
                probs_low, value[pl.ds(0, keys), head_cols], 1, 0
            ).astype(LOW)
            log_total[rows, head_cols] = jnp.broadcast_to(
                highest + jnp.log(total_exp), (TILE, HD)
            )
        pump()
    fetch_out[0].finish()
    out_copy = mover.here(out_all, out_here)
    out_copy.wait()
    scatter = GroupScatter(
        p,
        mover,
        (core_send, core_recv, chip_send, chip_recv, along_send, along_recv, total_ref),
        lambda rows: contract(mixed[rows, :], out_here[...], 1, 0),
    )
    scatter.start_core(0)
    scatter.start_core(1)
    scatter.start_chip()
    pump()
    scatter.start_along()
    pump()
    branch = scatter.result()
    hidden = residual[...] + branch
    residual[...] = hidden
    normed_two, inverse = normalise(hidden)
    inverse_two[...] = jnp.broadcast_to(inverse, inverse_two.shape)
    second_rows[...] = normed_two.astype(LOW)

    def row_view(low, chip, core):
        return second_all.at[p.shard_rows(low, chip, core)]

    second_local = mover.here(second_rows, row_view(p.low, p.chip, p.core))
    gather = GroupGather(p, mover, row_view, second_rows)
    pump(2)
    gather.relay_along()
    gather.relay_chip()
    pump(2)
    gather.relay_corner()
    pump(len(pending))
    for piece in (gather, grads["own"], grads["other"]):
        piece.finish()
    second_local.wait()
    grads["swap"].wait_send()
    grads["local"].wait()
    normed_copy.wait()
    for chunk in fetch_gate + fetch_up + fetch_down:
        chunk.finish()
    for chunk in (
        fetch_query + fetch_key + fetch_value + fetch_out + fetch_gate + fetch_up + fetch_down
    ):
        chunk.drain()


def attention_forward(tokens_in, out_grad, seg_col, seg_row, freqs, weights):
    w_query, w_key, w_value, w_out, w_gate, w_up, w_down = weights
    span = tokens_in.shape[2]
    length, width = 4 * span, 4 * tokens_in.shape[3]
    cols = w_query.shape[1] // 2
    hidden = w_gate.shape[1] // 2

    def low(*shape):
        return jax.ShapeDtypeStruct(shape, LOW)

    def full(*shape):
        return jax.ShapeDtypeStruct(shape, FULL)

    in_hbm = [
        low(width, 3 * cols), low(cols, width), low(width, hidden), low(width, hidden), low(hidden, width),
        low(length, width), low(length, width), low(length, width),
    ]
    in_vmem = [
        low(length, cols), low(length, cols), low(length, cols), low(length, cols), full(length, cols),
        full(length, HD), full(length, HD), full(length, HD), full(8, length), full(length // 8, width),
        full(length // 8, HD), low(length // 8, width),
    ]
    vmem = pl.BlockSpec(memory_space=pltpu.VMEM)
    return pl.pallas_call(
        attention_kernel,
        out_shape=in_hbm + in_vmem,
        in_specs=[HBM] * 4 + [vmem] + [HBM] * 7,
        out_specs=[HBM] * len(in_hbm) + [vmem] * len(in_vmem),
        scratch_shapes=[
            pltpu.VMEM((length, width), LOW),
            pltpu.VMEM((width, 3 * cols), LOW),
            pltpu.VMEM((cols, width), LOW),
            pltpu.VMEM((length // 8, width), LOW),
            *scatter_buffers(width),
            pltpu.SemaphoreType.DMA((128,)),
            pltpu.SemaphoreType.DMA((128,)),
            pltpu.SemaphoreType.DMA((32,)),
        ],
        compiler_params=pltpu.CompilerParams(
            collective_id=1, has_side_effects=True, vmem_limit_bytes=60 * 1024 * 1024
        ),
    )(tokens_in, out_grad, seg_col, seg_row, freqs, *weights)


def xor_permute(values, axis, size, mask):
    return lax.ppermute(values, axis, [(place, place ^ mask) for place in range(size)])


def pick_blocks(blocks, index):
    stack = jnp.stack(blocks, axis=0)
    return [
        lax.dynamic_index_in_dim(stack, index ^ place, 0, keepdims=False)
        for place in range(len(blocks))
    ]


def token_routes(offset):
    routes = []
    for high in range(2):
        for low in range(2):
            for chip in range(2):
                for core in range(2):
                    source = (high * 2 + low) * 4 + chip * 2 + core
                    target = (core * 2 + chip) * 4 + ((2 * high + low) ^ offset)
                    routes.append((source, target))
    return routes


def from_rows(rows, model_index, quarter):
    row_count, width = rows.shape
    parts = jnp.transpose(rows.reshape(row_count, 4, width // 4), (1, 0, 2))
    blocks = []
    for offset in range(4):
        part = lax.dynamic_index_in_dim(parts, quarter ^ offset, 0, keepdims=False)
        blocks.append(lax.ppermute(part, ("ctx", "mp"), token_routes(offset)))
    return jnp.concatenate(pick_blocks(blocks, model_index), axis=0).reshape(
        2, 1, 2 * row_count, width // 4
    )


def half_of(values, axis, which):
    size = values.shape[axis] // 2
    return lax.dynamic_slice_in_dim(values, which * size, size, axis)


def return_grads(grad, axis, dp_index, high, low):
    cut = 1 - axis
    sent = half_of(grad, cut, 1 - dp_index).astype(jnp.bfloat16)
    total = half_of(grad, cut, dp_index) + xor_permute(sent, "dp", 2, 1).astype(jnp.float32)
    sent = half_of(total, cut, 1 - high).astype(jnp.bfloat16)
    total = half_of(total, cut, high) + xor_permute(sent, "ctx", 4, 2).astype(jnp.float32)
    sent = half_of(total, cut, 1 - low).astype(jnp.bfloat16)
    mine = half_of(total, cut, low)
    return mine, xor_permute(sent, "ctx", 4, 1).astype(jnp.float32)


def place_halves(mine, other, axis, low):
    first = jnp.where(low == 0, mine, other)
    second = jnp.where(low == 0, other, mine)
    return jnp.concatenate([first, second], axis=axis)


GROUPS = [
    [(high * 2 + low) * 4 + chip * 2 + core for core in range(2) for chip in range(2) for low in range(2)]
    for high in range(2)
]


def gather_rows(rows):
    return lax.all_gather(rows, ("ctx", "mp"), axis=0, tiled=True, axis_index_groups=GROUPS)


def scatter_rows(terms):
    return lax.psum_scatter(
        terms.astype(jnp.bfloat16),
        ("ctx", "mp"),
        scatter_dimension=0,
        tiled=True,
        axis_index_groups=GROUPS,
    ).astype(jnp.float32)


def per_device_grouped(
    tokens_in, out_grad, segment_ids, w_query, w_key, w_value, w_out, w_gate, w_up, w_down
):
    dp_index = lax.axis_index("dp")
    ctx_index = lax.axis_index("ctx")
    model_index = lax.axis_index("mp")
    high = ctx_index // 2
    low = ctx_index % 2
    quarter = 2 * high + low
    score_scale = 1.0 / math.sqrt(HD)
    span = segment_ids.shape[2]

    segment_float = segment_ids[:, 0].astype(jnp.float32)
    segment_cols = jnp.broadcast_to(segment_float[:, :, None], (2, span, HD))
    segment_rows = jnp.broadcast_to(segment_float[:, None, :], (2, 8, span))
    freq_half = jnp.power(10000.0, -2.0 * jnp.arange(HD // 2, dtype=jnp.float32) / HD)
    freqs = jnp.broadcast_to(jnp.concatenate([freq_half, freq_half])[None], (8, HD))
    (
        query_key_value, out_part, gate_part, up_part, down_part, grad_low, second_low, normed_low,
        query_low, key_low, value_low, mixed_low, log_totals, cosine, sine_part, seg_col, seg_row, residual,
        inverse_wide, kept,
    ) = attention_forward(
        tokens_in, out_grad, segment_cols, segment_rows, freqs,
        (w_query, w_key, w_value, w_out, w_gate, w_up, w_down),
    )
    inverse_two = inverse_wide[:, :1]
    length = seg_col.shape[0]
    row_count = length // 8
    local_cols = query_low.shape[1]
    head_count = local_cols // HD
    row_start = ((model_index % 2) * 4 + (model_index // 2) * 2 + low) * row_count

    def own_rows(values):
        return lax.dynamic_slice_in_dim(values, row_start, row_count, 0)

    normed_rows, inverse_one = layer_norm(kept.astype(jnp.float32))
    grad_rows = own_rows(grad_low)
    centred = residual - jnp.mean(residual, axis=-1, keepdims=True)
    normed_two = centred * inverse_two
    places = jnp.arange(length, dtype=jnp.int32)
    allowed = (seg_col[:, :1] == seg_row[:1]) & (places[None, :] <= places[:, None])

    def turned(values, sine_used):
        parts = values.reshape(length, head_count, 2, HD // 2)
        swapped = jnp.concatenate([parts[:, :, 1:], parts[:, :, :1]], axis=2)
        return (
            (
                parts * cosine.reshape(length, 1, 2, HD // 2)
                + swapped * sine_used.reshape(length, 1, 2, HD // 2)
            )
            .astype(jnp.bfloat16)
            .reshape(length, local_cols)
        )

    gate_lin = jnp.dot(second_low, gate_part, preferred_element_type=jnp.float32)
    up_lin = jnp.dot(second_low, up_part, preferred_element_type=jnp.float32)
    sigmoid_gate = jax.nn.sigmoid(gate_lin)
    hidden_low = (gate_lin * sigmoid_gate * up_lin).astype(jnp.bfloat16)
    down_grads = return_grads(dot_cols(hidden_low, grad_low), 0, dp_index, high, low)
    hidden_grad = dot_rows(grad_low, down_part)
    gate_grad = (
        hidden_grad * up_lin * sigmoid_gate * (1.0 + gate_lin * (1.0 - sigmoid_gate))
    ).astype(jnp.bfloat16)
    up_grad = (hidden_grad * gate_lin * sigmoid_gate).astype(jnp.bfloat16)
    normed_grad = scatter_rows(dot_rows(gate_grad, gate_part) + dot_rows(up_grad, up_part))
    gate_grads = return_grads(dot_cols(second_low, gate_grad), 1, dp_index, high, low)
    up_grads = return_grads(dot_cols(second_low, up_grad), 1, dp_index, high, low)
    feed = scatter_rows(jnp.dot(hidden_low, down_part, preferred_element_type=jnp.float32))
    tokens_out = from_rows((residual + feed).astype(jnp.bfloat16), model_index, quarter)
    residual_grad = grad_rows.astype(jnp.float32) + norm_backward(
        normed_grad, normed_two, inverse_two
    )
    residual_low = gather_rows(residual_grad.astype(jnp.bfloat16))
    out_grads = return_grads(dot_cols(mixed_low, residual_low), 0, dp_index, high, low)
    mixed_grad = dot_rows(residual_low, out_part).astype(jnp.bfloat16)
    query_parts = []
    key_parts = []
    value_parts = []
    for head_index in range(head_count):
        cols = slice(head_index * HD, (head_index + 1) * HD)
        query_head = query_low[:, cols]
        key_head = key_low[:, cols]
        mixed_head = mixed_grad[:, cols]
        scores = dot_rows(query_head, key_head) * score_scale
        scores = jnp.where(allowed, scores, NEG_FILL)
        probs = jnp.exp(scores - log_totals[:, head_index * HD : head_index * HD + 1])
        value_parts.append(dot_cols(probs.astype(jnp.bfloat16), mixed_head))
        probs_grad = dot_rows(mixed_head, value_low[:, cols])
        row_dot = jnp.sum(probs * probs_grad, axis=-1, keepdims=True)
        scores_grad = (probs * (probs_grad - row_dot)).astype(jnp.bfloat16)
        query_parts.append(
            jnp.dot(scores_grad, key_head, preferred_element_type=jnp.float32) * score_scale
        )
        key_parts.append(dot_cols(scores_grad, query_head) * score_scale)
    query_grad = turned(jnp.concatenate(query_parts, axis=-1), -sine_part)
    key_grad = turned(jnp.concatenate(key_parts, axis=-1), -sine_part)
    value_grad = jnp.concatenate(value_parts, axis=-1).astype(jnp.bfloat16)
    three_grad = jnp.concatenate([query_grad, key_grad, value_grad], axis=-1)
    input_sum = scatter_rows(dot_rows(three_grad, query_key_value))
    three_grads = return_grads(dot_cols(normed_low, three_grad), 1, dp_index, high, low)
    grad_in_rows = residual_grad + norm_backward(input_sum, normed_rows, inverse_one)
    grad_in = from_rows(grad_in_rows.astype(jnp.bfloat16), model_index, quarter)

    def columns(pair, which):
        cols = slice(which * local_cols, (which + 1) * local_cols)
        return place_halves(pair[0][:, cols], pair[1][:, cols], 1, low)

    return (
        tokens_out,
        grad_in.astype(jnp.float32),
        columns(three_grads, 0),
        columns(three_grads, 1),
        columns(three_grads, 2),
        place_halves(*out_grads, 0, low),
        place_halves(*gate_grads, 1, low),
        place_halves(*up_grads, 1, low),
        place_halves(*down_grads, 0, low),
    )


def solution(mesh):
    in_specs = (
        P(None, "dp", "ctx", "mp"),
        P(None, "dp", "ctx", "mp"),
        P(None, "dp", "ctx"),
        P(("dp", "ctx"), "mp"),
        P(("dp", "ctx"), "mp"),
        P(("dp", "ctx"), "mp"),
        P("mp", ("dp", "ctx")),
        P(("dp", "ctx"), "mp"),
        P(("dp", "ctx"), "mp"),
        P("mp", ("dp", "ctx")),
    )
    out_specs = (
        P(None, "dp", "ctx", "mp"),
        P(None, "dp", "ctx", "mp"),
        P(("dp", "ctx"), "mp"),
        P(("dp", "ctx"), "mp"),
        P(("dp", "ctx"), "mp"),
        P("mp", ("dp", "ctx")),
        P(("dp", "ctx"), "mp"),
        P(("dp", "ctx"), "mp"),
        P("mp", ("dp", "ctx")),
    )
    grouped = mesh.shape["ctx"] == 4 and mesh.shape["mp"] == 4 and mesh.shape["dp"] == 2
    per_device = per_device_grouped if grouped else per_device_general
    return jax.shard_map(
        per_device, mesh=mesh, in_specs=in_specs, out_specs=out_specs, check_vma=False
    )
```

```python
import math

import jax
import jax.numpy as jnp
from jax import lax
from jax.experimental import pallas as pl
from jax.experimental.pallas import tpu as pltpu
from jax.sharding import PartitionSpec as P

HD = 128


EPSILON = 1e-05
NEG_FILL = -1e30


def layer_norm(values):
    centred = values - jnp.mean(values, axis=-1, keepdims=True)
    inverse = lax.rsqrt(jnp.mean(centred * centred, axis=-1, keepdims=True) + EPSILON)
    return (centred * inverse, inverse)


def norm_backward(upstream, normed, inverse):
    plain_mean = jnp.mean(upstream, axis=-1, keepdims=True)
    cross_mean = jnp.mean(upstream * normed, axis=-1, keepdims=True)
    return inverse * (upstream - plain_mean - normed * cross_mean)


def doc_positions(segment):
    length = segment.shape[-1]
    places = jnp.arange(length, dtype=jnp.int32)
    opening = jnp.ones(segment.shape[:-1] + (1,), dtype=bool)
    change = jnp.concatenate([opening, segment[..., 1:] != segment[..., :-1]], axis=-1)
    starts = lax.cummax(jnp.where(change, places, jnp.int32(0)), axis=segment.ndim - 1)
    return places - starts


def rope_angles(positions):
    freq_table = jnp.power(10000.0, -2.0 * jnp.arange(HD // 2, dtype=jnp.float32) / HD)
    turned = positions.astype(jnp.float32)[..., None] * freq_table
    return (jnp.cos(turned), jnp.sin(turned))


def rope_turn(values, cosine, sine_part):
    half_size = values.shape[-1] // 2
    leading = values[..., :half_size]
    trailing = values[..., half_size:]
    return jnp.concatenate(
        [leading * cosine - trailing * sine_part, trailing * cosine + leading * sine_part], axis=-1
    )


def dot_rows(left_mat, right_mat):
    return lax.dot_general(
        left_mat, right_mat, (((1,), (1,)), ((), ())), preferred_element_type=jnp.float32
    )


def dot_cols(left_mat, right_mat):
    return lax.dot_general(
        left_mat, right_mat, (((0,), (0,)), ((), ())), preferred_element_type=jnp.float32
    )


def fetch_weights(w_query, w_key, w_value, w_gate, w_up, w_out, w_down):
    return (
        lax.all_gather(w_query, ("dp", "ctx"), axis=0, tiled=True),
        lax.all_gather(w_key, ("dp", "ctx"), axis=0, tiled=True),
        lax.all_gather(w_value, ("dp", "ctx"), axis=0, tiled=True),
        lax.all_gather(w_gate, ("dp", "ctx"), axis=0, tiled=True),
        lax.all_gather(w_up, ("dp", "ctx"), axis=0, tiled=True),
        lax.all_gather(w_out, ("dp", "ctx"), axis=1, tiled=True),
        lax.all_gather(w_down, ("dp", "ctx"), axis=1, tiled=True),
    )


def per_device_general(
    tokens_in, out_grad, segment_ids, w_query, w_key, w_value, w_out, w_gate, w_up, w_down
):
    micro_count = tokens_in.shape[0]
    seq_local = tokens_in.shape[1]
    span_len = tokens_in.shape[2]
    local_width = tokens_in.shape[3]
    ctx_index = lax.axis_index("ctx")
    model_index = lax.axis_index("mp")
    tokens_all, grads_all = (
        lax.all_gather(tokens_in, "mp", axis=3, tiled=True),
        lax.all_gather(out_grad, "mp", axis=3, tiled=True),
    )
    segments_all = lax.all_gather(segment_ids, "ctx", axis=2, tiled=True)
    feature_width = tokens_all.shape[3]
    seq_length = segments_all.shape[2]
    row_count = seq_local * span_len
    score_scale = 1.0 / math.sqrt(HD)
    positions = doc_positions(segments_all)
    query_places = ctx_index * span_len + jnp.arange(span_len, dtype=jnp.int32)
    key_places = jnp.arange(seq_length, dtype=jnp.int32)
    causal = key_places[None, :] <= query_places[:, None]
    outputs = []
    input_grads = []
    totals = None
    for micro_step in range(micro_count):
        full_weights = fetch_weights(w_query, w_key, w_value, w_gate, w_up, w_out, w_down)
        query_full, key_full, value_full, gate_full, up_full, out_full, down_full = full_weights
        head_count = query_full.shape[1] // HD
        segment_seq = segments_all[micro_step]
        segment_own = lax.dynamic_slice_in_dim(segment_seq, ctx_index * span_len, span_len, 1)
        position_own = lax.dynamic_slice_in_dim(
            positions[micro_step], ctx_index * span_len, span_len, 1
        )
        allowed = (segment_own[:, :, None] == segment_seq[:, None, :]) & causal[None]
        cosine, sine_part = rope_angles(position_own)
        cosine = cosine[:, :, None, :]
        sine_part = sine_part[:, :, None, :]
        inputs = tokens_all[micro_step].astype(jnp.float32)
        normed, inverse_one = layer_norm(inputs)
        normed_low = normed.astype(jnp.bfloat16).reshape(row_count, feature_width)

        def project(matrix):
            product = jnp.dot(normed_low, matrix, preferred_element_type=jnp.float32)
            return product.reshape(seq_local, span_len, head_count, HD)

        query_low = (
            rope_turn(project(query_full), cosine, sine_part)
            .astype(jnp.bfloat16)
            .reshape(seq_local, span_len, head_count * HD)
        )
        key_low = (
            rope_turn(project(key_full), cosine, sine_part)
            .astype(jnp.bfloat16)
            .reshape(seq_local, span_len, head_count * HD)
        )
        value_low = (
            project(value_full).astype(jnp.bfloat16).reshape(seq_local, span_len, head_count * HD)
        )
        key_seq, value_seq = (
            lax.all_gather(key_low, "ctx", axis=1, tiled=True),
            lax.all_gather(value_low, "ctx", axis=1, tiled=True),
        )
        mixed_parts = []
        log_totals = []
        for head_index in range(head_count):
            head_cols = slice(head_index * HD, (head_index + 1) * HD)
            scores = (
                jnp.einsum(
                    "sqd,skd->sqk",
                    query_low[..., head_cols],
                    key_seq[..., head_cols],
                    preferred_element_type=jnp.float32,
                )
                * score_scale
            )
            scores = jnp.where(allowed, scores, NEG_FILL)
            highest = jnp.max(scores, axis=-1, keepdims=True)
            exp_terms = jnp.exp(scores - highest)
            total_exp = jnp.sum(exp_terms, axis=-1, keepdims=True)
            probs_low = (exp_terms / total_exp).astype(jnp.bfloat16)
            mixed_parts.append(
                jnp.einsum(
                    "sqk,skd->sqd",
                    probs_low,
                    value_seq[..., head_cols],
                    preferred_element_type=jnp.float32,
                )
            )
            log_totals.append(highest + jnp.log(total_exp))
        mixed_low = (
            jnp.concatenate(mixed_parts, axis=-1)
            .astype(jnp.bfloat16)
            .reshape(row_count, head_count * HD)
        )
        branch = jnp.dot(mixed_low, out_full, preferred_element_type=jnp.float32)
        branch = lax.psum(branch, "mp")
        residual = inputs + branch.reshape(seq_local, span_len, feature_width)
        normed_two, inverse_two = layer_norm(residual)
        second_low = normed_two.astype(jnp.bfloat16).reshape(row_count, feature_width)
        gate_lin = jnp.dot(second_low, gate_full, preferred_element_type=jnp.float32)
        up_lin = jnp.dot(second_low, up_full, preferred_element_type=jnp.float32)
        sigmoid_gate = jax.nn.sigmoid(gate_lin)
        hidden_low = (gate_lin * sigmoid_gate * up_lin).astype(jnp.bfloat16)
        feed_terms = jnp.dot(hidden_low, down_full, preferred_element_type=jnp.float32).reshape(
            seq_local, span_len, feature_width
        )
        feed_own = lax.psum_scatter(
            feed_terms.astype(jnp.bfloat16), "mp", scatter_dimension=2, tiled=True
        ).astype(jnp.float32)
        residual_own = lax.dynamic_slice_in_dim(residual, model_index * local_width, local_width, 2)
        outputs.append((residual_own + feed_own).astype(jnp.bfloat16))
        back_weights = (
            lax.all_gather(w_query, ("dp", "ctx"), axis=0, tiled=True),
            lax.all_gather(w_key, ("dp", "ctx"), axis=0, tiled=True),
            lax.all_gather(w_value, ("dp", "ctx"), axis=0, tiled=True),
            lax.all_gather(w_gate, ("dp", "ctx"), axis=0, tiled=True),
            lax.all_gather(w_up, ("dp", "ctx"), axis=0, tiled=True),
            lax.all_gather(w_out, ("dp", "ctx"), axis=1, tiled=True),
            lax.all_gather(w_down, ("dp", "ctx"), axis=1, tiled=True),
        )
        key_back, value_back = (
            lax.all_gather(key_low, "ctx", axis=1, tiled=True),
            lax.all_gather(value_low, "ctx", axis=1, tiled=True),
        )
        query_back, key_mat, value_mat, gate_back, up_back, out_back, down_back = back_weights
        grad_low = grads_all[micro_step].reshape(row_count, feature_width)
        grad_float = grads_all[micro_step].astype(jnp.float32)
        hidden_grad = dot_rows(grad_low, down_back)
        gate_grad = (
            hidden_grad * up_lin * sigmoid_gate * (1.0 + gate_lin * (1.0 - sigmoid_gate))
        ).astype(jnp.bfloat16)
        up_grad = (hidden_grad * gate_lin * sigmoid_gate).astype(jnp.bfloat16)
        normed_grad = dot_rows(gate_grad, gate_back) + dot_rows(up_grad, up_back)
        normed_grad = lax.psum(normed_grad, "mp").reshape(seq_local, span_len, feature_width)
        residual_grad = grad_float + norm_backward(normed_grad, normed_two, inverse_two)
        residual_low = residual_grad.astype(jnp.bfloat16).reshape(row_count, feature_width)
        mixed_grad = (
            dot_rows(residual_low, out_back)
            .astype(jnp.bfloat16)
            .reshape(seq_local, span_len, head_count * HD)
        )
        query_parts = []
        key_parts = []
        value_parts = []
        for head_index in range(head_count):
            head_cols = slice(head_index * HD, (head_index + 1) * HD)
            query_head = query_low[..., head_cols]
            key_head = key_back[..., head_cols]
            mixed_head = mixed_grad[..., head_cols]
            scores = (
                jnp.einsum("sqd,skd->sqk", query_head, key_head, preferred_element_type=jnp.float32)
                * score_scale
            )
            scores = jnp.where(allowed, scores, NEG_FILL)
            probs = jnp.exp(scores - log_totals[head_index])
            probs_low = probs.astype(jnp.bfloat16)
            value_parts.append(
                jnp.einsum(
                    "sqk,sqd->skd", probs_low, mixed_head, preferred_element_type=jnp.float32
                )
            )
            probs_grad = jnp.einsum(
                "sqd,skd->sqk",
                mixed_head,
                value_back[..., head_cols],
                preferred_element_type=jnp.float32,
            )
            row_dot = jnp.sum(probs * probs_grad, axis=-1, keepdims=True)
            scores_grad = (probs * (probs_grad - row_dot)).astype(jnp.bfloat16)
            query_parts.append(
                jnp.einsum(
                    "sqk,skd->sqd", scores_grad, key_head, preferred_element_type=jnp.float32
                )
                * score_scale
            )
            key_parts.append(
                jnp.einsum(
                    "sqk,sqd->skd", scores_grad, query_head, preferred_element_type=jnp.float32
                )
                * score_scale
            )
        key_terms = jnp.concatenate(key_parts, axis=-1)
        value_terms = jnp.concatenate(value_parts, axis=-1)
        key_grad_own, value_grad_own = (
            lax.psum_scatter(key_terms, "ctx", scatter_dimension=1, tiled=True),
            lax.psum_scatter(value_terms, "ctx", scatter_dimension=1, tiled=True),
        )
        query_sum = jnp.concatenate(query_parts, axis=-1).reshape(
            seq_local, span_len, head_count, HD
        )
        query_grad = (
            rope_turn(query_sum, cosine, -sine_part)
            .astype(jnp.bfloat16)
            .reshape(row_count, head_count * HD)
        )
        key_grad = (
            rope_turn(key_grad_own.reshape(seq_local, span_len, head_count, HD), cosine, -sine_part)
            .astype(jnp.bfloat16)
            .reshape(row_count, head_count * HD)
        )
        value_grad = value_grad_own.astype(jnp.bfloat16).reshape(row_count, head_count * HD)
        input_terms = (
            dot_rows(query_grad, query_back)
            + dot_rows(key_grad, key_mat)
            + dot_rows(value_grad, value_mat)
        )
        input_sum = (
            lax.psum(input_terms.astype(jnp.bfloat16), "mp")
            .astype(jnp.float32)
            .reshape(seq_local, span_len, feature_width)
        )
        grad_whole = residual_grad + norm_backward(input_sum, normed, inverse_one)
        input_grads.append(
            lax.dynamic_slice_in_dim(grad_whole, model_index * local_width, local_width, 2)
        )
        new_terms = (
            dot_cols(normed_low, query_grad),
            dot_cols(normed_low, key_grad),
            dot_cols(normed_low, value_grad),
            dot_cols(second_low, gate_grad),
            dot_cols(second_low, up_grad),
            dot_cols(mixed_low, residual_low),
            dot_cols(hidden_low, grad_low),
        )
        if totals is None:
            totals = new_terms
        else:
            totals = tuple((older + newer for older, newer in zip(totals, new_terms)))
    grads_total = (
        lax.psum_scatter(
            totals[0].astype(jnp.bfloat16), ("dp", "ctx"), scatter_dimension=0, tiled=True
        ).astype(jnp.float32),
        lax.psum_scatter(
            totals[1].astype(jnp.bfloat16), ("dp", "ctx"), scatter_dimension=0, tiled=True
        ).astype(jnp.float32),
        lax.psum_scatter(
            totals[2].astype(jnp.bfloat16), ("dp", "ctx"), scatter_dimension=0, tiled=True
        ).astype(jnp.float32),
        lax.psum_scatter(
            totals[3].astype(jnp.bfloat16), ("dp", "ctx"), scatter_dimension=0, tiled=True
        ).astype(jnp.float32),
        lax.psum_scatter(
            totals[4].astype(jnp.bfloat16), ("dp", "ctx"), scatter_dimension=0, tiled=True
        ).astype(jnp.float32),
        lax.psum_scatter(
            totals[5].astype(jnp.bfloat16), ("dp", "ctx"), scatter_dimension=1, tiled=True
        ).astype(jnp.float32),
        lax.psum_scatter(
            totals[6].astype(jnp.bfloat16), ("dp", "ctx"), scatter_dimension=1, tiled=True
        ).astype(jnp.float32),
    )
    return (
        jnp.stack(outputs, axis=0),
        jnp.stack(input_grads, axis=0),
        grads_total[0],
        grads_total[1],
        grads_total[2],
        grads_total[5],
        grads_total[3],
        grads_total[4],
        grads_total[6],
    )


MESH = pl.DeviceIdType.MESH
HBM = pl.BlockSpec(memory_space=pl.ANY)
LOW = jnp.bfloat16
FULL = jnp.float32
TILE = 256


def contract(left, right, left_dim, right_dim):
    return lax.dot_general(
        left, right, (((left_dim,), (right_dim,)), ((), ())), preferred_element_type=FULL
    )


def aligned(start, size, unit=None):
    return pl.ds(pl.multiple_of(start, size if unit is None else unit), size)


class Place:
    def __init__(self):
        self.dp = lax.axis_index("dp")
        self.ctx = lax.axis_index("ctx")
        self.mp = lax.axis_index("mp")
        self.high = self.ctx // 2
        self.low = self.ctx % 2
        self.chip = self.mp // 2
        self.core = self.mp % 2
        self.home = self.dp * 4 + self.ctx

    def along(self, mask):
        other = self.ctx + mask - 2 * (self.ctx & mask)
        return (self.dp, other, self.mp)

    def across(self):
        return (1 - self.dp, self.ctx, self.mp)

    def beside_chip(self):
        return (self.dp, self.ctx, (1 - self.chip) * 2 + self.core)

    def beside_core(self):
        return (self.dp, self.ctx, self.chip * 2 + 1 - self.core)

    def shard_rows(self, low, chip, core, size=128):
        return aligned((core * 4 + chip * 2 + low) * 128, size, 128)


class Mover:
    def __init__(self, send, receive, local):
        self.send, self.receive, self.local = send, receive, local
        self.remote_count = 0
        self.local_count = 0

    def to(self, source, target, device):
        slot = self.remote_count
        self.remote_count += 1
        copy = pltpu.make_async_remote_copy(
            src_ref=source,
            dst_ref=target,
            send_sem=self.send.at[slot],
            recv_sem=self.receive.at[slot],
            device_id=device,
            device_id_type=MESH,
        )
        copy.start()
        return copy

    def here(self, source, target):
        slot = self.local_count
        self.local_count += 1
        copy = pltpu.make_async_copy(source, target, self.local.at[slot])
        copy.start()
        return copy


def greet(partners):
    barrier = pltpu.get_barrier_semaphore()
    for partner in partners:
        pl.semaphore_signal(barrier, inc=1, device_id=partner, device_id_type=MESH)
    pl.semaphore_wait(barrier, len(partners))


class GroupGather:
    def __init__(self, place, mover, view, own):
        self.place, self.mover, self.view = place, mover, view
        p = place
        landing = view(p.low, p.chip, p.core)
        self.along = mover.to(own, landing, p.along(1))
        self.chip = mover.to(own, landing, p.beside_chip())
        self.core = mover.to(own, landing, p.beside_core())
        self.sent = [self.along, self.chip, self.core]

    def relay_along(self):
        p = self.place
        self.along.wait_recv()
        piece = self.view(1 - p.low, p.chip, p.core)
        self.corner = self.mover.to(piece, piece, p.beside_chip())
        self.along_core = self.mover.to(piece, piece, p.beside_core())
        self.sent += [self.corner, self.along_core]

    def relay_chip(self):
        p = self.place
        self.chip.wait_recv()
        piece = self.view(p.low, 1 - p.chip, p.core)
        self.chip_core = self.mover.to(piece, piece, p.beside_core())
        self.sent.append(self.chip_core)

    def relay_corner(self):
        p = self.place
        self.corner.wait_recv()
        piece = self.view(1 - p.low, 1 - p.chip, p.core)
        self.corner_core = self.mover.to(piece, piece, p.beside_core())
        self.sent.append(self.corner_core)

    def finish(self):
        for copy in (self.core, self.along_core, self.chip_core, self.corner_core):
            copy.wait_recv()
        for copy in self.sent:
            copy.wait_send()


class GroupScatter:
    def __init__(self, place, mover, buffers, terms):
        self.place, self.mover, self.buffers, self.terms = place, mover, buffers, terms
        self.sent = []

    def half(self, part):
        return pl.ds(part * TILE, TILE)

    def rows(self, chip, core):
        return self.place.shard_rows(0, chip, core, TILE)

    def start_core(self, part):
        p = self.place
        core_send, core_recv = self.buffers[:2]
        chip = 1 - p.chip if part == 0 else p.chip
        core_send[self.half(part), :] = self.terms(self.rows(chip, 1 - p.core)).astype(LOW)
        copy = self.mover.to(
            core_send.at[self.half(part)], core_recv.at[self.half(part)], p.beside_core()
        )
        self.sent.append(copy)
        if part == 0:
            self.core_first = copy
        else:
            self.core_second = copy

    def start_chip(self):
        p = self.place
        core_recv, chip_send, chip_recv = self.buffers[1:4]
        total = self.terms(self.rows(1 - p.chip, p.core))
        self.core_first.wait_recv()
        chip_send[...] = (total + core_recv[self.half(0), :].astype(FULL)).astype(LOW)
        self.chip_copies = []
        for which in (1 - p.low, p.low):
            rows = aligned(which * 128, 128)
            self.chip_copies.append(
                self.mover.to(chip_send.at[rows], chip_recv.at[rows], p.beside_chip())
            )
        self.sent += self.chip_copies

    def start_along(self):
        p = self.place
        core_recv, _, chip_recv, along_send, along_recv, total_ref = self.buffers[1:]
        total = self.terms(self.rows(p.chip, p.core))
        self.core_second.wait_recv()
        total_ref[...] = total + core_recv[self.half(1), :].astype(FULL)
        self.chip_copies[0].wait_recv()
        rows = aligned((1 - p.low) * 128, 128)
        along_send[...] = (total_ref[rows, :] + chip_recv[rows, :].astype(FULL)).astype(LOW)
        self.along = self.mover.to(along_send, along_recv, p.along(1))
        self.sent.append(self.along)

    def result(self):
        p = self.place
        chip_recv, _, along_recv, total_ref = self.buffers[3:]
        self.chip_copies[1].wait_recv()
        rows = aligned(p.low * 128, 128)
        total = total_ref[rows, :] + chip_recv[rows, :].astype(FULL)
        self.along.wait_recv()
        total = total + along_recv[...].astype(FULL)
        for copy in self.sent:
            copy.wait_send()
        return total


def scatter_buffers(width):
    return [
        pltpu.VMEM((2 * TILE, width), LOW),
        pltpu.VMEM((2 * TILE, width), LOW),
        pltpu.VMEM((TILE, width), LOW),
        pltpu.VMEM((TILE, width), LOW),
        pltpu.VMEM((TILE // 2, width), LOW),
        pltpu.VMEM((TILE // 2, width), LOW),
        pltpu.VMEM((TILE, width), FULL),
    ]


class WeightFetch:
    def __init__(self, place, mover, shard, whole, axis, start, size, landing):
        self.place, self.mover = place, mover
        half = shard.shape[axis] // 2
        block = shard.shape[1 - axis]

        def source(which):
            part = aligned(which * half + start, size, 128)
            return shard.at[:, part] if axis == 1 else shard.at[part, :]

        def target(ctx):
            span = aligned((place.dp * 4 + ctx) * block, block, 128)
            part = pl.ds(landing, size)
            return whole.at[span, part] if axis == 1 else whole.at[part, span]

        self.source, self.target = source, target

    def start(self):
        p = self.place
        mine = self.source(p.low)
        other = self.source(1 - p.low)
        spot = self.target(p.ctx)
        self.near = [
            self.mover.to(mine, spot, p.along(2)),
            self.mover.to(other, spot, p.along(3)),
            self.mover.to(other, spot, p.along(1)),
        ]
        self.local = self.mover.here(mine, spot)

    def cross(self):
        p = self.place
        self.far = [self.mover.to(self.source(p.low), self.target(p.ctx), p.across())]
        for copy, mask in ((self.near[2], 1), (self.near[0], 2), (self.near[1], 3)):
            copy.wait_recv()
            block = self.target(p.along(mask)[1])
            self.far.append(self.mover.to(block, block, p.across()))

    def finish(self):
        self.local.wait()
        for copy in self.far:
            copy.wait_recv()

    def drain(self):
        for copy in self.near + self.far:
            copy.wait_send()


def normalise(values):
    centred = values - jnp.mean(values, axis=-1, keepdims=True)
    inverse = lax.rsqrt(jnp.mean(centred * centred, axis=-1, keepdims=True) + EPSILON)
    return centred * inverse, inverse


def allowed_mask(seg_col, seg_row, start, keys):
    rows = seg_col[pl.ds(start, TILE), :][:, :1]
    cols = seg_row[0:1, pl.ds(0, keys)]
    row_place = start + lax.broadcasted_iota(jnp.int32, (TILE, keys), 0)
    col_place = lax.broadcasted_iota(jnp.int32, (TILE, keys), 1)
    return (rows == cols) & (col_place <= row_place)


def turn(values, cosine, sine_part):
    parts = []
    for start in range(0, values.shape[1], HD):
        head = values[:, start : start + HD]
        parts.append(head * cosine + pltpu.roll(head, HD // 2, 1) * sine_part)
    return jnp.concatenate(parts, axis=1)


def attention_kernel(
    tokens_in, out_grad, seg_col_in, seg_row_in, freqs, w_query, w_key, w_value, w_out, w_gate, w_up, w_down,
    qkv_all, out_all, gate_all, up_all, down_all, grads_all, second_all, normed_out,
    query, key, value, mixed, log_total, cosine, sine_part, seg_col, seg_row, residual, inverse_two, kept,
    tokens, qkv_here, out_here, second_rows, core_send, core_recv, chip_send, chip_recv, along_send, along_recv,
    total_ref, send, receive, local,
):
    p = Place()
    mover = Mover(send, receive, local)
    greet([p.along(1), p.along(2), p.along(3), p.across(), p.beside_chip(), p.beside_core()])
    length, width = tokens.shape
    span, feats = tokens_in.shape[2:]
    cols = w_query.shape[1] // 2
    score_scale = 1.0 / math.sqrt(HD)

    def fetch(shard, whole, axis, landing=0, pieces=1):
        size = shard.shape[axis] // 2 // pieces
        return [
            WeightFetch(p, mover, shard, whole, axis, piece * size, size, landing + piece * size)
            for piece in range(pieces)
        ]

    fetch_query = fetch(w_query, qkv_all, 1, 0)
    fetch_key = fetch(w_key, qkv_all, 1, cols)
    fetch_value = fetch(w_value, qkv_all, 1, 2 * cols)
    fetch_out = fetch(w_out, out_all, 0)
    fetch_gate = fetch(w_gate, gate_all, 1, 0, 2)
    fetch_up = fetch(w_up, up_all, 1, 0, 2)
    fetch_down = fetch(w_down, down_all, 0, 0, 2)

    def block_of(whole, ctx, model):
        return whole.at[aligned(ctx * span, span), aligned(model * feats, feats)]

    def own_view(whole):
        return lambda low, chip, core: block_of(whole, p.high * 2 + low, chip * 2 + core)

    def other_view(whole):
        return lambda low, chip, core: block_of(whole, (1 - p.high) * 2 + low, chip * 2 + core)

    seg_copies = []
    for mask in (1, 2, 3):
        goal = p.high if mask == 1 else 1 - p.high
        spot = aligned(p.ctx * span, span)
        seg_copies.append(mover.to(seg_col_in.at[goal], seg_col.at[spot], p.along(mask)))
        seg_copies.append(mover.to(seg_row_in.at[goal], seg_row.at[:, spot], p.along(mask)))
    seg_local = [
        mover.here(seg_col_in.at[p.high], seg_col.at[aligned(p.ctx * span, span)]),
        mover.here(seg_row_in.at[p.high], seg_row.at[:, aligned(p.ctx * span, span)]),
    ]
    here = block_of(tokens, p.ctx, p.mp)
    swap = mover.to(tokens_in.at[1 - p.high, 0], here, p.along(2))
    own_tokens = tokens_in.at[p.high, 0]
    tokens_local = mover.here(own_tokens, here)
    gather_own = GroupGather(p, mover, own_view(tokens), own_tokens)
    for chunk in fetch_query + fetch_key:
        chunk.start()
    for copy in seg_copies:
        copy.wait()
    for copy in seg_local:
        copy.wait()
    for start in range(0, length, TILE):
        rows = pl.ds(start, TILE)
        keys = start + TILE
        allowed = allowed_mask(seg_col, seg_row, start, keys)
        position = jnp.sum(jnp.where(allowed, 1.0, 0.0), axis=1, keepdims=True) - 1.0
        angle = position * freqs[0:1, :]
        cosine[rows, :] = jnp.cos(angle)
        lane = lax.broadcasted_iota(jnp.int32, (TILE, HD), 1)
        sine = jnp.sin(angle)
        sine_part[rows, :] = jnp.where(lane < HD // 2, -sine, sine)
    swap.wait_recv()
    gather_other = GroupGather(
        p, mover, other_view(tokens), block_of(tokens, p.along(2)[1], p.mp)
    )
    fetch_value[0].start()
    gather_own.relay_along()
    gather_own.relay_chip()
    gather_own.relay_corner()
    fetch_query[0].cross()
    gather_other.relay_along()
    gather_other.relay_chip()
    gather_other.relay_corner()
    fetch_out[0].start()
    fetch_key[0].cross()
    tokens_local.wait()
    swap.wait_send()
    gather_own.finish()
    gather_other.finish()
    my_rows = p.shard_rows(p.low, p.chip, p.core)
    kept[...] = tokens[my_rows, :]
    residual[...] = kept[...].astype(FULL)
    for start in range(0, length, 128):
        rows = pl.ds(start, 128)
        tokens[rows, :] = normalise(tokens[rows, :].astype(FULL))[0].astype(LOW)
    normed_copy = mover.here(tokens, normed_out)
    fetch_value[0].cross()
    fetch_gate[0].start()
    for chunk in fetch_query + fetch_key + fetch_value:
        chunk.finish()
    qkv_copy = mover.here(qkv_all, qkv_here)
    qkv_copy.wait()
    for start in range(0, length, TILE):
        rows = pl.ds(start, TILE)
        three = contract(tokens[rows, :], qkv_here[...], 1, 0)
        query[rows, :] = turn(three[:, :cols], cosine[rows, :], sine_part[rows, :]).astype(LOW)
        key[rows, :] = turn(three[:, cols : 2 * cols], cosine[rows, :], sine_part[rows, :]).astype(
            LOW
        )
        value[rows, :] = three[:, 2 * cols :].astype(LOW)

    grads = {}

    def grad_start():
        spot = block_of(grads_all, p.ctx, p.mp)
        own = out_grad.at[p.high, 0]
        grads["swap"] = mover.to(out_grad.at[1 - p.high, 0], spot, p.along(2))
        grads["local"] = mover.here(own, spot)
        grads["own"] = GroupGather(p, mover, own_view(grads_all), own)

    def grad_second():
        grads["swap"].wait_recv()
        grads["other"] = GroupGather(
            p, mover, other_view(grads_all), block_of(grads_all, p.along(2)[1], p.mp)
        )

    pending = [
        fetch_out[0].cross,
        grad_start,
        fetch_gate[1].start,
        grad_second,
        fetch_gate[0].cross,
        lambda: (grads["own"].relay_along(), grads["own"].relay_chip()),
        fetch_up[0].start,
        lambda: (grads["own"].relay_corner(), grads["other"].relay_along()),
        lambda: (grads["other"].relay_chip(), grads["other"].relay_corner()),
        fetch_gate[1].cross,
        fetch_up[1].start,
        fetch_up[0].cross,
        fetch_down[0].start,
        fetch_up[1].cross,
        fetch_down[1].start,
        fetch_down[0].cross,
        fetch_down[1].cross,
    ]

    def pump(count=1):
        for _ in range(min(count, len(pending))):
            pending.pop(0)()

    head_count = cols // HD
    for start in range(0, length, TILE):
        rows = pl.ds(start, TILE)
        keys = start + TILE
        allowed = allowed_mask(seg_col, seg_row, start, keys)
        for head in range(head_count):
            head_cols = pl.ds(head * HD, HD)
            scores = contract(query[rows, head_cols], key[pl.ds(0, keys), head_cols], 1, 1)
            scores = jnp.where(allowed, scores * score_scale, NEG_FILL)
            highest = jnp.max(scores, axis=-1, keepdims=True)
            exp_terms = jnp.exp(scores - highest)
            total_exp = jnp.sum(exp_terms, axis=-1, keepdims=True)
            probs_low = (exp_terms * (1.0 / total_exp)).astype(LOW)
            mixed[rows, head_cols] = contract(
                probs_low, value[pl.ds(0, keys), head_cols], 1, 0
            ).astype(LOW)
            log_total[rows, head_cols] = jnp.broadcast_to(
                highest + jnp.log(total_exp), (TILE, HD)
            )
        pump()
    fetch_out[0].finish()
    out_copy = mover.here(out_all, out_here)
    out_copy.wait()
    scatter = GroupScatter(
        p,
        mover,
        (core_send, core_recv, chip_send, chip_recv, along_send, along_recv, total_ref),
        lambda rows: contract(mixed[rows, :], out_here[...], 1, 0),
    )
    scatter.start_core(0)
    scatter.start_core(1)
    scatter.start_chip()
    pump()
    scatter.start_along()
    pump()
    branch = scatter.result()
    hidden = residual[...] + branch
    residual[...] = hidden
    normed_two, inverse = normalise(hidden)
    inverse_two[...] = jnp.broadcast_to(inverse, inverse_two.shape)
    second_rows[...] = normed_two.astype(LOW)

    def row_view(low, chip, core):
        return second_all.at[p.shard_rows(low, chip, core)]

    second_local = mover.here(second_rows, row_view(p.low, p.chip, p.core))
    gather = GroupGather(p, mover, row_view, second_rows)
    pump(2)
    gather.relay_along()
    gather.relay_chip()
    pump(2)
    gather.relay_corner()
    pump(len(pending))
    for piece in (gather, grads["own"], grads["other"]):
        piece.finish()
    second_local.wait()
    grads["swap"].wait_send()
    grads["local"].wait()
    normed_copy.wait()
    for chunk in fetch_gate + fetch_up + fetch_down:
        chunk.finish()
    for chunk in (
        fetch_query + fetch_key + fetch_value + fetch_out + fetch_gate + fetch_up + fetch_down
    ):
        chunk.drain()


def attention_forward(tokens_in, out_grad, seg_col, seg_row, freqs, weights):
    w_query, w_key, w_value, w_out, w_gate, w_up, w_down = weights
    span = tokens_in.shape[2]
    length, width = 4 * span, 4 * tokens_in.shape[3]
    cols = w_query.shape[1] // 2
    hidden = w_gate.shape[1] // 2

    def low(*shape):
        return jax.ShapeDtypeStruct(shape, LOW)

    def full(*shape):
        return jax.ShapeDtypeStruct(shape, FULL)

    in_hbm = [
        low(width, 3 * cols), low(cols, width), low(width, hidden), low(width, hidden), low(hidden, width),
        low(length, width), low(length, width), low(length, width),
    ]
    in_vmem = [
        low(length, cols), low(length, cols), low(length, cols), low(length, cols), full(length, cols),
        full(length, HD), full(length, HD), full(length, HD), full(8, length), full(length // 8, width),
        full(length // 8, HD), low(length // 8, width),
    ]
    vmem = pl.BlockSpec(memory_space=pltpu.VMEM)
    return pl.pallas_call(
        attention_kernel,
        out_shape=in_hbm + in_vmem,
        in_specs=[HBM] * 4 + [vmem] + [HBM] * 7,
        out_specs=[HBM] * len(in_hbm) + [vmem] * len(in_vmem),
        scratch_shapes=[
            pltpu.VMEM((length, width), LOW),
            pltpu.VMEM((width, 3 * cols), LOW),
            pltpu.VMEM((cols, width), LOW),
            pltpu.VMEM((length // 8, width), LOW),
            *scatter_buffers(width),
            pltpu.SemaphoreType.DMA((128,)),
            pltpu.SemaphoreType.DMA((128,)),
            pltpu.SemaphoreType.DMA((32,)),
        ],
        compiler_params=pltpu.CompilerParams(
            collective_id=1, has_side_effects=True, vmem_limit_bytes=60 * 1024 * 1024
        ),
    )(tokens_in, out_grad, seg_col, seg_row, freqs, *weights)


class Staging:
    def __init__(self, ref):
        self.ref, self.last = ref, None

    def free(self):
        if self.last is not None:
            self.last.wait()
            self.last = None


class GradReturn:
    def __init__(self, place, mover, axis, terms, sends, receives, loads, stage, out):
        self.place, self.mover, self.axis, self.terms = place, mover, axis, terms
        self.across_send, self.along_send, self.beside_send = sends
        self.across_recv, self.along_recv, self.beside_recv = receives
        self.loads, self.stage, self.out = loads, stage, out
        self.blocks = [place.along(3)[1], place.along(2)[1], place.along(1)[1], place.ctx]
        self.across_copies, self.along_copies = [None] * 4, [None] * 2

    def target(self, which):
        size = self.out.shape[self.axis] // 2
        part = aligned(which * size, size)
        return self.out.at[:, part] if self.axis == 1 else self.out.at[part, :]

    def across(self, step, before=None):
        p = self.place
        value = self.terms((1 - p.dp) * 4 + self.blocks[step]).astype(LOW)
        if before is not None:
            before.across_copies[step].wait_send()
            before.across_copies[step] = None
        self.across_send[step] = value
        self.across_copies[step] = self.mover.to(
            self.across_send.at[step], self.across_recv.at[step], p.across()
        )
        self.recv_across = getattr(self, "recv_across", [])
        self.recv_across.append(self.across_copies[step])

    def summed(self, step, along_step=None):
        p = self.place
        self.recv_across[step].wait_recv()
        first = self.mover.here(self.across_recv.at[step], self.loads[0])
        second = None
        if along_step is not None:
            self.along_recvs[along_step].wait_recv()
            second = self.mover.here(self.along_recv.at[along_step], self.loads[1])
        value = self.terms(p.dp * 4 + self.blocks[step])
        first.wait()
        value = value + self.loads[0][...].astype(FULL)
        if second is not None:
            second.wait()
            value = value + self.loads[1][...].astype(FULL)
        return value

    def along(self, step, before=None):
        value = self.summed(step).astype(LOW)
        if before is not None:
            before.along_copies[step].wait_send()
            before.along_copies[step] = None
        self.along_send[step] = value
        self.along_copies[step] = self.mover.to(
            self.along_send.at[step], self.along_recv.at[step], self.place.along(2)
        )
        self.along_recvs = getattr(self, "along_recvs", [])
        self.along_recvs.append(self.along_copies[step])

    def beside(self, before=None):
        value = self.summed(2, 0).astype(LOW)
        if before is not None:
            before.beside_copy.wait_send()
            before.beside_copy = None
        self.beside_send[...] = value
        self.beside_copy = self.mover.to(
            self.beside_send, self.beside_recv, self.place.along(1)
        )
        self.recv_beside = self.beside_copy

    def own(self):
        value = self.summed(3, 1)
        self.stage.free()
        self.stage.ref[...] = value
        self.stage.last = self.mover.here(self.stage.ref, self.target(self.place.low))

    def last(self):
        self.recv_beside.wait_recv()
        load = self.mover.here(self.beside_recv, self.loads[2])
        load.wait()
        self.stage.free()
        self.stage.ref[...] = self.loads[2][...].astype(FULL)
        self.stage.last = self.mover.here(self.stage.ref, self.target(1 - self.place.low))

    def drain(self):
        for copy in self.across_copies + self.along_copies + [self.beside_copy]:
            if copy is not None:
                copy.wait_send()


def give_credit(place, credit):
    for slot, partner in enumerate((place.beside_core(), place.beside_chip(), place.along(1))):
        pl.semaphore_signal(credit.at[slot], inc=1, device_id=partner, device_id_type=MESH)


def block_cols(ref, block):
    return ref[:, aligned(block * TILE, TILE)]


def feed_kernel(
    second_all, grads_all, gate_all, up_all, down_all,
    residual, inverse_two,
    grad_gate, grad_up, grad_down, back_all, gate_far, gate_mid, gate_near, up_far, up_mid, up_near,
    down_far, down_mid, down_near,
    out_rows, back_rows,
    second, grads, gate_here, up_here, down_here, hidden, gate_back, up_back,
    wide_far, wide_mid, wide_near, wide_loads, wide_stage, tall_far, tall_mid, tall_near, tall_loads, tall_stage,
    core_send, core_recv, chip_send, chip_recv, along_send, along_recv, total_ref,
    back_low, credit, send, receive, local,
):
    p = Place()
    mover = Mover(send, receive, local)
    loads = [
        mover.here(source, target)
        for source, target in (
            (second_all, second), (gate_all, gate_here), (up_all, up_here), (grads_all, grads), (down_all, down_here),
        )
    ]
    greet([p.along(1), p.along(2), p.across(), p.beside_chip(), p.beside_core()])
    for copy in loads:
        copy.wait()
    length = second.shape[0]
    units = hidden.shape[1]

    def one_block(index, carry):
        rows = aligned(index * TILE, TILE)
        for start in range(0, units, TILE):
            cols = pl.ds(start, TILE)
            gate = contract(second[rows, :], gate_here[:, cols], 1, 0)
            up = contract(second[rows, :], up_here[:, cols], 1, 0)
            back = contract(grads[rows, :], down_here[cols, :], 1, 1)
            share = jax.nn.sigmoid(gate)
            silu = gate * share
            hidden[rows, cols] = (silu * up).astype(LOW)
            gate_back[rows, cols] = (back * up * share * (1.0 + gate * (1.0 - share))).astype(LOW)
            up_back[rows, cols] = (back * silu).astype(LOW)
        return carry

    lax.fori_loop(0, length // TILE, one_block, 0)

    wide_staging, tall_staging = Staging(wide_stage), Staging(tall_stage)
    wide_blocks = [wide_loads.at[slot] for slot in range(3)]
    tall_blocks = [tall_loads.at[slot] for slot in range(3)]
    return_down = GradReturn(
        p, mover, 0, lambda block: contract(hidden[...], block_cols(grads, block), 0, 0),
        (tall_far, tall_mid, tall_near), (down_far, down_mid, down_near), tall_blocks, tall_staging, grad_down,
    )
    return_gate = GradReturn(
        p, mover, 1, lambda block: contract(block_cols(second, block), gate_back[...], 0, 0),
        (wide_far, wide_mid, wide_near), (gate_far, gate_mid, gate_near), wide_blocks, wide_staging, grad_gate,
    )
    return_up = GradReturn(
        p, mover, 1, lambda block: contract(block_cols(second, block), up_back[...], 0, 0),
        (wide_far, wide_mid, wide_near), (up_far, up_mid, up_near), wide_blocks, wide_staging, grad_up,
    )
    buffers = (core_send, core_recv, chip_send, chip_recv, along_send, along_recv, total_ref)
    scatter_back = GroupScatter(
        p, mover, buffers,
        lambda rows: contract(gate_back[rows, :], gate_here[...], 1, 1)
        + contract(up_back[rows, :], up_here[...], 1, 1),
    )
    scatter_feed = GroupScatter(
        p, mover, buffers, lambda rows: contract(hidden[rows, :], down_here[...], 1, 0)
    )

    return_down.across(0)
    scatter_back.start_core(0)
    return_down.across(1)
    scatter_back.start_core(1)
    scatter_back.start_chip()
    return_down.across(2)
    return_down.across(3)
    scatter_back.start_along()
    return_gate.across(0)
    return_gate.across(1)
    my_rows = p.shard_rows(p.low, p.chip, p.core)
    normed_grad = scatter_back.result()
    give_credit(p, credit)
    hidden_rows = residual[...]
    inverse = inverse_two[:, :1]
    normed = (hidden_rows - jnp.mean(hidden_rows, axis=-1, keepdims=True)) * inverse
    back_value = grads[my_rows, :].astype(FULL) + norm_backward(normed_grad, normed, inverse)
    back_rows[...] = back_value
    back_low[...] = back_value.astype(LOW)

    def row_view(low, chip, core):
        return back_all.at[p.shard_rows(low, chip, core)]

    back_local = mover.here(back_low, row_view(p.low, p.chip, p.core))
    gather = GroupGather(p, mover, row_view, back_low)
    return_gate.across(2)
    return_gate.across(3)
    return_down.along(0)
    gather.relay_along()
    gather.relay_chip()
    return_down.along(1)
    gather.relay_corner()
    pl.semaphore_wait(credit.at[0], 1)
    scatter_feed.start_core(0)
    return_up.across(0, return_gate)
    return_up.across(1, return_gate)
    scatter_feed.start_core(1)
    pl.semaphore_wait(credit.at[1], 1)
    scatter_feed.start_chip()
    return_gate.along(0)
    return_gate.along(1)
    pl.semaphore_wait(credit.at[2], 1)
    scatter_feed.start_along()
    return_down.beside()
    return_down.own()
    return_up.across(2, return_gate)
    return_up.across(3, return_gate)
    gather.finish()
    back_local.wait()
    out_rows[...] = (hidden_rows + scatter_feed.result()).astype(LOW)
    return_down.last()
    return_gate.beside()
    return_gate.own()
    return_up.along(0, return_gate)
    return_up.along(1, return_gate)
    return_gate.last()
    return_up.beside(return_gate)
    return_up.own()
    return_up.last()
    for part in (return_down, return_gate, return_up):
        part.drain()
    wide_staging.free()
    tall_staging.free()


def feed_both_ways(second_all, grads_all, gate_all, up_all, down_all, residual, inverse_two):
    length, width = second_all.shape
    units = gate_all.shape[1]

    def low(*shape):
        return jax.ShapeDtypeStruct(shape, LOW)

    def full(*shape):
        return jax.ShapeDtypeStruct(shape, FULL)

    wide, tall = (TILE, units), (units, TILE)
    in_hbm = [full(TILE, 2 * units), full(TILE, 2 * units), full(2 * units, TILE), low(length, width)]
    for block in (wide, wide, tall):
        in_hbm += [low(4, *block), low(2, *block), low(*block)]
    in_vmem = [low(length // 8, width), full(length // 8, width)]
    vmem = pl.BlockSpec(memory_space=pltpu.VMEM)

    def sending(block):
        return [
            pltpu.VMEM((4, *block), LOW),
            pltpu.VMEM((2, *block), LOW),
            pltpu.VMEM(block, LOW),
            pltpu.VMEM((3, *block), LOW),
            pltpu.VMEM(block, FULL),
        ]

    outs = pl.pallas_call(
        feed_kernel,
        out_shape=in_hbm + in_vmem,
        in_specs=[HBM] * 5 + [vmem] * 2,
        out_specs=[HBM] * len(in_hbm) + [vmem] * len(in_vmem),
        scratch_shapes=[
            pltpu.VMEM((length, width), LOW),
            pltpu.VMEM((length, width), LOW),
            pltpu.VMEM((width, units), LOW),
            pltpu.VMEM((width, units), LOW),
            pltpu.VMEM((units, width), LOW),
            pltpu.VMEM((length, units), LOW),
            pltpu.VMEM((length, units), LOW),
            pltpu.VMEM((length, units), LOW),
            *sending(wide),
            *sending(tall),
            *scatter_buffers(width),
            pltpu.VMEM((length // 8, width), LOW),
            pltpu.SemaphoreType.REGULAR((3,)),
            pltpu.SemaphoreType.DMA((64,)),
            pltpu.SemaphoreType.DMA((64,)),
            pltpu.SemaphoreType.DMA((64,)),
        ],
        compiler_params=pltpu.CompilerParams(
            collective_id=2, has_side_effects=True, vmem_limit_bytes=62 * 1024 * 1024
        ),
    )(second_all, grads_all, gate_all, up_all, down_all, residual, inverse_two)
    return outs[:4] + outs[-2:]


def xor_permute(values, axis, size, mask):
    return lax.ppermute(values, axis, [(place, place ^ mask) for place in range(size)])


def pick_blocks(blocks, index):
    stack = jnp.stack(blocks, axis=0)
    return [
        lax.dynamic_index_in_dim(stack, index ^ place, 0, keepdims=False)
        for place in range(len(blocks))
    ]


def token_routes(offset):
    routes = []
    for high in range(2):
        for low in range(2):
            for chip in range(2):
                for core in range(2):
                    source = (high * 2 + low) * 4 + chip * 2 + core
                    target = (core * 2 + chip) * 4 + ((2 * high + low) ^ offset)
                    routes.append((source, target))
    return routes


def from_rows(rows, model_index, quarter):
    row_count, width = rows.shape
    parts = jnp.transpose(rows.reshape(row_count, 4, width // 4), (1, 0, 2))
    blocks = []
    for offset in range(4):
        part = lax.dynamic_index_in_dim(parts, quarter ^ offset, 0, keepdims=False)
        blocks.append(lax.ppermute(part, ("ctx", "mp"), token_routes(offset)))
    return jnp.concatenate(pick_blocks(blocks, model_index), axis=0).reshape(
        2, 1, 2 * row_count, width // 4
    )


def half_of(values, axis, which):
    size = values.shape[axis] // 2
    return lax.dynamic_slice_in_dim(values, which * size, size, axis)


def return_grads(grad, axis, dp_index, high, low):
    cut = 1 - axis
    sent = half_of(grad, cut, 1 - dp_index).astype(jnp.bfloat16)
    total = half_of(grad, cut, dp_index) + xor_permute(sent, "dp", 2, 1).astype(jnp.float32)
    sent = half_of(total, cut, 1 - high).astype(jnp.bfloat16)
    total = half_of(total, cut, high) + xor_permute(sent, "ctx", 4, 2).astype(jnp.float32)
    sent = half_of(total, cut, 1 - low).astype(jnp.bfloat16)
    mine = half_of(total, cut, low)
    return mine, xor_permute(sent, "ctx", 4, 1).astype(jnp.float32)


def place_halves(mine, other, axis, low):
    first = jnp.where(low == 0, mine, other)
    second = jnp.where(low == 0, other, mine)
    return jnp.concatenate([first, second], axis=axis)


GROUPS = [
    [(high * 2 + low) * 4 + chip * 2 + core for core in range(2) for chip in range(2) for low in range(2)]
    for high in range(2)
]


def gather_rows(rows):
    return lax.all_gather(rows, ("ctx", "mp"), axis=0, tiled=True, axis_index_groups=GROUPS)


def scatter_rows(terms):
    return lax.psum_scatter(
        terms.astype(jnp.bfloat16),
        ("ctx", "mp"),
        scatter_dimension=0,
        tiled=True,
        axis_index_groups=GROUPS,
    ).astype(jnp.float32)


def per_device_grouped(
    tokens_in, out_grad, segment_ids, w_query, w_key, w_value, w_out, w_gate, w_up, w_down
):
    dp_index = lax.axis_index("dp")
    ctx_index = lax.axis_index("ctx")
    model_index = lax.axis_index("mp")
    high = ctx_index // 2
    low = ctx_index % 2
    quarter = 2 * high + low
    score_scale = 1.0 / math.sqrt(HD)
    span = segment_ids.shape[2]

    segment_float = segment_ids[:, 0].astype(jnp.float32)
    segment_cols = jnp.broadcast_to(segment_float[:, :, None], (2, span, HD))
    segment_rows = jnp.broadcast_to(segment_float[:, None, :], (2, 8, span))
    freq_half = jnp.power(10000.0, -2.0 * jnp.arange(HD // 2, dtype=jnp.float32) / HD)
    freqs = jnp.broadcast_to(jnp.concatenate([freq_half, freq_half])[None], (8, HD))
    (
        query_key_value, out_part, gate_part, up_part, down_part, grad_low, second_low, normed_low,
        query_low, key_low, value_low, mixed_low, log_totals, cosine, sine_part, seg_col, seg_row, residual,
        inverse_wide, kept,
    ) = attention_forward(
        tokens_in, out_grad, segment_cols, segment_rows, freqs,
        (w_query, w_key, w_value, w_out, w_gate, w_up, w_down),
    )
    length = seg_col.shape[0]
    row_count = length // 8
    local_cols = query_low.shape[1]
    head_count = local_cols // HD
    normed_rows, inverse_one = layer_norm(kept.astype(jnp.float32))
    places = jnp.arange(length, dtype=jnp.int32)
    allowed = (seg_col[:, :1] == seg_row[:1]) & (places[None, :] <= places[:, None])

    def turned(values, sine_used):
        parts = values.reshape(length, head_count, 2, HD // 2)
        swapped = jnp.concatenate([parts[:, :, 1:], parts[:, :, :1]], axis=2)
        return (
            (
                parts * cosine.reshape(length, 1, 2, HD // 2)
                + swapped * sine_used.reshape(length, 1, 2, HD // 2)
            )
            .astype(jnp.bfloat16)
            .reshape(length, local_cols)
        )

    grad_gate, grad_up, grad_down, residual_low, out_rows, residual_grad = feed_both_ways(
        second_low, grad_low, gate_part, up_part, down_part, residual, inverse_wide
    )
    tokens_out = from_rows(out_rows, model_index, quarter)
    out_grads = return_grads(dot_cols(mixed_low, residual_low), 0, dp_index, high, low)
    mixed_grad = dot_rows(residual_low, out_part).astype(jnp.bfloat16)
    query_parts = []
    key_parts = []
    value_parts = []
    for head_index in range(head_count):
        cols = slice(head_index * HD, (head_index + 1) * HD)
        query_head = query_low[:, cols]
        key_head = key_low[:, cols]
        mixed_head = mixed_grad[:, cols]
        scores = dot_rows(query_head, key_head) * score_scale
        scores = jnp.where(allowed, scores, NEG_FILL)
        probs = jnp.exp(scores - log_totals[:, head_index * HD : head_index * HD + 1])
        value_parts.append(dot_cols(probs.astype(jnp.bfloat16), mixed_head))
        probs_grad = dot_rows(mixed_head, value_low[:, cols])
        row_dot = jnp.sum(probs * probs_grad, axis=-1, keepdims=True)
        scores_grad = (probs * (probs_grad - row_dot)).astype(jnp.bfloat16)
        query_parts.append(
            jnp.dot(scores_grad, key_head, preferred_element_type=jnp.float32) * score_scale
        )
        key_parts.append(dot_cols(scores_grad, query_head) * score_scale)
    query_grad = turned(jnp.concatenate(query_parts, axis=-1), -sine_part)
    key_grad = turned(jnp.concatenate(key_parts, axis=-1), -sine_part)
    value_grad = jnp.concatenate(value_parts, axis=-1).astype(jnp.bfloat16)
    three_grad = jnp.concatenate([query_grad, key_grad, value_grad], axis=-1)
    input_sum = scatter_rows(dot_rows(three_grad, query_key_value))
    three_grads = return_grads(dot_cols(normed_low, three_grad), 1, dp_index, high, low)
    grad_in_rows = residual_grad + norm_backward(input_sum, normed_rows, inverse_one)
    grad_in = from_rows(grad_in_rows.astype(jnp.bfloat16), model_index, quarter)

    def columns(pair, which):
        cols = slice(which * local_cols, (which + 1) * local_cols)
        return place_halves(pair[0][:, cols], pair[1][:, cols], 1, low)

    return (
        tokens_out,
        grad_in.astype(jnp.float32),
        columns(three_grads, 0),
        columns(three_grads, 1),
        columns(three_grads, 2),
        place_halves(*out_grads, 0, low),
        grad_gate,
        grad_up,
        grad_down,
    )


def solution(mesh):
    in_specs = (
        P(None, "dp", "ctx", "mp"),
        P(None, "dp", "ctx", "mp"),
        P(None, "dp", "ctx"),
        P(("dp", "ctx"), "mp"),
        P(("dp", "ctx"), "mp"),
        P(("dp", "ctx"), "mp"),
        P("mp", ("dp", "ctx")),
        P(("dp", "ctx"), "mp"),
        P(("dp", "ctx"), "mp"),
        P("mp", ("dp", "ctx")),
    )
    out_specs = (
        P(None, "dp", "ctx", "mp"),
        P(None, "dp", "ctx", "mp"),
        P(("dp", "ctx"), "mp"),
        P(("dp", "ctx"), "mp"),
        P(("dp", "ctx"), "mp"),
        P("mp", ("dp", "ctx")),
        P(("dp", "ctx"), "mp"),
        P(("dp", "ctx"), "mp"),
        P("mp", ("dp", "ctx")),
    )
    grouped = mesh.shape["ctx"] == 4 and mesh.shape["mp"] == 4 and mesh.shape["dp"] == 2
    per_device = per_device_grouped if grouped else per_device_general
    return jax.shard_map(
        per_device, mesh=mesh, in_specs=in_specs, out_specs=out_specs, check_vma=False
    )
```

```python
import functools
import math
import types

import jax
import jax.numpy as jnp
from jax import lax
from jax.experimental import pallas as pl
from jax.experimental.pallas import tpu as pltpu
from jax.sharding import PartitionSpec as P

HD = 128


EPSILON = 1e-05
NEG_FILL = -1e30


def layer_norm(values):
    centred = values - jnp.mean(values, axis=-1, keepdims=True)
    inverse = lax.rsqrt(jnp.mean(centred * centred, axis=-1, keepdims=True) + EPSILON)
    return (centred * inverse, inverse)


def norm_backward(upstream, normed, inverse):
    plain_mean = jnp.mean(upstream, axis=-1, keepdims=True)
    cross_mean = jnp.mean(upstream * normed, axis=-1, keepdims=True)
    return inverse * (upstream - plain_mean - normed * cross_mean)


def doc_positions(segment):
    length = segment.shape[-1]
    places = jnp.arange(length, dtype=jnp.int32)
    opening = jnp.ones(segment.shape[:-1] + (1,), dtype=bool)
    change = jnp.concatenate([opening, segment[..., 1:] != segment[..., :-1]], axis=-1)
    starts = lax.cummax(jnp.where(change, places, jnp.int32(0)), axis=segment.ndim - 1)
    return places - starts


def rope_angles(positions):
    freq_table = jnp.power(10000.0, -2.0 * jnp.arange(HD // 2, dtype=jnp.float32) / HD)
    turned = positions.astype(jnp.float32)[..., None] * freq_table
    return (jnp.cos(turned), jnp.sin(turned))


def rope_turn(values, cosine, sine_part):
    half_size = values.shape[-1] // 2
    leading = values[..., :half_size]
    trailing = values[..., half_size:]
    return jnp.concatenate(
        [leading * cosine - trailing * sine_part, trailing * cosine + leading * sine_part], axis=-1
    )


def dot_rows(left_mat, right_mat):
    return lax.dot_general(
        left_mat, right_mat, (((1,), (1,)), ((), ())), preferred_element_type=jnp.float32
    )


def dot_cols(left_mat, right_mat):
    return lax.dot_general(
        left_mat, right_mat, (((0,), (0,)), ((), ())), preferred_element_type=jnp.float32
    )


def fetch_weights(w_query, w_key, w_value, w_gate, w_up, w_out, w_down):
    return (
        lax.all_gather(w_query, ("dp", "ctx"), axis=0, tiled=True),
        lax.all_gather(w_key, ("dp", "ctx"), axis=0, tiled=True),
        lax.all_gather(w_value, ("dp", "ctx"), axis=0, tiled=True),
        lax.all_gather(w_gate, ("dp", "ctx"), axis=0, tiled=True),
        lax.all_gather(w_up, ("dp", "ctx"), axis=0, tiled=True),
        lax.all_gather(w_out, ("dp", "ctx"), axis=1, tiled=True),
        lax.all_gather(w_down, ("dp", "ctx"), axis=1, tiled=True),
    )


def per_device_general(
    tokens_in, out_grad, segment_ids, w_query, w_key, w_value, w_out, w_gate, w_up, w_down
):
    micro_count = tokens_in.shape[0]
    seq_local = tokens_in.shape[1]
    span_len = tokens_in.shape[2]
    local_width = tokens_in.shape[3]
    ctx_index = lax.axis_index("ctx")
    model_index = lax.axis_index("mp")
    tokens_all, grads_all = (
        lax.all_gather(tokens_in, "mp", axis=3, tiled=True),
        lax.all_gather(out_grad, "mp", axis=3, tiled=True),
    )
    segments_all = lax.all_gather(segment_ids, "ctx", axis=2, tiled=True)
    feature_width = tokens_all.shape[3]
    seq_length = segments_all.shape[2]
    row_count = seq_local * span_len
    score_scale = 1.0 / math.sqrt(HD)
    positions = doc_positions(segments_all)
    query_places = ctx_index * span_len + jnp.arange(span_len, dtype=jnp.int32)
    key_places = jnp.arange(seq_length, dtype=jnp.int32)
    causal = key_places[None, :] <= query_places[:, None]
    outputs = []
    input_grads = []
    totals = None
    for micro_step in range(micro_count):
        full_weights = fetch_weights(w_query, w_key, w_value, w_gate, w_up, w_out, w_down)
        query_full, key_full, value_full, gate_full, up_full, out_full, down_full = full_weights
        head_count = query_full.shape[1] // HD
        segment_seq = segments_all[micro_step]
        segment_own = lax.dynamic_slice_in_dim(segment_seq, ctx_index * span_len, span_len, 1)
        position_own = lax.dynamic_slice_in_dim(
            positions[micro_step], ctx_index * span_len, span_len, 1
        )
        allowed = (segment_own[:, :, None] == segment_seq[:, None, :]) & causal[None]
        cosine, sine_part = rope_angles(position_own)
        cosine = cosine[:, :, None, :]
        sine_part = sine_part[:, :, None, :]
        inputs = tokens_all[micro_step].astype(jnp.float32)
        normed, inverse_one = layer_norm(inputs)
        normed_low = normed.astype(jnp.bfloat16).reshape(row_count, feature_width)

        def project(matrix):
            product = jnp.dot(normed_low, matrix, preferred_element_type=jnp.float32)
            return product.reshape(seq_local, span_len, head_count, HD)

        query_low = (
            rope_turn(project(query_full), cosine, sine_part)
            .astype(jnp.bfloat16)
            .reshape(seq_local, span_len, head_count * HD)
        )
        key_low = (
            rope_turn(project(key_full), cosine, sine_part)
            .astype(jnp.bfloat16)
            .reshape(seq_local, span_len, head_count * HD)
        )
        value_low = (
            project(value_full).astype(jnp.bfloat16).reshape(seq_local, span_len, head_count * HD)
        )
        key_seq, value_seq = (
            lax.all_gather(key_low, "ctx", axis=1, tiled=True),
            lax.all_gather(value_low, "ctx", axis=1, tiled=True),
        )
        mixed_parts = []
        log_totals = []
        for head_index in range(head_count):
            head_cols = slice(head_index * HD, (head_index + 1) * HD)
            scores = (
                jnp.einsum(
                    "sqd,skd->sqk",
                    query_low[..., head_cols],
                    key_seq[..., head_cols],
                    preferred_element_type=jnp.float32,
                )
                * score_scale
            )
            scores = jnp.where(allowed, scores, NEG_FILL)
            highest = jnp.max(scores, axis=-1, keepdims=True)
            exp_terms = jnp.exp(scores - highest)
            total_exp = jnp.sum(exp_terms, axis=-1, keepdims=True)
            probs_low = (exp_terms / total_exp).astype(jnp.bfloat16)
            mixed_parts.append(
                jnp.einsum(
                    "sqk,skd->sqd",
                    probs_low,
                    value_seq[..., head_cols],
                    preferred_element_type=jnp.float32,
                )
            )
            log_totals.append(highest + jnp.log(total_exp))
        mixed_low = (
            jnp.concatenate(mixed_parts, axis=-1)
            .astype(jnp.bfloat16)
            .reshape(row_count, head_count * HD)
        )
        branch = jnp.dot(mixed_low, out_full, preferred_element_type=jnp.float32)
        branch = lax.psum(branch, "mp")
        residual = inputs + branch.reshape(seq_local, span_len, feature_width)
        normed_two, inverse_two = layer_norm(residual)
        second_low = normed_two.astype(jnp.bfloat16).reshape(row_count, feature_width)
        gate_lin = jnp.dot(second_low, gate_full, preferred_element_type=jnp.float32)
        up_lin = jnp.dot(second_low, up_full, preferred_element_type=jnp.float32)
        sigmoid_gate = jax.nn.sigmoid(gate_lin)
        hidden_low = (gate_lin * sigmoid_gate * up_lin).astype(jnp.bfloat16)
        feed_terms = jnp.dot(hidden_low, down_full, preferred_element_type=jnp.float32).reshape(
            seq_local, span_len, feature_width
        )
        feed_own = lax.psum_scatter(
            feed_terms.astype(jnp.bfloat16), "mp", scatter_dimension=2, tiled=True
        ).astype(jnp.float32)
        residual_own = lax.dynamic_slice_in_dim(residual, model_index * local_width, local_width, 2)
        outputs.append((residual_own + feed_own).astype(jnp.bfloat16))
        back_weights = (
            lax.all_gather(w_query, ("dp", "ctx"), axis=0, tiled=True),
            lax.all_gather(w_key, ("dp", "ctx"), axis=0, tiled=True),
            lax.all_gather(w_value, ("dp", "ctx"), axis=0, tiled=True),
            lax.all_gather(w_gate, ("dp", "ctx"), axis=0, tiled=True),
            lax.all_gather(w_up, ("dp", "ctx"), axis=0, tiled=True),
            lax.all_gather(w_out, ("dp", "ctx"), axis=1, tiled=True),
            lax.all_gather(w_down, ("dp", "ctx"), axis=1, tiled=True),
        )
        key_back, value_back = (
            lax.all_gather(key_low, "ctx", axis=1, tiled=True),
            lax.all_gather(value_low, "ctx", axis=1, tiled=True),
        )
        query_back, key_mat, value_mat, gate_back, up_back, out_back, down_back = back_weights
        grad_low = grads_all[micro_step].reshape(row_count, feature_width)
        grad_float = grads_all[micro_step].astype(jnp.float32)
        hidden_grad = dot_rows(grad_low, down_back)
        gate_grad = (
            hidden_grad * up_lin * sigmoid_gate * (1.0 + gate_lin * (1.0 - sigmoid_gate))
        ).astype(jnp.bfloat16)
        up_grad = (hidden_grad * gate_lin * sigmoid_gate).astype(jnp.bfloat16)
        normed_grad = dot_rows(gate_grad, gate_back) + dot_rows(up_grad, up_back)
        normed_grad = lax.psum(normed_grad, "mp").reshape(seq_local, span_len, feature_width)
        residual_grad = grad_float + norm_backward(normed_grad, normed_two, inverse_two)
        residual_low = residual_grad.astype(jnp.bfloat16).reshape(row_count, feature_width)
        mixed_grad = (
            dot_rows(residual_low, out_back)
            .astype(jnp.bfloat16)
            .reshape(seq_local, span_len, head_count * HD)
        )
        query_parts = []
        key_parts = []
        value_parts = []
        for head_index in range(head_count):
            head_cols = slice(head_index * HD, (head_index + 1) * HD)
            query_head = query_low[..., head_cols]
            key_head = key_back[..., head_cols]
            mixed_head = mixed_grad[..., head_cols]
            scores = (
                jnp.einsum("sqd,skd->sqk", query_head, key_head, preferred_element_type=jnp.float32)
                * score_scale
            )
            scores = jnp.where(allowed, scores, NEG_FILL)
            probs = jnp.exp(scores - log_totals[head_index])
            probs_low = probs.astype(jnp.bfloat16)
            value_parts.append(
                jnp.einsum(
                    "sqk,sqd->skd", probs_low, mixed_head, preferred_element_type=jnp.float32
                )
            )
            probs_grad = jnp.einsum(
                "sqd,skd->sqk",
                mixed_head,
                value_back[..., head_cols],
                preferred_element_type=jnp.float32,
            )
            row_dot = jnp.sum(probs * probs_grad, axis=-1, keepdims=True)
            scores_grad = (probs * (probs_grad - row_dot)).astype(jnp.bfloat16)
            query_parts.append(
                jnp.einsum(
                    "sqk,skd->sqd", scores_grad, key_head, preferred_element_type=jnp.float32
                )
                * score_scale
            )
            key_parts.append(
                jnp.einsum(
                    "sqk,sqd->skd", scores_grad, query_head, preferred_element_type=jnp.float32
                )
                * score_scale
            )
        key_terms = jnp.concatenate(key_parts, axis=-1)
        value_terms = jnp.concatenate(value_parts, axis=-1)
        key_grad_own, value_grad_own = (
            lax.psum_scatter(key_terms, "ctx", scatter_dimension=1, tiled=True),
            lax.psum_scatter(value_terms, "ctx", scatter_dimension=1, tiled=True),
        )
        query_sum = jnp.concatenate(query_parts, axis=-1).reshape(
            seq_local, span_len, head_count, HD
        )
        query_grad = (
            rope_turn(query_sum, cosine, -sine_part)
            .astype(jnp.bfloat16)
            .reshape(row_count, head_count * HD)
        )
        key_grad = (
            rope_turn(key_grad_own.reshape(seq_local, span_len, head_count, HD), cosine, -sine_part)
            .astype(jnp.bfloat16)
            .reshape(row_count, head_count * HD)
        )
        value_grad = value_grad_own.astype(jnp.bfloat16).reshape(row_count, head_count * HD)
        input_terms = (
            dot_rows(query_grad, query_back)
            + dot_rows(key_grad, key_mat)
            + dot_rows(value_grad, value_mat)
        )
        input_sum = (
            lax.psum(input_terms.astype(jnp.bfloat16), "mp")
            .astype(jnp.float32)
            .reshape(seq_local, span_len, feature_width)
        )
        grad_whole = residual_grad + norm_backward(input_sum, normed, inverse_one)
        input_grads.append(
            lax.dynamic_slice_in_dim(grad_whole, model_index * local_width, local_width, 2)
        )
        new_terms = (
            dot_cols(normed_low, query_grad),
            dot_cols(normed_low, key_grad),
            dot_cols(normed_low, value_grad),
            dot_cols(second_low, gate_grad),
            dot_cols(second_low, up_grad),
            dot_cols(mixed_low, residual_low),
            dot_cols(hidden_low, grad_low),
        )
        if totals is None:
            totals = new_terms
        else:
            totals = tuple((older + newer for older, newer in zip(totals, new_terms)))
    grads_total = (
        lax.psum_scatter(
            totals[0].astype(jnp.bfloat16), ("dp", "ctx"), scatter_dimension=0, tiled=True
        ).astype(jnp.float32),
        lax.psum_scatter(
            totals[1].astype(jnp.bfloat16), ("dp", "ctx"), scatter_dimension=0, tiled=True
        ).astype(jnp.float32),
        lax.psum_scatter(
            totals[2].astype(jnp.bfloat16), ("dp", "ctx"), scatter_dimension=0, tiled=True
        ).astype(jnp.float32),
        lax.psum_scatter(
            totals[3].astype(jnp.bfloat16), ("dp", "ctx"), scatter_dimension=0, tiled=True
        ).astype(jnp.float32),
        lax.psum_scatter(
            totals[4].astype(jnp.bfloat16), ("dp", "ctx"), scatter_dimension=0, tiled=True
        ).astype(jnp.float32),
        lax.psum_scatter(
            totals[5].astype(jnp.bfloat16), ("dp", "ctx"), scatter_dimension=1, tiled=True
        ).astype(jnp.float32),
        lax.psum_scatter(
            totals[6].astype(jnp.bfloat16), ("dp", "ctx"), scatter_dimension=1, tiled=True
        ).astype(jnp.float32),
    )
    return (
        jnp.stack(outputs, axis=0),
        jnp.stack(input_grads, axis=0),
        grads_total[0],
        grads_total[1],
        grads_total[2],
        grads_total[5],
        grads_total[3],
        grads_total[4],
        grads_total[6],
    )


MESH = pl.DeviceIdType.MESH
HBM = pl.BlockSpec(memory_space=pl.ANY)
LOW = jnp.bfloat16
FULL = jnp.float32
TILE = 256
PIECES = 4
VMEM_BYTES = 63 * 1024 * 1024


def contract(left, right, left_dim, right_dim):
    return lax.dot_general(
        left, right, (((left_dim,), (right_dim,)), ((), ())), preferred_element_type=FULL
    )


def aligned(start, size, unit=None):
    return pl.ds(pl.multiple_of(start, size if unit is None else unit), size)


class Place:
    def __init__(self):
        self.dp = lax.axis_index("dp")
        self.ctx = lax.axis_index("ctx")
        self.mp = lax.axis_index("mp")
        self.high = self.ctx // 2
        self.low = self.ctx % 2
        self.chip = self.mp // 2
        self.core = self.mp % 2
        self.home = self.dp * 4 + self.ctx
        self.inner = self.high != self.low

    def along(self, mask):
        other = self.ctx + mask - 2 * (self.ctx & mask)
        return (self.dp, other, self.mp)

    def across(self):
        return (1 - self.dp, self.ctx, self.mp)

    def beside_chip(self):
        return (self.dp, self.ctx, (1 - self.chip) * 2 + self.core)

    def beside_core(self):
        return (self.dp, self.ctx, self.chip * 2 + 1 - self.core)

    def shard_rows(self, low, chip, core, size=128):
        return aligned((core * 4 + chip * 2 + low) * 128, size, 128)


class Mover:
    def __init__(self, send, receive, local):
        self.send, self.receive, self.local = send, receive, local
        self.remote_count = 0
        self.local_count = 0

    def to(self, source, target, device):
        slot = self.remote_count
        self.remote_count += 1
        copy = pltpu.make_async_remote_copy(
            src_ref=source,
            dst_ref=target,
            send_sem=self.send.at[slot],
            recv_sem=self.receive.at[slot],
            device_id=device,
            device_id_type=MESH,
        )
        copy.start()
        return copy

    def hold(self, source, target, device, receive_slot=None):
        slot = self.remote_count
        self.remote_count += 1
        copy = pltpu.make_async_remote_copy(
            src_ref=source,
            dst_ref=target,
            send_sem=self.send.at[slot],
            recv_sem=self.receive.at[slot if receive_slot is None else receive_slot],
            device_id=device,
            device_id_type=MESH,
        )
        return HeldCopy(copy, slot)

    def here(self, source, target):
        slot = self.local_count
        self.local_count += 1
        copy = pltpu.make_async_copy(source, target, self.local.at[slot])
        copy.start()
        return copy


class HeldCopy:
    def __init__(self, copy, slot):
        self.copy, self.slot = copy, slot

    def start_if(self, wanted):
        @pl.when(wanted)
        def _():
            self.copy.start()

    def wait_send_if(self, wanted):
        @pl.when(wanted)
        def _():
            self.copy.wait_send()

    def wait_recv(self):
        self.copy.wait_recv()


def greet(partners):
    barrier = pltpu.get_barrier_semaphore()
    for partner in partners:
        pl.semaphore_signal(barrier, inc=1, device_id=partner, device_id_type=MESH)
    pl.semaphore_wait(barrier, len(partners))


class GroupGather:
    def __init__(self, place, mover, view, own):
        self.place, self.mover, self.view = place, mover, view
        p = place
        landing = view(p.low, p.chip, p.core)
        self.along = mover.to(own, landing, p.along(1))
        self.chip = mover.to(own, landing, p.beside_chip())
        self.core = mover.to(own, landing, p.beside_core())
        self.sent = [self.along, self.chip, self.core]

    def relay_along(self):
        p = self.place
        self.along.wait_recv()
        piece = self.view(1 - p.low, p.chip, p.core)
        self.corner = self.mover.to(piece, piece, p.beside_chip())
        self.along_core = self.mover.to(piece, piece, p.beside_core())
        self.sent += [self.corner, self.along_core]

    def relay_chip(self):
        p = self.place
        self.chip.wait_recv()
        piece = self.view(p.low, 1 - p.chip, p.core)
        self.chip_core = self.mover.to(piece, piece, p.beside_core())
        self.sent.append(self.chip_core)

    def relay_corner(self):
        p = self.place
        self.corner.wait_recv()
        piece = self.view(1 - p.low, 1 - p.chip, p.core)
        self.corner_core = self.mover.to(piece, piece, p.beside_core())
        self.sent.append(self.corner_core)

    def finish(self):
        for copy in (self.core, self.along_core, self.chip_core, self.corner_core):
            copy.wait_recv()
        for copy in self.sent:
            copy.wait_send()


class GroupScatter:
    def __init__(self, place, mover, buffers, terms):
        self.place, self.mover, self.buffers, self.terms = place, mover, buffers, terms
        self.sent = []

    def half(self, part):
        return pl.ds(part * TILE, TILE)

    def rows(self, chip, core):
        return self.place.shard_rows(0, chip, core, TILE)

    def start_core(self, part):
        p = self.place
        core_send, core_recv = self.buffers[:2]
        chip = 1 - p.chip if part == 0 else p.chip
        core_send[self.half(part), :] = self.terms(self.rows(chip, 1 - p.core)).astype(LOW)
        copy = self.mover.to(
            core_send.at[self.half(part)], core_recv.at[self.half(part)], p.beside_core()
        )
        self.sent.append(copy)
        if part == 0:
            self.core_first = copy
        else:
            self.core_second = copy

    def start_chip(self):
        p = self.place
        core_recv, chip_send, chip_recv = self.buffers[1:4]
        total = self.terms(self.rows(1 - p.chip, p.core))
        self.core_first.wait_recv()
        chip_send[...] = (total + core_recv[self.half(0), :].astype(FULL)).astype(LOW)
        self.chip_copies = []
        for which in (1 - p.low, p.low):
            rows = aligned(which * 128, 128)
            self.chip_copies.append(
                self.mover.to(chip_send.at[rows], chip_recv.at[rows], p.beside_chip())
            )
        self.sent += self.chip_copies

    def start_along(self):
        p = self.place
        core_recv, _, chip_recv, along_send, along_recv, total_ref = self.buffers[1:]
        total = self.terms(self.rows(p.chip, p.core))
        self.core_second.wait_recv()
        total_ref[...] = total + core_recv[self.half(1), :].astype(FULL)
        self.chip_copies[0].wait_recv()
        rows = aligned((1 - p.low) * 128, 128)
        along_send[...] = (total_ref[rows, :] + chip_recv[rows, :].astype(FULL)).astype(LOW)
        self.along = self.mover.to(along_send, along_recv, p.along(1))
        self.sent.append(self.along)

    def result(self):
        p = self.place
        chip_recv, _, along_recv, total_ref = self.buffers[3:]
        self.chip_copies[1].wait_recv()
        rows = aligned(p.low * 128, 128)
        total = total_ref[rows, :] + chip_recv[rows, :].astype(FULL)
        self.along.wait_recv()
        total = total + along_recv[...].astype(FULL)
        for copy in self.sent:
            copy.wait_send()
        return total


def scatter_buffers(width):
    return [
        pltpu.VMEM((2 * TILE, width), LOW),
        pltpu.VMEM((2 * TILE, width), LOW),
        pltpu.VMEM((TILE, width), LOW),
        pltpu.VMEM((TILE, width), LOW),
        pltpu.VMEM((TILE // 2, width), LOW),
        pltpu.VMEM((TILE // 2, width), LOW),
        pltpu.VMEM((TILE, width), FULL),
    ]


class WeightFetch:
    def __init__(self, place, mover, shard, whole, axis, start, size, landing):
        self.place, self.mover = place, mover
        half = shard.shape[axis] // 2
        block = shard.shape[1 - axis]

        def source(which):
            part = aligned(which * half + start, size, 128)
            return shard.at[:, part] if axis == 1 else shard.at[part, :]

        def target(ctx):
            span = aligned((place.dp * 4 + ctx) * block, block, 128)
            part = pl.ds(landing, size)
            return whole.at[span, part] if axis == 1 else whole.at[part, span]

        self.source, self.target = source, target

    def start(self):
        p = self.place
        mine = self.source(p.low)
        other = self.source(1 - p.low)
        spot = self.target(p.ctx)
        self.beside = self.mover.to(other, spot, p.along(1))
        self.corner = self.mover.hold(other, spot, p.along(3))
        self.corner.start_if(p.inner)
        self.ahead = self.mover.to(mine, spot, p.along(2))
        self.far = []

    def start_own(self):
        p = self.place
        mine, spot = self.source(p.low), self.target(p.ctx)
        self.own_far = self.mover.to(mine, spot, p.across())

    def send_across(self, mask):
        p = self.place
        block = self.target(p.along(mask)[1])
        self.far.append(self.mover.to(block, block, p.across()))

    def forward(self):
        p = self.place
        self.beside.wait_recv()
        block = self.target(p.along(1)[1])
        self.passed = self.mover.hold(block, block, p.along(2), self.corner.slot)
        self.passed.start_if(p.inner)
        self.send_across(1)

    def cross(self):
        self.ahead.wait_recv()
        self.send_across(2)
        self.corner.wait_recv()
        self.send_across(3)

    def finish(self):
        for copy in self.far + [self.own_far]:
            copy.wait_recv()

    def drain(self):
        for copy in self.far + [self.own_far, self.beside, self.ahead]:
            copy.wait_send()
        for copy in (self.corner, self.passed):
            copy.wait_send_if(self.place.inner)


def normalise(values):
    centred = values - jnp.mean(values, axis=-1, keepdims=True)
    inverse = lax.rsqrt(jnp.mean(centred * centred, axis=-1, keepdims=True) + EPSILON)
    return centred * inverse, inverse


def allowed_mask(seg_col, seg_row, start, keys):
    rows = seg_col[pl.ds(start, TILE), :][:, :1]
    cols = seg_row[0:1, pl.ds(0, keys)]
    row_place = start + lax.broadcasted_iota(jnp.int32, (TILE, keys), 0)
    col_place = lax.broadcasted_iota(jnp.int32, (TILE, keys), 1)
    return (rows == cols) & (col_place <= row_place)


def turn(values, cosine, sine_part):
    parts = []
    for start in range(0, values.shape[1], HD):
        head = values[:, start : start + HD]
        parts.append(head * cosine + pltpu.roll(head, HD // 2, 1) * sine_part)
    return jnp.concatenate(parts, axis=1)


class Staging:
    def __init__(self):
        self.last = None

    def free(self):
        if self.last is not None:
            self.last.wait()
            self.last = None


class GradReturn:
    def __init__(self, place, mover, axis, terms, sends, receives, loads, stage, own_out, before=None):
        self.place, self.mover, self.axis, self.terms = place, mover, axis, terms
        self.across_send, self.along_send, self.beside_send = sends
        self.across_recv, self.along_recv, self.beside_recv = receives
        self.loads, (self.stage, self.stage_ref), self.own_out = loads, stage, own_out
        self.before = before
        self.blocks = [place.along(3)[1], place.along(2)[1], place.along(1)[1], place.ctx]
        self.size = own_out.shape[0]
        self.arriving, self.leaving, self.here = {}, {}, set()

    def send(self, key, source, target, device):
        copy = self.mover.to(source, target, device)
        self.arriving[key] = self.leaving[key] = copy

    def arrived(self, key):
        if key not in self.here:
            self.here.add(key)
            self.arriving[key].wait_recv()

    def free(self, key):
        if self.before is not None:
            self.before.leaving.pop(key).wait_send()

    def part(self, half):
        count = self.size // 2
        return pl.ds(0, self.size) if half is None else pl.ds(half * count, count)

    def across(self, step):
        p = self.place
        value = self.terms((1 - p.dp) * 4 + self.blocks[step], self.part(None)).astype(LOW)
        self.free((0, step))
        self.across_send[step] = value
        self.send((0, step), self.across_send.at[step], self.across_recv.at[step], p.across())

    def summed(self, step, half, others):
        part = self.part(half)
        self.arrived((0, step))
        copies = [
            self.mover.here(self.across_recv.at[step, part, :], self.loads.at[0, part, :])
        ]
        for along_half in others:
            self.arrived((1, step - 2, along_half))
            spot = self.part(along_half)
            copies.append(
                self.mover.here(self.along_recv.at[step - 2, spot, :], self.loads.at[1, spot, :])
            )
        value = self.terms(self.place.dp * 4 + self.blocks[step], part)
        for copy in copies:
            copy.wait()
        value = value + self.loads[0, part, :].astype(FULL)
        if others:
            value = value + self.loads[1, part, :].astype(FULL)
        return value

    def along(self, step, half):
        part = self.part(half)
        value = self.summed(step, half, ()).astype(LOW)
        self.free((1, step, half))
        self.along_send[step, part, :] = value
        source = self.along_send.at[step, part, :]
        target = self.along_recv.at[step, part, :]
        self.send((1, step, half), source, target, self.place.along(2))

    def beside(self, half):
        part = self.part(half)
        value = self.summed(2, half, (half,)).astype(LOW)
        self.free((2, half))
        self.beside_send[part, :] = value
        source, target = self.beside_send.at[part, :], self.beside_recv.at[part, :]
        self.send((2, half), source, target, self.place.along(1))

    def own(self):
        value = self.summed(3, None, (0, 1))
        self.stage.free()
        self.stage_ref[...] = value
        self.stage.last = self.mover.here(self.stage_ref, self.own_out)

    def drain(self):
        for half in range(2):
            self.arrived((2, half))
        for copy in self.leaving.values():
            copy.wait_send()


def give_credit(place, credit):
    for slot, partner in enumerate((place.beside_core(), place.beside_chip(), place.along(1))):
        pl.semaphore_signal(credit.at[slot], inc=1, device_id=partner, device_id_type=MESH)


def block_cols(ref, block):
    return ref[:, aligned(block * TILE, TILE)]


class RowReturn:
    def __init__(self, place, send, receive, local):
        self.place, self.send, self.receive, self.local = place, send, receive, local
        self.goal = place.core * 2 + place.chip
        self.stays = place.ctx == self.goal

    def partners(self):
        p = self.place
        targets = [(p.dp, self.goal, model) for model in range(4)]
        sources = [(p.dp, ctx, p.low * 2 + p.high) for ctx in range(4)]
        return targets, sources

    def greet(self, others):
        p = self.place
        barrier = pltpu.get_barrier_semaphore()
        for other in others:
            pl.semaphore_signal(barrier, inc=1, device_id=other, device_id_type=MESH)
        targets, sources = self.partners()
        for model, target in enumerate(targets):

            @pl.when(jnp.logical_not(self.stays & (p.mp == model)))
            def _(target=target):
                pl.semaphore_signal(barrier, inc=1, device_id=target, device_id_type=MESH)

        for ctx, source in enumerate(sources):

            @pl.when(jnp.logical_not(self.stays & (p.ctx == ctx)))
            def _(source=source):
                pl.semaphore_signal(barrier, inc=1, device_id=source, device_id_type=MESH)

        @pl.when(self.stays)
        def _():
            pl.semaphore_wait(barrier, len(others) + 6)

        @pl.when(jnp.logical_not(self.stays))
        def _():
            pl.semaphore_wait(barrier, len(others) + 8)

    def copy(self, model):
        size = self.rows.shape[1] // 4
        return pltpu.make_async_remote_copy(
            src_ref=self.rows.at[:, pl.ds(model * size, size)],
            dst_ref=self.landing,
            send_sem=self.send.at[model],
            recv_sem=self.receive.at[self.place.ctx],
            device_id=(self.place.dp, self.goal, model),
            device_id_type=MESH,
        )

    def own_copy(self):
        size = self.rows.shape[1] // 4
        source = self.rows.at[:, aligned(self.place.mp * size, size)]
        return pltpu.make_async_copy(source, self.landing, self.local)

    def start(self, rows, whole):
        p = self.place
        self.rows, self.whole = rows, whole
        count = rows.shape[0]
        self.landing = whole.at[p.high, 0, aligned(p.low * count, count), :]
        for model in range(4):

            @pl.when(jnp.logical_not(self.stays & (p.mp == model)))
            def _(model=model):
                self.copy(model).start()

        @pl.when(self.stays)
        def _():
            self.own_copy().start()

    def finish(self):
        p = self.place
        for model in range(4):

            @pl.when(jnp.logical_not(self.stays & (p.mp == model)))
            def _(model=model):
                self.copy(model).wait_send()

        for ctx in range(4):

            @pl.when(jnp.logical_not(self.stays & (p.ctx == ctx)))
            def _(ctx=ctx):
                count = self.rows.shape[0]
                spot = self.whole.at[ctx // 2, 0, pl.ds((ctx % 2) * count, count), :]
                pltpu.make_async_remote_copy(
                    src_ref=spot,
                    dst_ref=spot,
                    send_sem=self.send.at[0],
                    recv_sem=self.receive.at[ctx],
                    device_id=(p.dp, ctx, p.low * 2 + p.high),
                    device_id_type=MESH,
                ).wait_recv()

        @pl.when(self.stays)
        def _():
            self.own_copy().wait()


ORDER = (
    64, 33, 0, 8, 65, 9, 2, 1, 3, 44, 10, 69, 5, 45, 66, 4, 11, 13, 53, 21,
    46, 75, 12, 67, 25, 47, 6, 40, 72, 70, 68, 77, 32, 7, 76, 71, 73, 42, 14, 49,
    20, 15, 28, 17, 29, 79, 61, 74, 86, 41, 43, 84, 85, 83, 103, 16, 37, 36, 78, 87,
    88, 89, 57, 90, 80, 22, 30, 34, 81, 31, 18, 38, 23, 104, 24, 82, 19, 35, 39, 106,
    60, 105, 111, 26, 48, 27, 62, 107, 50, 56, 108, 110, 109, 63, 112, 52, 51, 113, 114, 58,
    115, 175, 120, 59, 119, 54, 55, 124, 116, 121, 125, 118, 122, 117, 91, 92, 93, 127, 131, 126,
    94, 132, 135, 136, 142, 143, 134, 128, 176, 146, 147, 95, 133, 138, 96, 97, 180, 145, 123, 137,
    177, 98, 140, 179, 139, 178, 183, 185, 154, 155, 189, 149, 148, 188, 144, 130, 184, 156, 141, 129,
    181, 187, 186, 190, 99, 182, 164, 151, 100, 165, 153, 150, 170, 166, 169, 157, 168, 101, 159, 102,
    173, 172, 158, 160, 171, 191, 167, 163, 161, 152, 162, 174, 192,
)


def run_steps(steps, order):
    for place in order:
        steps[place]()


def layer_kernel(
    tokens_in, out_grad, seg_row_in, w_query, w_key, w_value, w_out, w_gate, w_up, w_down,
    freqs,
    tokens_out, down_own, down_near, gate_own, gate_near, up_own, up_near, out_own, out_near, three_own, three_near,
    qkv_all, out_all, gate_all, up_all, down_all, grads_all, second_all, normed_all, back_all,
    query_all, key_all, value_all, mixed_all,
    gate_far, gate_mid, up_far, up_mid, down_far, down_mid, three_far, three_mid, out_far, out_mid,
    grad_in,
    second, grads, gate_here, up_here, down_here, hidden, gate_back, up_back, out_here, key_sum, value_sum,
    wide_far, wide_mid, wide_near, wide_loads, wide_stage, tall_far, tall_mid, tall_near, tall_loads, tall_stage,
    core_send, core_recv, chip_send, chip_recv, along_send, along_recv, total_ref, rows_low, back_rows, landed,
    residual, inverse_two, log_total, cosine, sine_part, seg_col, seg_row, kept,
    credit, send, receive, local, feed_send, feed_receive, feed_local, row_send, row_receive, row_local,
):
    p = Place()
    mover = Mover(send, receive, local)
    feed_return = RowReturn(p, feed_send, feed_receive, feed_local)
    row_return = RowReturn(p, row_send, row_receive, row_local)
    row_return.greet(
        [p.along(1), p.along(2), p.along(3), p.across(), p.beside_chip(), p.beside_core()]
    )
    length = grads.shape[0]
    units = hidden.shape[1]
    span, feats = tokens_in.shape[2:]
    cols = out_here.shape[0]
    head_count = cols // HD
    blocks = length // TILE
    score_scale = 1.0 / math.sqrt(HD)
    tokens = grads
    first, later = pl.ds(0, length), pl.ds(length, length)
    query, key, value, mixed = [up_here.at[first, pl.ds(slot * cols, cols)] for slot in range(4)]
    three_back = up_here.at[later, pl.ds(0, 3 * cols)]
    mixed_back = up_here.at[later, pl.ds(3 * cols, cols)]
    qkv_here = gate_here.at[:, pl.ds(0, 3 * cols)]
    attended = ((query, query_all), (key, key_all), (value, value_all), (mixed, mixed_all))
    my_rows = p.shard_rows(p.low, p.chip, p.core)
    steps = []
    step = steps.append
    made = types.SimpleNamespace()

    def block_of(whole, ctx, model):
        return whole.at[aligned(ctx * span, span), aligned(model * feats, feats)]

    def own_view(whole):
        return lambda low, chip, core: block_of(whole, p.high * 2 + low, chip * 2 + core)

    def other_view(whole):
        return lambda low, chip, core: block_of(whole, (1 - p.high) * 2 + low, chip * 2 + core)

    def row_view(whole):
        return lambda low, chip, core: whole.at[p.shard_rows(low, chip, core)]

    def relays(gather):
        step(lambda: gather().relay_along())
        step(lambda: gather().relay_chip())
        step(lambda: gather().relay_corner())

    def fetch(shard, whole, axis, landing=0, pieces=1):
        size = shard.shape[axis] // 2 // pieces
        for piece in range(pieces):
            chunk = WeightFetch(
                p, mover, shard, whole, axis, piece * size, size, landing + piece * size
            )
            chunks.append(chunk)
            for action in (chunk.start, chunk.start_own, chunk.forward, chunk.cross):
                step(action)

    chunks = []
    fetch(w_query, qkv_all, 1, 0)
    fetch(w_key, qkv_all, 1, cols)
    fetch(w_value, qkv_all, 1, 2 * cols)
    fetch(w_out, out_all, 0)
    fetch(w_gate, gate_all, 1, 0, PIECES)
    fetch(w_up, up_all, 1, 0, PIECES)
    fetch(w_down, down_all, 0, 0, PIECES)
    of_gate, of_up, of_down = [chunks[4 + slot * PIECES :][:PIECES] for slot in range(3)]

    @step
    def _():
        made.seg = []
        spot = aligned(p.ctx * span, span)
        for mask in (1, 2, 3):
            goal = p.high if mask == 1 else 1 - p.high
            made.seg.append(
                mover.to(seg_row_in.at[goal], seg_row.at[:, spot], p.along(mask))
            )
        made.seg.append(mover.here(seg_row_in.at[p.high], seg_row.at[:, spot]))
        here = block_of(tokens, p.ctx, p.mp)
        made.swap = mover.to(tokens_in.at[1 - p.high, 0], here, p.along(2))
        own_tokens = tokens_in.at[p.high, 0]
        made.tokens = mover.here(own_tokens, here)
        made.own = GroupGather(p, mover, own_view(tokens), own_tokens)

    @step
    def _():
        made.swap.wait_recv()
        theirs = block_of(tokens, p.along(2)[1], p.mp)
        made.other = GroupGather(p, mover, other_view(tokens), theirs)

    relays(lambda: made.own)
    relays(lambda: made.other)

    @step
    def _():
        for copy in made.seg:
            copy.wait()
        for begin in range(0, length, TILE):
            rows = pl.ds(begin, TILE)
            numbers = jnp.broadcast_to(seg_row[0:1, rows], (HD, TILE))
            seg_col[rows, :] = numbers.T
            allowed = allowed_mask(seg_col, seg_row, begin, begin + TILE)
            position = jnp.sum(jnp.where(allowed, 1.0, 0.0), axis=1, keepdims=True) - 1.0
            angle = position * freqs[0:1, :]
            cosine[rows, :] = jnp.cos(angle)
            lane = lax.broadcasted_iota(jnp.int32, (TILE, HD), 1)
            sine = jnp.sin(angle)
            sine_part[rows, :] = jnp.where(lane < HD // 2, -sine, sine)

    @step
    def _():
        made.tokens.wait()
        made.swap.wait_send()
        made.own.finish()
        made.other.finish()
        kept[...] = tokens[my_rows, :]
        residual[...] = kept[...].astype(FULL)
        for begin in range(0, length, 128):
            rows = pl.ds(begin, 128)
            tokens[rows, :] = normalise(tokens[rows, :].astype(FULL))[0].astype(LOW)
        made.normed = mover.here(tokens, normed_all)

    def load_blocks(shards, whole, here, axis, begin=0, size=None):
        copies = []
        size = whole.shape[0] if size is None else size

        def cut(ref, block):
            span = aligned(block * TILE, TILE)
            return ref.at[span, :] if axis == 1 else ref.at[pl.ds(begin, size), span]

        for turn_by in range(1, 8):
            block = lax.rem(p.home + turn_by, 8)
            copies.append(mover.here(cut(whole, block), cut(here, block)))
        landing = 0
        for shard in shards:
            half = shard.shape[axis] // 2
            spot = aligned(p.home * TILE, TILE)
            if axis == 1:
                source = shard.at[:, aligned(p.low * half, half)]
                target = here.at[spot, pl.ds(landing, half)]
            else:
                source = shard.at[aligned(p.low * half + begin, size), :]
                target = here.at[pl.ds(begin, size), spot]
            copies.append(mover.here(source, target))
            landing += half
        return copies

    def wait_all(copies):
        for copy in copies:
            copy.wait()

    @step
    def _():
        for chunk in chunks[:3]:
            chunk.finish()
        wait_all(load_blocks((w_query, w_key, w_value), qkv_all, qkv_here, 1))
        for begin in range(0, length, TILE):
            rows = pl.ds(begin, TILE)
            three = contract(tokens[rows, :], qkv_here[...], 1, 0)
            turned = [
                turn(three[:, start : start + cols], cosine[rows, :], sine_part[rows, :])
                for start in (0, cols)
            ]
            query[rows, :] = turned[0].astype(LOW)
            key[rows, :] = turned[1].astype(LOW)
            value[rows, :] = three[:, 2 * cols :].astype(LOW)

    @step
    def _():
        spot = block_of(grads_all, p.ctx, p.mp)
        own = out_grad.at[p.high, 0]
        made.cot_swap = mover.to(out_grad.at[1 - p.high, 0], spot, p.along(2))
        made.cot_own = GroupGather(p, mover, own_view(grads_all), own)

    @step
    def _():
        made.cot_swap.wait_recv()
        theirs = block_of(grads_all, p.along(2)[1], p.mp)
        made.cot_other = GroupGather(p, mover, other_view(grads_all), theirs)

    relays(lambda: made.cot_own)
    relays(lambda: made.cot_other)

    def attend(begin):
        rows = pl.ds(begin, TILE)
        keys = begin + TILE
        allowed = allowed_mask(seg_col, seg_row, begin, keys)
        for head in range(head_count):
            head_cols = pl.ds(head * HD, HD)
            scores = contract(query[rows, head_cols], key[pl.ds(0, keys), head_cols], 1, 1)
            scores = jnp.where(allowed, scores * score_scale, NEG_FILL)
            highest = jnp.max(scores, axis=-1, keepdims=True)
            exp_terms = jnp.exp(scores - highest)
            total_exp = jnp.sum(exp_terms, axis=-1, keepdims=True)
            probs_low = (exp_terms * (1.0 / total_exp)).astype(LOW)
            mixed[rows, head_cols] = contract(
                probs_low, value[pl.ds(0, keys), head_cols], 1, 0
            ).astype(LOW)
            log_total[rows, head_cols] = jnp.broadcast_to(
                highest + jnp.log(total_exp), (TILE, HD)
            )

    for block in range(blocks):
        step(functools.partial(attend, block * TILE))

    buffers = (core_send, core_recv, chip_send, chip_recv, along_send, along_recv, total_ref)

    def scatter_steps(terms, waits=True):
        scatter = GroupScatter(p, mover, buffers, terms)

        def stage(action, slot, part=None):
            def run():
                if waits and part != 1:
                    pl.semaphore_wait(credit.at[slot], 1)
                action() if part is None else action(part)

            return run

        step(stage(scatter.start_core, 0, 0))
        step(stage(scatter.start_core, 0, 1))
        step(stage(scatter.start_chip, 1))
        step(stage(scatter.start_along, 2))
        return scatter

    branch_sum = scatter_steps( lambda rows: contract(mixed[rows, :], out_here[...], 1, 0), False
    )
    back_sum = scatter_steps(
        lambda rows: contract(gate_back[rows, :], gate_here[...], 1, 1)
        + contract(up_back[rows, :], up_here[...], 1, 1),
    )
    feed_sum = scatter_steps( lambda rows: contract(hidden[rows, :], down_here[...], 1, 0)
    )
    input_sum = scatter_steps( lambda rows: contract(three_back[rows, :], qkv_here[...], 1, 1)
    )

    @step
    def _():
        chunks[3].finish()
        load = load_blocks((w_out,), out_all, out_here, 0)
        made.saves = [mover.here(source, target) for source, target in attended]
        wait_all(load)

    @step
    def _():
        branch = branch_sum.result()
        give_credit(p, credit)
        hidden_rows = residual[...] + branch
        residual[...] = hidden_rows
        normed_two, inverse = normalise(hidden_rows)
        inverse_two[...] = jnp.broadcast_to(inverse, inverse_two.shape)
        rows_low[...] = normed_two.astype(LOW)
        view = row_view(second_all)
        made.second_local = mover.here(rows_low, view(p.low, p.chip, p.core))
        made.second = GroupGather(p, mover, view, rows_low)

    relays(lambda: made.second)

    @step
    def _():
        for chunk in of_gate:
            chunk.finish()
        made.gate_load = load_blocks((w_gate,), gate_all, gate_here, 1)

    @step
    def _():
        for copy in made.saves:
            copy.wait()
        for chunk in of_up:
            chunk.finish()
        made.up_load = load_blocks((w_up,), up_all, up_here, 1)

    @step
    def _():
        made.second.finish()
        made.second_local.wait()
        made.second_load = mover.here(second_all, second)

    @step
    def _():
        made.cot_own.finish()
        made.cot_other.finish()
        made.cot_swap.wait_send()
        made.normed.wait()
        made.cot_load = [mover.here(out_grad.at[p.high, 0], block_of(grads, p.ctx, p.mp))]
        for turn_by in range(1, 16):
            which = lax.rem(p.ctx * 4 + p.mp + turn_by, 16)
            made.cot_load.append(
                mover.here(
                    block_of(grads_all, which // 4, lax.rem(which, 4)),
                    block_of(grads, which // 4, lax.rem(which, 4)),
                )
            )

    def hidden_block(block):
        if block == 0:
            made.second_load.wait()
            wait_all(made.gate_load + made.up_load)
        rows = pl.ds(block * TILE, TILE)
        for begin in range(0, units, TILE):
            part = pl.ds(begin, TILE)
            gate = contract(second[rows, :], gate_here[:, part], 1, 0)
            up = contract(second[rows, :], up_here[:, part], 1, 0)
            share = jax.nn.sigmoid(gate)
            silu = gate * share
            hidden[rows, part] = (silu * up).astype(LOW)
            gate_back[rows, part] = (up * share * (1.0 + gate * (1.0 - share))).astype(LOW)
            up_back[rows, part] = silu.astype(LOW)

    for block in range(blocks):
        step(functools.partial(hidden_block, block))

    def back_block(begin, index, carry):
        rows, part = aligned(index * TILE, TILE), pl.ds(begin, TILE)
        back = contract(grads[rows, :], down_here[part, :], 1, 1)
        gate_back[rows, part] = (back * gate_back[rows, part].astype(FULL)).astype(LOW)
        up_back[rows, part] = (back * up_back[rows, part].astype(FULL)).astype(LOW)
        return carry

    def back_piece(which):
        piece = units // PIECES
        of_down[which].finish()
        wait_all(load_blocks((w_down,), down_all, down_here, 0, which * piece, piece))
        for begin in range(which * piece, (which + 1) * piece, TILE):
            lax.fori_loop(0, blocks, functools.partial(back_block, begin), 0)

    for which in range(PIECES):
        step(functools.partial(back_piece, which))

    def narrow(ref):
        part = pl.ds(0, 3 * cols)
        return ref.at[:, part] if len(ref.shape) == 2 else ref.at[:, :, part]

    def short(ref):
        part = pl.ds(0, cols)
        return ref.at[part, :] if len(ref.shape) == 2 else ref.at[:, part, :]

    def left_terms(left, right):
        def terms(block, part):
            span = aligned(block * TILE + part.start, part.size, 128)
            return contract(left[:, span], right[...], 0, 0)

        return terms

    def right_terms(left, right):
        return lambda block, part: contract(left[:, part], block_cols(right, block), 0, 0)

    wide_staging, tall_staging = Staging(), Staging()
    wide_sends, tall_sends = (wide_far, wide_mid, wide_near), (tall_far, tall_mid, tall_near)
    return_down = GradReturn(
        p, mover, 0, right_terms(hidden, grads), tall_sends, (down_far, down_mid, down_near), tall_loads,
        (tall_staging, tall_stage), down_own,
    )
    return_gate = GradReturn(
        p, mover, 1, left_terms(second, gate_back), wide_sends, (gate_far, gate_mid, gate_near), wide_loads,
        (wide_staging, wide_stage), gate_own,
    )
    return_up = GradReturn(
        p, mover, 1, left_terms(second, up_back), wide_sends, (up_far, up_mid, up_near), wide_loads,
        (wide_staging, wide_stage), up_own, return_gate,
    )
    return_out = GradReturn(
        p, mover, 0, right_terms(mixed, down_here), [short(ref) for ref in tall_sends],
        (out_far, out_mid, out_near), short(tall_loads), (tall_staging, short(tall_stage)), out_own, return_down,
    )
    return_three = GradReturn(
        p, mover, 1, left_terms(grads, three_back), [narrow(ref) for ref in wide_sends],
        (three_far, three_mid, three_near), narrow(wide_loads), (wide_staging, narrow(wide_stage)), three_own,
        return_up,
    )
    returns = [return_down, return_gate, return_up, return_out, return_three]
    for part in returns:
        for which in range(4):
            step(functools.partial(part.across, which))
        for which in range(2):
            for half in range(2):
                step(functools.partial(part.along, which, half))
        for half in range(2):
            step(functools.partial(part.beside, half))
        step(part.own)

    @step
    def _():
        wait_all(made.cot_load)

    @step
    def _():
        normed_grad = back_sum.result()
        give_credit(p, credit)
        inverse = inverse_two[:, :1]
        centred = residual[...] - jnp.mean(residual[...], axis=-1, keepdims=True)
        back_value = grads[my_rows, :].astype(FULL) + norm_backward(
            normed_grad, centred * inverse, inverse
        )
        back_rows[...] = back_value
        rows_low[...] = back_value.astype(LOW)
        view = row_view(back_all)
        made.back_local = mover.here(rows_low, view(p.low, p.chip, p.core))
        made.back = GroupGather(p, mover, view, rows_low)

    relays(lambda: made.back)

    @step
    def _():
        made.refill = [mover.here(source, target) for target, source in attended]
        made.refill += load_blocks((w_query, w_key, w_value), qkv_all, qkv_here, 1)

    @step
    def _():
        made.norm_load = mover.here(normed_all, grads)

    @step
    def _():
        made.norm_load.wait()

    @step
    def _():
        made.back.finish()
        made.back_local.wait()
        made.back_load = mover.here(back_all, down_here)

    @step
    def _():
        rows_low[...] = (residual[...] + feed_sum.result()).astype(LOW)
        give_credit(p, credit)
        feed_return.start(rows_low, tokens_out)

    @step
    def _():
        made.back_load.wait()
        wait_all(made.refill)
        for begin in range(0, length, TILE):
            rows = pl.ds(begin, TILE)
            mixed_back[rows, :] = contract(down_here[rows, :], out_here[...], 1, 1).astype(LOW)

    def attend_back(begin):
        rows = pl.ds(begin, TILE)
        keys = begin + TILE
        key_rows = pl.ds(0, keys)
        allowed = allowed_mask(seg_col, seg_row, begin, keys)
        query_parts = []
        for head in range(head_count):
            head_cols = pl.ds(head * HD, HD)
            query_head, key_head = query[rows, head_cols], key[key_rows, head_cols]
            mixed_head = mixed_back[rows, head_cols]
            scores = contract(query_head, key_head, 1, 1) * score_scale
            scores = jnp.where(allowed, scores, NEG_FILL)
            probs = jnp.exp(scores - log_total[rows, pl.ds(head * HD, 1)])
            value_terms = contract(probs.astype(LOW), mixed_head, 0, 0)
            probs_back = contract(mixed_head, value[key_rows, head_cols], 1, 1)
            row_dot = jnp.sum(probs * probs_back, axis=-1, keepdims=True)
            scores_back = (probs * (probs_back - row_dot)).astype(LOW)
            query_parts.append(contract(scores_back, key_head, 1, 0) * score_scale)
            key_terms = contract(scores_back, query_head, 0, 0)
            if keys == length:
                key_sum[key_rows, head_cols] = key_terms
                value_sum[key_rows, head_cols] = value_terms
            else:
                key_sum[key_rows, head_cols] += key_terms
                value_sum[key_rows, head_cols] += value_terms
        three_back[rows, pl.ds(0, cols)] = turn(
            jnp.concatenate(query_parts, axis=1), cosine[rows, :], -sine_part[rows, :]
        ).astype(LOW)

    for block in range(blocks):
        step(functools.partial(attend_back, block * TILE))

    @step
    def _():
        for begin in range(0, length, TILE):
            rows = pl.ds(begin, TILE)
            three_back[rows, pl.ds(cols, cols)] = turn(
                key_sum[rows, :] * score_scale, cosine[rows, :], -sine_part[rows, :]
            ).astype(LOW)
            three_back[rows, pl.ds(2 * cols, cols)] = value_sum[rows, :].astype(LOW)

    @step
    def _():
        kept_normed, inverse = normalise(kept[...].astype(FULL))
        summed = input_sum.result()
        feed_return.finish()
        rows_low[...] = (back_rows[...] + norm_backward(summed, kept_normed, inverse)).astype(LOW)
        row_return.start(rows_low, landed)

    @step
    def _():
        row_return.finish()
        grad_in[...] = landed[...].astype(FULL)
        for part in returns + chunks:
            part.drain()
        wide_staging.free()
        tall_staging.free()

    run_steps(steps, ORDER)


def whole_layer(tokens_in, out_grad, seg_row, weights, freqs):
    span, feats = tokens_in.shape[2:]
    length, width = 4 * span, 4 * feats
    cols, units = weights[0].shape[1] // 2, weights[4].shape[1] // 2

    def low(*shape):
        return jax.ShapeDtypeStruct(shape, LOW)

    def full(*shape):
        return jax.ShapeDtypeStruct(shape, FULL)

    wide, tall = (TILE, units), (units, TILE)
    in_hbm = [low(2, 1, span, feats)]
    for block in (tall, wide, wide, (cols, TILE), (TILE, 3 * cols)):
        in_hbm += [full(*block), low(*block)]
    in_hbm += [low(width, 3 * cols), low(cols, width), low(width, units), low(width, units), low(units, width)]
    in_hbm += [low(length, width)] * 4 + [low(length, cols)] * 4
    for block in (wide, wide, tall, (TILE, 3 * cols), (cols, TILE)):
        in_hbm += [low(4, *block), low(2, *block)]
    vmem = pl.BlockSpec(memory_space=pltpu.VMEM)

    def sending(block):
        return [
            pltpu.VMEM((4, *block), LOW),
            pltpu.VMEM((2, *block), LOW),
            pltpu.VMEM(block, LOW),
            pltpu.VMEM((2, *block), LOW),
            pltpu.VMEM(block, FULL),
        ]

    row_semaphores = [
        pltpu.SemaphoreType.DMA((4,)),
        pltpu.SemaphoreType.DMA((4,)),
        pltpu.SemaphoreType.DMA,
    ]
    outs = pl.pallas_call(
        layer_kernel,
        out_shape=in_hbm + [full(2, 1, span, feats)],
        in_specs=[HBM] * 10 + [vmem],
        out_specs=[HBM] * len(in_hbm) + [vmem],
        scratch_shapes=[
            pltpu.VMEM((length, width), LOW),
            pltpu.VMEM((length, width), LOW),
            pltpu.VMEM((width, units), LOW),
            pltpu.VMEM((width, units), LOW),
            pltpu.VMEM((units, width), LOW),
            pltpu.VMEM((length, units), LOW),
            pltpu.VMEM((length, units), LOW),
            pltpu.VMEM((length, units), LOW),
            pltpu.VMEM((cols, width), LOW),
            pltpu.VMEM((length, cols), FULL),
            pltpu.VMEM((length, cols), FULL),
            *sending(wide),
            *sending(tall),
            *scatter_buffers(width),
            pltpu.VMEM((length // 8, width), LOW),
            pltpu.VMEM((length // 8, width), FULL),
            pltpu.VMEM((2, 1, span, feats), LOW),
            pltpu.VMEM((length // 8, width), FULL),
            pltpu.VMEM((length // 8, HD), FULL),
            pltpu.VMEM((length, cols), FULL),
            *[pltpu.VMEM((length, HD), FULL)] * 3,
            pltpu.VMEM((8, length), FULL),
            pltpu.VMEM((length // 8, width), LOW),
            pltpu.SemaphoreType.REGULAR((3,)),
            pltpu.SemaphoreType.DMA((288,)),
            pltpu.SemaphoreType.DMA((288,)),
            pltpu.SemaphoreType.DMA((256,)),
            *row_semaphores,
            *row_semaphores,
        ],
        compiler_params=pltpu.CompilerParams(
            collective_id=1, has_side_effects=True, vmem_limit_bytes=VMEM_BYTES
        ),
    )(tokens_in, out_grad, seg_row, *weights, freqs)
    return outs[:11] + outs[-1:]


def hand_over_kernel(*refs):
    tokens_in, grad_in, *halves = refs[:12]
    tokens_out, grad_out, down, gate, up, out, query, key, value = refs[12:21]
    held, own_held, far_held, wide_held = refs[21:23], refs[23:28], refs[28:33], refs[33:38]
    load, save = refs[38:]
    low = lax.axis_index("ctx") % 2
    started, saves = [], []

    def copy(source, target, semaphores, which):
        made = pltpu.make_async_copy(source, target, semaphores.at[len(which)])
        made.start()
        which.append(made)
        return made

    owns = [copy(halves[2 * slot], own_held[slot], load, started) for slot in range(5)]
    fars = [copy(halves[2 * slot + 1], far_held[slot], load, started) for slot in range(5)]
    rows = [copy(ref, here, load, started) for ref, here in zip((tokens_in, grad_in), held)]

    def place(source, targets, axis, which):
        begin = 0
        for target in targets:
            size = target.shape[axis] // 2
            spot, part = aligned(which * size, size), pl.ds(begin, size)
            begin += size
            if axis == 1:
                copy(source.at[:, part], target.at[:, spot], save, saves)
            else:
                copy(source.at[part, :], target.at[spot, :], save, saves)

    goals = (((down,), 0), ((gate,), 1), ((up,), 1), ((out,), 0), ((query, key, value), 1))
    for slot, (targets, axis) in enumerate(goals):
        owns[slot].wait()
        place(own_held[slot], targets, axis, low)
    for slot, (targets, axis) in enumerate(goals):
        fars[slot].wait()
        wide_held[slot][...] = far_held[slot][...].astype(FULL)
        place(wide_held[slot], targets, axis, 1 - low)
    for made, here, target in zip(rows, held, (tokens_out, grad_out)):
        made.wait()
        copy(here, target, save, saves)
    for made in saves:
        made.wait()


def hand_over(arrays, shapes):
    tokens_out, *halves, grad_in = arrays
    held = [tokens_out, grad_in, *halves[::2], *halves[1::2]]
    return pl.pallas_call(
        hand_over_kernel,
        out_shape=[jax.ShapeDtypeStruct(shape, kind) for shape, kind in shapes],
        in_specs=[HBM] * 12,
        out_specs=[HBM] * len(shapes),
        scratch_shapes=[
            *[pltpu.VMEM(array.shape, array.dtype) for array in held],
            *[pltpu.VMEM(array.shape, FULL) for array in halves[1::2]],
            pltpu.SemaphoreType.DMA((16,)),
            pltpu.SemaphoreType.DMA((24,)),
        ],
        compiler_params=pltpu.CompilerParams(vmem_limit_bytes=VMEM_BYTES),
    )(tokens_out, grad_in, *halves)


def per_device_grouped(
    tokens_in, out_grad, segment_ids, w_query, w_key, w_value, w_out, w_gate, w_up, w_down
):
    span = segment_ids.shape[2]
    segment_float = segment_ids[:, 0].astype(jnp.float32)
    segment_rows = jnp.broadcast_to(segment_float[:, None, :], (2, 8, span))
    freq_half = jnp.power(10000.0, -2.0 * jnp.arange(HD // 2, dtype=jnp.float32) / HD)
    freqs = jnp.broadcast_to(jnp.concatenate([freq_half, freq_half])[None], (8, HD))
    results = whole_layer(
        tokens_in, out_grad, segment_rows, (w_query, w_key, w_value, w_out, w_gate, w_up, w_down), freqs
    )
    full = jnp.float32
    (
        tokens_out, grad_in, grad_down, grad_gate, grad_up, grad_out, grad_query, grad_key, grad_value,
    ) = hand_over(
        results,
        [
            (tokens_in.shape, jnp.bfloat16),
            (tokens_in.shape, full),
            *[
                (weight.shape, full)
                for weight in (w_down, w_gate, w_up, w_out, w_query, w_key, w_value)
            ],
        ],
    )
    return (
        tokens_out,
        grad_in,
        grad_query,
        grad_key,
        grad_value,
        grad_out,
        grad_gate,
        grad_up,
        grad_down,
    )


def solution(mesh):
    in_specs = (
        P(None, "dp", "ctx", "mp"),
        P(None, "dp", "ctx", "mp"),
        P(None, "dp", "ctx"),
        P(("dp", "ctx"), "mp"),
        P(("dp", "ctx"), "mp"),
        P(("dp", "ctx"), "mp"),
        P("mp", ("dp", "ctx")),
        P(("dp", "ctx"), "mp"),
        P(("dp", "ctx"), "mp"),
        P("mp", ("dp", "ctx")),
    )
    out_specs = (
        P(None, "dp", "ctx", "mp"),
        P(None, "dp", "ctx", "mp"),
        P(("dp", "ctx"), "mp"),
        P(("dp", "ctx"), "mp"),
        P(("dp", "ctx"), "mp"),
        P("mp", ("dp", "ctx")),
        P(("dp", "ctx"), "mp"),
        P(("dp", "ctx"), "mp"),
        P("mp", ("dp", "ctx")),
    )
    grouped = mesh.shape["ctx"] == 4 and mesh.shape["mp"] == 4 and mesh.shape["dp"] == 2
    per_device = per_device_grouped if grouped else per_device_general
    return jax.shard_map(
        per_device, mesh=mesh, in_specs=in_specs, out_specs=out_specs, check_vma=False
    )
```

```python
import functools
import math
import types

import jax
import jax.numpy as jnp
import numpy as np
from jax import lax
from jax.experimental import pallas as pl
from jax.experimental.pallas import tpu as pltpu
from jax.sharding import PartitionSpec as P

HD = 128


EPSILON = 1e-05
NEG_FILL = -1e30


def layer_norm(values):
    centred = values - jnp.mean(values, axis=-1, keepdims=True)
    inverse = lax.rsqrt(jnp.mean(centred * centred, axis=-1, keepdims=True) + EPSILON)
    return (centred * inverse, inverse)


def norm_backward(upstream, normed, inverse):
    plain_mean = jnp.mean(upstream, axis=-1, keepdims=True)
    cross_mean = jnp.mean(upstream * normed, axis=-1, keepdims=True)
    return inverse * (upstream - plain_mean - normed * cross_mean)


def doc_positions(segment):
    length = segment.shape[-1]
    places = jnp.arange(length, dtype=jnp.int32)
    opening = jnp.ones(segment.shape[:-1] + (1,), dtype=bool)
    change = jnp.concatenate([opening, segment[..., 1:] != segment[..., :-1]], axis=-1)
    starts = lax.cummax(jnp.where(change, places, jnp.int32(0)), axis=segment.ndim - 1)
    return places - starts


def rope_angles(positions):
    freq_table = jnp.power(10000.0, -2.0 * jnp.arange(HD // 2, dtype=jnp.float32) / HD)
    turned = positions.astype(jnp.float32)[..., None] * freq_table
    return (jnp.cos(turned), jnp.sin(turned))


def rope_turn(values, cosine, sine_part):
    half_size = values.shape[-1] // 2
    leading = values[..., :half_size]
    trailing = values[..., half_size:]
    return jnp.concatenate(
        [leading * cosine - trailing * sine_part, trailing * cosine + leading * sine_part], axis=-1
    )


def dot_rows(left_mat, right_mat):
    return lax.dot_general(
        left_mat, right_mat, (((1,), (1,)), ((), ())), preferred_element_type=jnp.float32
    )


def dot_cols(left_mat, right_mat):
    return lax.dot_general(
        left_mat, right_mat, (((0,), (0,)), ((), ())), preferred_element_type=jnp.float32
    )


def fetch_weights(w_query, w_key, w_value, w_gate, w_up, w_out, w_down):
    return (
        lax.all_gather(w_query, ("dp", "ctx"), axis=0, tiled=True),
        lax.all_gather(w_key, ("dp", "ctx"), axis=0, tiled=True),
        lax.all_gather(w_value, ("dp", "ctx"), axis=0, tiled=True),
        lax.all_gather(w_gate, ("dp", "ctx"), axis=0, tiled=True),
        lax.all_gather(w_up, ("dp", "ctx"), axis=0, tiled=True),
        lax.all_gather(w_out, ("dp", "ctx"), axis=1, tiled=True),
        lax.all_gather(w_down, ("dp", "ctx"), axis=1, tiled=True),
    )


def per_device_general(
    tokens_in, out_grad, segment_ids, w_query, w_key, w_value, w_out, w_gate, w_up, w_down
):
    micro_count = tokens_in.shape[0]
    seq_local = tokens_in.shape[1]
    span_len = tokens_in.shape[2]
    local_width = tokens_in.shape[3]
    ctx_index = lax.axis_index("ctx")
    model_index = lax.axis_index("mp")
    tokens_all, grads_all = (
        lax.all_gather(tokens_in, "mp", axis=3, tiled=True),
        lax.all_gather(out_grad, "mp", axis=3, tiled=True),
    )
    segments_all = lax.all_gather(segment_ids, "ctx", axis=2, tiled=True)
    feature_width = tokens_all.shape[3]
    seq_length = segments_all.shape[2]
    row_count = seq_local * span_len
    score_scale = 1.0 / math.sqrt(HD)
    positions = doc_positions(segments_all)
    query_places = ctx_index * span_len + jnp.arange(span_len, dtype=jnp.int32)
    key_places = jnp.arange(seq_length, dtype=jnp.int32)
    causal = key_places[None, :] <= query_places[:, None]
    outputs = []
    input_grads = []
    totals = None
    for micro_step in range(micro_count):
        full_weights = fetch_weights(w_query, w_key, w_value, w_gate, w_up, w_out, w_down)
        query_full, key_full, value_full, gate_full, up_full, out_full, down_full = full_weights
        head_count = query_full.shape[1] // HD
        segment_seq = segments_all[micro_step]
        segment_own = lax.dynamic_slice_in_dim(segment_seq, ctx_index * span_len, span_len, 1)
        position_own = lax.dynamic_slice_in_dim(
            positions[micro_step], ctx_index * span_len, span_len, 1
        )
        allowed = (segment_own[:, :, None] == segment_seq[:, None, :]) & causal[None]
        cosine, sine_part = rope_angles(position_own)
        cosine = cosine[:, :, None, :]
        sine_part = sine_part[:, :, None, :]
        inputs = tokens_all[micro_step].astype(jnp.float32)
        normed, inverse_one = layer_norm(inputs)
        normed_low = normed.astype(jnp.bfloat16).reshape(row_count, feature_width)

        def project(matrix):
            product = jnp.dot(normed_low, matrix, preferred_element_type=jnp.float32)
            return product.reshape(seq_local, span_len, head_count, HD)

        query_low = (
            rope_turn(project(query_full), cosine, sine_part)
            .astype(jnp.bfloat16)
            .reshape(seq_local, span_len, head_count * HD)
        )
        key_low = (
            rope_turn(project(key_full), cosine, sine_part)
            .astype(jnp.bfloat16)
            .reshape(seq_local, span_len, head_count * HD)
        )
        value_low = (
            project(value_full).astype(jnp.bfloat16).reshape(seq_local, span_len, head_count * HD)
        )
        key_seq, value_seq = (
            lax.all_gather(key_low, "ctx", axis=1, tiled=True),
            lax.all_gather(value_low, "ctx", axis=1, tiled=True),
        )
        mixed_parts = []
        log_totals = []
        for head_index in range(head_count):
            head_cols = slice(head_index * HD, (head_index + 1) * HD)
            scores = (
                jnp.einsum(
                    "sqd,skd->sqk",
                    query_low[..., head_cols],
                    key_seq[..., head_cols],
                    preferred_element_type=jnp.float32,
                )
                * score_scale
            )
            scores = jnp.where(allowed, scores, NEG_FILL)
            highest = jnp.max(scores, axis=-1, keepdims=True)
            exp_terms = jnp.exp(scores - highest)
            total_exp = jnp.sum(exp_terms, axis=-1, keepdims=True)
            probs_low = (exp_terms / total_exp).astype(jnp.bfloat16)
            mixed_parts.append(
                jnp.einsum(
                    "sqk,skd->sqd",
                    probs_low,
                    value_seq[..., head_cols],
                    preferred_element_type=jnp.float32,
                )
            )
            log_totals.append(highest + jnp.log(total_exp))
        mixed_low = (
            jnp.concatenate(mixed_parts, axis=-1)
            .astype(jnp.bfloat16)
            .reshape(row_count, head_count * HD)
        )
        branch = jnp.dot(mixed_low, out_full, preferred_element_type=jnp.float32)
        branch = lax.psum(branch, "mp")
        residual = inputs + branch.reshape(seq_local, span_len, feature_width)
        normed_two, inverse_two = layer_norm(residual)
        second_low = normed_two.astype(jnp.bfloat16).reshape(row_count, feature_width)
        gate_lin = jnp.dot(second_low, gate_full, preferred_element_type=jnp.float32)
        up_lin = jnp.dot(second_low, up_full, preferred_element_type=jnp.float32)
        sigmoid_gate = jax.nn.sigmoid(gate_lin)
        hidden_low = (gate_lin * sigmoid_gate * up_lin).astype(jnp.bfloat16)
        feed_terms = jnp.dot(hidden_low, down_full, preferred_element_type=jnp.float32).reshape(
            seq_local, span_len, feature_width
        )
        feed_own = lax.psum_scatter(
            feed_terms.astype(jnp.bfloat16), "mp", scatter_dimension=2, tiled=True
        ).astype(jnp.float32)
        residual_own = lax.dynamic_slice_in_dim(residual, model_index * local_width, local_width, 2)
        outputs.append((residual_own + feed_own).astype(jnp.bfloat16))
        back_weights = (
            lax.all_gather(w_query, ("dp", "ctx"), axis=0, tiled=True),
            lax.all_gather(w_key, ("dp", "ctx"), axis=0, tiled=True),
            lax.all_gather(w_value, ("dp", "ctx"), axis=0, tiled=True),
            lax.all_gather(w_gate, ("dp", "ctx"), axis=0, tiled=True),
            lax.all_gather(w_up, ("dp", "ctx"), axis=0, tiled=True),
            lax.all_gather(w_out, ("dp", "ctx"), axis=1, tiled=True),
            lax.all_gather(w_down, ("dp", "ctx"), axis=1, tiled=True),
        )
        key_back, value_back = (
            lax.all_gather(key_low, "ctx", axis=1, tiled=True),
            lax.all_gather(value_low, "ctx", axis=1, tiled=True),
        )
        query_back, key_mat, value_mat, gate_back, up_back, out_back, down_back = back_weights
        grad_low = grads_all[micro_step].reshape(row_count, feature_width)
        grad_float = grads_all[micro_step].astype(jnp.float32)
        hidden_grad = dot_rows(grad_low, down_back)
        gate_grad = (
            hidden_grad * up_lin * sigmoid_gate * (1.0 + gate_lin * (1.0 - sigmoid_gate))
        ).astype(jnp.bfloat16)
        up_grad = (hidden_grad * gate_lin * sigmoid_gate).astype(jnp.bfloat16)
        normed_grad = dot_rows(gate_grad, gate_back) + dot_rows(up_grad, up_back)
        normed_grad = lax.psum(normed_grad, "mp").reshape(seq_local, span_len, feature_width)
        residual_grad = grad_float + norm_backward(normed_grad, normed_two, inverse_two)
        residual_low = residual_grad.astype(jnp.bfloat16).reshape(row_count, feature_width)
        mixed_grad = (
            dot_rows(residual_low, out_back)
            .astype(jnp.bfloat16)
            .reshape(seq_local, span_len, head_count * HD)
        )
        query_parts = []
        key_parts = []
        value_parts = []
        for head_index in range(head_count):
            head_cols = slice(head_index * HD, (head_index + 1) * HD)
            query_head = query_low[..., head_cols]
            key_head = key_back[..., head_cols]
            mixed_head = mixed_grad[..., head_cols]
            scores = (
                jnp.einsum("sqd,skd->sqk", query_head, key_head, preferred_element_type=jnp.float32)
                * score_scale
            )
            scores = jnp.where(allowed, scores, NEG_FILL)
            probs = jnp.exp(scores - log_totals[head_index])
            probs_low = probs.astype(jnp.bfloat16)
            value_parts.append(
                jnp.einsum(
                    "sqk,sqd->skd", probs_low, mixed_head, preferred_element_type=jnp.float32
                )
            )
            probs_grad = jnp.einsum(
                "sqd,skd->sqk",
                mixed_head,
                value_back[..., head_cols],
                preferred_element_type=jnp.float32,
            )
            row_dot = jnp.sum(probs * probs_grad, axis=-1, keepdims=True)
            scores_grad = (probs * (probs_grad - row_dot)).astype(jnp.bfloat16)
            query_parts.append(
                jnp.einsum(
                    "sqk,skd->sqd", scores_grad, key_head, preferred_element_type=jnp.float32
                )
                * score_scale
            )
            key_parts.append(
                jnp.einsum(
                    "sqk,sqd->skd", scores_grad, query_head, preferred_element_type=jnp.float32
                )
                * score_scale
            )
        key_terms = jnp.concatenate(key_parts, axis=-1)
        value_terms = jnp.concatenate(value_parts, axis=-1)
        key_grad_own, value_grad_own = (
            lax.psum_scatter(key_terms, "ctx", scatter_dimension=1, tiled=True),
            lax.psum_scatter(value_terms, "ctx", scatter_dimension=1, tiled=True),
        )
        query_sum = jnp.concatenate(query_parts, axis=-1).reshape(
            seq_local, span_len, head_count, HD
        )
        query_grad = (
            rope_turn(query_sum, cosine, -sine_part)
            .astype(jnp.bfloat16)
            .reshape(row_count, head_count * HD)
        )
        key_grad = (
            rope_turn(key_grad_own.reshape(seq_local, span_len, head_count, HD), cosine, -sine_part)
            .astype(jnp.bfloat16)
            .reshape(row_count, head_count * HD)
        )
        value_grad = value_grad_own.astype(jnp.bfloat16).reshape(row_count, head_count * HD)
        input_terms = (
            dot_rows(query_grad, query_back)
            + dot_rows(key_grad, key_mat)
            + dot_rows(value_grad, value_mat)
        )
        input_sum = (
            lax.psum(input_terms.astype(jnp.bfloat16), "mp")
            .astype(jnp.float32)
            .reshape(seq_local, span_len, feature_width)
        )
        grad_whole = residual_grad + norm_backward(input_sum, normed, inverse_one)
        input_grads.append(
            lax.dynamic_slice_in_dim(grad_whole, model_index * local_width, local_width, 2)
        )
        new_terms = (
            dot_cols(normed_low, query_grad),
            dot_cols(normed_low, key_grad),
            dot_cols(normed_low, value_grad),
            dot_cols(second_low, gate_grad),
            dot_cols(second_low, up_grad),
            dot_cols(mixed_low, residual_low),
            dot_cols(hidden_low, grad_low),
        )
        if totals is None:
            totals = new_terms
        else:
            totals = tuple((older + newer for older, newer in zip(totals, new_terms)))
    grads_total = (
        lax.psum_scatter(
            totals[0].astype(jnp.bfloat16), ("dp", "ctx"), scatter_dimension=0, tiled=True
        ).astype(jnp.float32),
        lax.psum_scatter(
            totals[1].astype(jnp.bfloat16), ("dp", "ctx"), scatter_dimension=0, tiled=True
        ).astype(jnp.float32),
        lax.psum_scatter(
            totals[2].astype(jnp.bfloat16), ("dp", "ctx"), scatter_dimension=0, tiled=True
        ).astype(jnp.float32),
        lax.psum_scatter(
            totals[3].astype(jnp.bfloat16), ("dp", "ctx"), scatter_dimension=0, tiled=True
        ).astype(jnp.float32),
        lax.psum_scatter(
            totals[4].astype(jnp.bfloat16), ("dp", "ctx"), scatter_dimension=0, tiled=True
        ).astype(jnp.float32),
        lax.psum_scatter(
            totals[5].astype(jnp.bfloat16), ("dp", "ctx"), scatter_dimension=1, tiled=True
        ).astype(jnp.float32),
        lax.psum_scatter(
            totals[6].astype(jnp.bfloat16), ("dp", "ctx"), scatter_dimension=1, tiled=True
        ).astype(jnp.float32),
    )
    return (
        jnp.stack(outputs, axis=0),
        jnp.stack(input_grads, axis=0),
        grads_total[0],
        grads_total[1],
        grads_total[2],
        grads_total[5],
        grads_total[3],
        grads_total[4],
        grads_total[6],
    )


MESH = pl.DeviceIdType.MESH
HBM = pl.BlockSpec(memory_space=pl.ANY)
LOW = jnp.bfloat16
FULL = jnp.float32
TILE = 256
PIECES = 4
VMEM_BYTES = 63 * 1024 * 1024


def contract(left, right, left_dim, right_dim):
    return lax.dot_general(
        left, right, (((left_dim,), (right_dim,)), ((), ())), preferred_element_type=FULL
    )


def aligned(start, size, unit=None):
    return pl.ds(pl.multiple_of(start, size if unit is None else unit), size)


class Place:
    def __init__(self):
        self.dp = lax.axis_index("dp")
        self.ctx = lax.axis_index("ctx")
        self.mp = lax.axis_index("mp")
        self.high = self.ctx // 2
        self.low = self.ctx % 2
        self.chip = self.mp // 2
        self.core = self.mp % 2
        self.home = self.dp * 4 + self.ctx
        self.inner = self.high != self.low

    def along(self, mask):
        other = self.ctx + mask - 2 * (self.ctx & mask)
        return (self.dp, other, self.mp)

    def across(self):
        return (1 - self.dp, self.ctx, self.mp)

    def beside_chip(self):
        return (self.dp, self.ctx, (1 - self.chip) * 2 + self.core)

    def beside_core(self):
        return (self.dp, self.ctx, self.chip * 2 + 1 - self.core)

    def shard_rows(self, low, chip, core, size=128):
        return aligned((core * 4 + chip * 2 + low) * 128, size, 128)


class Mover:
    def __init__(self, send, receive, local):
        self.send, self.receive, self.local = send, receive, local
        self.remote_count = 0
        self.local_count = 0

    def to(self, source, target, device):
        slot = self.remote_count
        self.remote_count += 1
        copy = pltpu.make_async_remote_copy(
            src_ref=source,
            dst_ref=target,
            send_sem=self.send.at[slot],
            recv_sem=self.receive.at[slot],
            device_id=device,
            device_id_type=MESH,
        )
        copy.start()
        return copy

    def hold(self, source, target, device, receive_slot=None):
        slot = self.remote_count
        self.remote_count += 1
        copy = pltpu.make_async_remote_copy(
            src_ref=source,
            dst_ref=target,
            send_sem=self.send.at[slot],
            recv_sem=self.receive.at[slot if receive_slot is None else receive_slot],
            device_id=device,
            device_id_type=MESH,
        )
        return HeldCopy(copy, slot)

    def here(self, source, target):
        slot = self.local_count
        self.local_count += 1
        copy = pltpu.make_async_copy(source, target, self.local.at[slot])
        copy.start()
        return copy


class HeldCopy:
    def __init__(self, copy, slot):
        self.copy, self.slot = copy, slot

    def start_if(self, wanted):
        @pl.when(wanted)
        def _():
            self.copy.start()

    def wait_send_if(self, wanted):
        @pl.when(wanted)
        def _():
            self.copy.wait_send()

    def wait_recv(self):
        self.copy.wait_recv()


def greet(partners):
    barrier = pltpu.get_barrier_semaphore()
    for partner in partners:
        pl.semaphore_signal(barrier, inc=1, device_id=partner, device_id_type=MESH)
    pl.semaphore_wait(barrier, len(partners))


class GroupGather:
    def __init__(self, place, mover, view, own):
        self.place, self.mover, self.view = place, mover, view
        p = place
        landing = view(p.low, p.chip, p.core)
        self.along = mover.to(own, landing, p.along(1))
        self.chip = mover.to(own, landing, p.beside_chip())
        self.core = mover.to(own, landing, p.beside_core())
        self.sent = [self.along, self.chip, self.core]

    def relay_along(self):
        p = self.place
        self.along.wait_recv()
        piece = self.view(1 - p.low, p.chip, p.core)
        self.corner = self.mover.to(piece, piece, p.beside_chip())
        self.along_core = self.mover.to(piece, piece, p.beside_core())
        self.sent += [self.corner, self.along_core]

    def relay_chip(self):
        p = self.place
        self.chip.wait_recv()
        piece = self.view(p.low, 1 - p.chip, p.core)
        self.chip_core = self.mover.to(piece, piece, p.beside_core())
        self.sent.append(self.chip_core)

    def relay_corner(self):
        p = self.place
        self.corner.wait_recv()
        piece = self.view(1 - p.low, 1 - p.chip, p.core)
        self.corner_core = self.mover.to(piece, piece, p.beside_core())
        self.sent.append(self.corner_core)

    def finish(self):
        for copy in (self.core, self.along_core, self.chip_core, self.corner_core):
            copy.wait_recv()
        for copy in self.sent:
            copy.wait_send()


class GroupScatter:
    def __init__(self, place, mover, buffers, terms):
        self.place, self.mover, self.buffers, self.terms = place, mover, buffers, terms
        self.sent = []

    def half(self, part):
        return pl.ds(part * TILE, TILE)

    def rows(self, chip, core):
        return self.place.shard_rows(0, chip, core, TILE)

    def start_core(self, part):
        p = self.place
        core_send, core_recv = self.buffers[:2]
        chip = 1 - p.chip if part == 0 else p.chip
        core_send[self.half(part), :] = self.terms(self.rows(chip, 1 - p.core)).astype(LOW)
        copy = self.mover.to(
            core_send.at[self.half(part)], core_recv.at[self.half(part)], p.beside_core()
        )
        self.sent.append(copy)
        if part == 0:
            self.core_first = copy
        else:
            self.core_second = copy

    def start_chip(self):
        p = self.place
        core_recv, chip_send, chip_recv = self.buffers[1:4]
        total = self.terms(self.rows(1 - p.chip, p.core))
        self.core_first.wait_recv()
        chip_send[...] = (total + core_recv[self.half(0), :].astype(FULL)).astype(LOW)
        self.chip_copies = []
        for which in (1 - p.low, p.low):
            rows = aligned(which * 128, 128)
            self.chip_copies.append(
                self.mover.to(chip_send.at[rows], chip_recv.at[rows], p.beside_chip())
            )
        self.sent += self.chip_copies

    def start_along(self):
        p = self.place
        core_recv, _, chip_recv, along_send, along_recv, total_ref = self.buffers[1:]
        total = self.terms(self.rows(p.chip, p.core))
        self.core_second.wait_recv()
        total_ref[...] = total + core_recv[self.half(1), :].astype(FULL)
        self.chip_copies[0].wait_recv()
        rows = aligned((1 - p.low) * 128, 128)
        along_send[...] = (total_ref[rows, :] + chip_recv[rows, :].astype(FULL)).astype(LOW)
        self.along = self.mover.to(along_send, along_recv, p.along(1))
        self.sent.append(self.along)

    def result(self):
        p = self.place
        chip_recv, _, along_recv, total_ref = self.buffers[3:]
        self.chip_copies[1].wait_recv()
        rows = aligned(p.low * 128, 128)
        total = total_ref[rows, :] + chip_recv[rows, :].astype(FULL)
        self.along.wait_recv()
        total = total + along_recv[...].astype(FULL)
        for copy in self.sent:
            copy.wait_send()
        return total


def scatter_buffers(width):
    return [
        pltpu.VMEM((2 * TILE, width), LOW),
        pltpu.VMEM((2 * TILE, width), LOW),
        pltpu.VMEM((TILE, width), LOW),
        pltpu.VMEM((TILE, width), LOW),
        pltpu.VMEM((TILE // 2, width), LOW),
        pltpu.VMEM((TILE // 2, width), LOW),
        pltpu.VMEM((TILE, width), FULL),
    ]


class WeightFetch:
    def __init__(self, place, mover, shard, whole, axis, start, size, landing):
        self.place, self.mover = place, mover
        half = shard.shape[axis] // 2
        block = shard.shape[1 - axis]

        def source(which):
            part = aligned(which * half + start, size, 128)
            return shard.at[:, part] if axis == 1 else shard.at[part, :]

        def target(ctx):
            span = aligned((place.dp * 4 + ctx) * block, block, 128)
            part = pl.ds(landing, size)
            return whole.at[span, part] if axis == 1 else whole.at[part, span]

        self.source, self.target = source, target

    def start(self):
        p = self.place
        mine = self.source(p.low)
        other = self.source(1 - p.low)
        spot = self.target(p.ctx)
        self.beside = self.mover.to(other, spot, p.along(1))
        self.corner = self.mover.hold(other, spot, p.along(3))
        self.corner.start_if(p.inner)
        self.ahead = self.mover.to(mine, spot, p.along(2))
        self.far = []

    def start_own(self):
        p = self.place
        mine, spot = self.source(p.low), self.target(p.ctx)
        self.own_far = self.mover.to(mine, spot, p.across())

    def send_across(self, mask):
        p = self.place
        block = self.target(p.along(mask)[1])
        self.far.append(self.mover.to(block, block, p.across()))

    def forward(self):
        p = self.place
        self.beside.wait_recv()
        block = self.target(p.along(1)[1])
        self.passed = self.mover.hold(block, block, p.along(2), self.corner.slot)
        self.passed.start_if(p.inner)
        self.send_across(1)

    def cross(self):
        self.ahead.wait_recv()
        self.send_across(2)
        self.corner.wait_recv()
        self.send_across(3)

    def finish(self):
        for copy in self.far + [self.own_far]:
            copy.wait_recv()

    def drain(self):
        for copy in self.far + [self.own_far, self.beside, self.ahead]:
            copy.wait_send()
        for copy in (self.corner, self.passed):
            copy.wait_send_if(self.place.inner)


def normalise(values):
    centred = values - jnp.mean(values, axis=-1, keepdims=True)
    inverse = lax.rsqrt(jnp.mean(centred * centred, axis=-1, keepdims=True) + EPSILON)
    return centred * inverse, inverse


def allowed_mask(seg_col, seg_row, start, keys):
    rows = seg_col[pl.ds(start, TILE), :][:, :1]
    cols = seg_row[0:1, pl.ds(0, keys)]
    row_place = start + lax.broadcasted_iota(jnp.int32, (TILE, keys), 0)
    col_place = lax.broadcasted_iota(jnp.int32, (TILE, keys), 1)
    return (rows == cols) & (col_place <= row_place)


def turn(values, cosine, sine_part):
    parts = []
    for start in range(0, values.shape[1], HD):
        head = values[:, start : start + HD]
        parts.append(head * cosine + pltpu.roll(head, HD // 2, 1) * sine_part)
    return jnp.concatenate(parts, axis=1)


class Staging:
    def __init__(self):
        self.last = None

    def free(self):
        if self.last is not None:
            self.last.wait()
            self.last = None


class GradReturn:
    def __init__(self, place, mover, axis, terms, sends, receives, loads, stage, own_out, before=None):
        self.place, self.mover, self.axis, self.terms = place, mover, axis, terms
        self.across_send, self.along_send, self.beside_send = sends
        self.across_recv, self.along_recv, self.beside_recv = receives
        self.loads, (self.stage, self.stage_ref), self.own_out = loads, stage, own_out
        self.before = before
        self.blocks = [place.along(3)[1], place.along(2)[1], place.along(1)[1], place.ctx]
        self.size = own_out.shape[0]
        self.arriving, self.leaving, self.here = {}, {}, set()

    def send(self, key, source, target, device):
        copy = self.mover.to(source, target, device)
        self.arriving[key] = self.leaving[key] = copy

    def arrived(self, key):
        if key not in self.here:
            self.here.add(key)
            self.arriving[key].wait_recv()

    def free(self, key):
        if self.before is not None:
            self.before.leaving.pop(key).wait_send()

    def part(self, half):
        count = self.size // 2
        return pl.ds(0, self.size) if half is None else pl.ds(half * count, count)

    def across(self, step):
        p = self.place
        value = self.terms((1 - p.dp) * 4 + self.blocks[step], self.part(None)).astype(LOW)
        self.free((0, step))
        self.across_send[step] = value
        self.send((0, step), self.across_send.at[step], self.across_recv.at[step], p.across())

    def summed(self, step, half, others):
        part = self.part(half)
        self.arrived((0, step))
        copies = [
            self.mover.here(self.across_recv.at[step, part, :], self.loads.at[0, part, :])
        ]
        for along_half in others:
            self.arrived((1, step - 2, along_half))
            spot = self.part(along_half)
            copies.append(
                self.mover.here(self.along_recv.at[step - 2, spot, :], self.loads.at[1, spot, :])
            )
        value = self.terms(self.place.dp * 4 + self.blocks[step], part)
        for copy in copies:
            copy.wait()
        value = value + self.loads[0, part, :].astype(FULL)
        if others:
            value = value + self.loads[1, part, :].astype(FULL)
        return value

    def along(self, step, half):
        part = self.part(half)
        value = self.summed(step, half, ()).astype(LOW)
        self.free((1, step, half))
        self.along_send[step, part, :] = value
        source = self.along_send.at[step, part, :]
        target = self.along_recv.at[step, part, :]
        self.send((1, step, half), source, target, self.place.along(2))

    def beside(self, half):
        part = self.part(half)
        value = self.summed(2, half, (half,)).astype(LOW)
        self.free((2, half))
        self.beside_send[part, :] = value
        source, target = self.beside_send.at[part, :], self.beside_recv.at[part, :]
        self.send((2, half), source, target, self.place.along(1))

    def own(self):
        value = self.summed(3, None, (0, 1))
        self.stage.free()
        self.stage_ref[...] = value
        self.stage.last = self.mover.here(self.stage_ref, self.own_out)

    def drain(self):
        for half in range(2):
            self.arrived((2, half))
        for copy in self.leaving.values():
            copy.wait_send()


def give_credit(place, credit):
    for slot, partner in enumerate((place.beside_core(), place.beside_chip(), place.along(1))):
        pl.semaphore_signal(credit.at[slot], inc=1, device_id=partner, device_id_type=MESH)


def block_cols(ref, block):
    return ref[:, aligned(block * TILE, TILE)]


class RowReturn:
    def __init__(self, place, send, receive, local):
        self.place, self.send, self.receive, self.local = place, send, receive, local
        self.goal = place.core * 2 + place.chip
        self.stays = place.ctx == self.goal

    def partners(self):
        p = self.place
        targets = [(p.dp, self.goal, model) for model in range(4)]
        sources = [(p.dp, ctx, p.low * 2 + p.high) for ctx in range(4)]
        return targets, sources

    def greet(self, others):
        p = self.place
        barrier = pltpu.get_barrier_semaphore()
        for other in others:
            pl.semaphore_signal(barrier, inc=1, device_id=other, device_id_type=MESH)
        targets, sources = self.partners()
        for model, target in enumerate(targets):

            @pl.when(jnp.logical_not(self.stays & (p.mp == model)))
            def _(target=target):
                pl.semaphore_signal(barrier, inc=1, device_id=target, device_id_type=MESH)

        for ctx, source in enumerate(sources):

            @pl.when(jnp.logical_not(self.stays & (p.ctx == ctx)))
            def _(source=source):
                pl.semaphore_signal(barrier, inc=1, device_id=source, device_id_type=MESH)

        @pl.when(self.stays)
        def _():
            pl.semaphore_wait(barrier, len(others) + 6)

        @pl.when(jnp.logical_not(self.stays))
        def _():
            pl.semaphore_wait(barrier, len(others) + 8)

    def copy(self, model):
        size = self.rows.shape[1] // 4
        return pltpu.make_async_remote_copy(
            src_ref=self.rows.at[:, pl.ds(model * size, size)],
            dst_ref=self.landing,
            send_sem=self.send.at[model],
            recv_sem=self.receive.at[self.place.ctx],
            device_id=(self.place.dp, self.goal, model),
            device_id_type=MESH,
        )

    def own_copy(self):
        size = self.rows.shape[1] // 4
        source = self.rows.at[:, aligned(self.place.mp * size, size)]
        return pltpu.make_async_copy(source, self.landing, self.local)

    def start(self, rows, whole):
        p = self.place
        self.rows, self.whole = rows, whole
        count = rows.shape[0]
        self.landing = whole.at[p.high, 0, aligned(p.low * count, count), :]
        for model in range(4):

            @pl.when(jnp.logical_not(self.stays & (p.mp == model)))
            def _(model=model):
                self.copy(model).start()

        @pl.when(self.stays)
        def _():
            self.own_copy().start()

    def finish(self):
        p = self.place
        for model in range(4):

            @pl.when(jnp.logical_not(self.stays & (p.mp == model)))
            def _(model=model):
                self.copy(model).wait_send()

        for ctx in range(4):

            @pl.when(jnp.logical_not(self.stays & (p.ctx == ctx)))
            def _(ctx=ctx):
                count = self.rows.shape[0]
                spot = self.whole.at[ctx // 2, 0, pl.ds((ctx % 2) * count, count), :]
                pltpu.make_async_remote_copy(
                    src_ref=spot,
                    dst_ref=spot,
                    send_sem=self.send.at[0],
                    recv_sem=self.receive.at[ctx],
                    device_id=(p.dp, ctx, p.low * 2 + p.high),
                    device_id_type=MESH,
                ).wait_recv()

        @pl.when(self.stays)
        def _():
            self.own_copy().wait()


ORDER = (
    64, 33, 0, 8, 65, 9, 2, 1, 3, 44, 10, 69, 5, 45, 66, 4, 11, 13, 53, 21,
    46, 75, 12, 67, 25, 47, 6, 40, 72, 70, 68, 77, 32, 7, 76, 71, 73, 42, 14, 49,
    20, 15, 28, 17, 29, 79, 61, 74, 86, 41, 43, 84, 85, 83, 103, 16, 37, 36, 78, 87,
    88, 89, 57, 90, 80, 22, 30, 34, 81, 31, 18, 38, 23, 104, 24, 82, 19, 35, 39, 106,
    60, 105, 111, 26, 48, 27, 62, 107, 50, 56, 108, 110, 109, 63, 112, 52, 51, 113, 114, 58,
    115, 175, 120, 59, 119, 54, 55, 124, 116, 121, 125, 118, 122, 117, 91, 92, 93, 127, 131, 126,
    94, 132, 135, 136, 142, 143, 134, 128, 176, 146, 147, 95, 133, 138, 96, 97, 180, 145, 123, 137,
    177, 98, 140, 179, 139, 178, 183, 185, 154, 155, 189, 149, 148, 188, 144, 130, 184, 156, 141, 129,
    181, 187, 186, 190, 99, 182, 164, 151, 100, 165, 153, 150, 170, 166, 169, 157, 168, 101, 159, 102,
    173, 172, 158, 160, 171, 191, 167, 163, 161, 152, 162, 174, 192,
)


def run_steps(steps, order):
    for place in order:
        steps[place]()


def layer_kernel(
    tokens_in, out_grad, w_query, w_key, w_value, w_out, w_gate, w_up, w_down,
    segment, freqs,
    tokens_out, grad_rows, down_own, down_near, gate_own, gate_near, up_own, up_near, out_own, out_near, three_own, three_near,
    qkv_all, grads_all, normed_all, back_all,
    query_all, key_all, value_all, mixed_all,
    gate_far, gate_mid, up_far, up_mid, down_far, down_mid, three_far, three_mid, out_far, out_mid,
    second, grads, gate_here, up_here, down_here, pair, up_back, out_here, key_sum, value_sum,
    wide_far, wide_mid, wide_near, wide_loads, wide_stage, tall_far, tall_mid, tall_near, tall_loads, tall_stage,
    core_send, core_recv, chip_send, chip_recv, along_send, along_recv, total_ref, rows_low, back_rows,
    residual, inverse_two, log_total, cosine, sine_part, seg_col, seg_row, seg_mine, kept,
    credit, send, receive, local, feed_send, feed_receive, feed_local, row_send, row_receive, row_local,
):
    p = Place()
    mover = Mover(send, receive, local)
    feed_return = RowReturn(p, feed_send, feed_receive, feed_local)
    row_return = RowReturn(p, row_send, row_receive, row_local)
    row_return.greet(
        [p.along(1), p.along(2), p.along(3), p.across(), p.beside_chip(), p.beside_core()]
    )
    hidden, gate_back = pair.at[0], pair.at[1]
    length = grads.shape[0]
    units = hidden.shape[1]
    span, feats = tokens_in.shape[2:]
    cols = out_here.shape[0]
    head_count = cols // HD
    blocks = length // TILE
    score_scale = 1.0 / math.sqrt(HD)
    tokens = grads
    first, later = pl.ds(0, length), pl.ds(length, length)
    query, key, value, mixed = [up_here.at[first, pl.ds(slot * cols, cols)] for slot in range(4)]
    three_back = up_here.at[later, pl.ds(0, 3 * cols)]
    mixed_back = up_here.at[later, pl.ds(3 * cols, cols)]
    qkv_here = gate_here.at[:, pl.ds(0, 3 * cols)]
    qkv_early = pair.at[:, :, pl.ds(0, 3 * cols)]
    attended = ((query, query_all), (key, key_all), (value, value_all), (mixed, mixed_all))
    early = [up_back.at[:, pl.ds(slot * cols, cols)] for slot in range(4)]
    query_early, key_early, value_early, mixed_early = early
    my_rows = p.shard_rows(p.low, p.chip, p.core)
    steps = []
    step = steps.append
    made = types.SimpleNamespace()

    def block_of(whole, ctx, model):
        return whole.at[aligned(ctx * span, span), aligned(model * feats, feats)]

    def own_view(whole):
        return lambda low, chip, core: block_of(whole, p.high * 2 + low, chip * 2 + core)

    def other_view(whole):
        return lambda low, chip, core: block_of(whole, (1 - p.high) * 2 + low, chip * 2 + core)

    def row_view(whole):
        return lambda low, chip, core: whole.at[p.shard_rows(low, chip, core)]

    def relays(gather):
        step(lambda: gather().relay_along())
        step(lambda: gather().relay_chip())
        step(lambda: gather().relay_corner())

    def fetch(shard, whole, axis, landing=0, pieces=1):
        size = shard.shape[axis] // 2 // pieces
        for piece in range(pieces):
            chunk = WeightFetch(
                p, mover, shard, whole, axis, piece * size, size, landing + piece * size
            )
            chunks.append(chunk)
            for action in (chunk.start, chunk.start_own, chunk.forward, chunk.cross):
                step(action)

    chunks = []
    fetch(w_query, qkv_all, 1, 0)
    fetch(w_key, qkv_all, 1, cols)
    fetch(w_value, qkv_all, 1, 2 * cols)
    fetch(w_out, out_here, 0)
    fetch(w_gate, gate_here, 1, 0, PIECES)
    fetch(w_up, up_here, 1, 0, PIECES)
    fetch(w_down, down_here, 0, 0, PIECES)
    of_gate, of_up, of_down = [chunks[4 + slot * PIECES :][:PIECES] for slot in range(3)]

    @step
    def _():
        spot = aligned(p.home * TILE, TILE)
        made.own_blocks = []
        for shard, whole in ((w_out, out_here), (w_down, down_here)):
            half = shard.shape[0] // 2
            source = shard.at[aligned(p.low * half, half), :]
            made.own_blocks.append(mover.here(source, whole.at[:, spot]))
        for shard, whole in ((w_gate, gate_here), (w_up, up_here)):
            half = shard.shape[1] // 2
            source = shard.at[:, aligned(p.low * half, half)]
            made.own_blocks.append(mover.here(source, whole.at[spot, :]))
        made.seg = []
        for which in range(2):
            numbers = segment[which].astype(FULL)
            seg_mine[which] = jnp.broadcast_to(numbers, seg_mine.shape[1:])
        spot = aligned(p.ctx * span, span)
        for mask in (1, 2, 3):
            goal = p.high if mask == 1 else 1 - p.high
            made.seg.append(
                mover.to(seg_mine.at[goal], seg_row.at[:, spot], p.along(mask))
            )
        made.seg.append(mover.here(seg_mine.at[p.high], seg_row.at[:, spot]))
        here = block_of(tokens, p.ctx, p.mp)
        made.swap = mover.to(tokens_in.at[1 - p.high, 0], here, p.along(2))
        own_tokens = tokens_in.at[p.high, 0]
        made.tokens = mover.here(own_tokens, here)
        made.own = GroupGather(p, mover, own_view(tokens), own_tokens)

    @step
    def _():
        made.swap.wait_recv()
        theirs = block_of(tokens, p.along(2)[1], p.mp)
        made.other = GroupGather(p, mover, other_view(tokens), theirs)

    relays(lambda: made.own)
    relays(lambda: made.other)

    @step
    def _():
        for copy in made.seg:
            copy.wait()
        for begin in range(0, length, TILE):
            rows = pl.ds(begin, TILE)
            numbers = jnp.broadcast_to(seg_row[0:1, rows], (HD, TILE))
            seg_col[rows, :] = numbers.T
            allowed = allowed_mask(seg_col, seg_row, begin, begin + TILE)
            position = jnp.sum(jnp.where(allowed, 1.0, 0.0), axis=1, keepdims=True) - 1.0
            angle = position * freqs[0:1, :]
            cosine[rows, :] = jnp.cos(angle)
            lane = lax.broadcasted_iota(jnp.int32, (TILE, HD), 1)
            sine = jnp.sin(angle)
            sine_part[rows, :] = jnp.where(lane < HD // 2, -sine, sine)

    @step
    def _():
        made.tokens.wait()
        made.swap.wait_send()
        made.own.finish()
        made.other.finish()
        kept[...] = tokens[my_rows, :]
        residual[...] = kept[...].astype(FULL)
        for begin in range(0, length, 128):
            rows = pl.ds(begin, 128)
            tokens[rows, :] = normalise(tokens[rows, :].astype(FULL))[0].astype(LOW)
        made.normed = mover.here(tokens, normed_all)

    def load_three(cut):
        copies = []
        for turn_by in range(1, 8):
            block = lax.rem(p.home + turn_by, 8)
            source = qkv_all.at[aligned(block * TILE, TILE), :]
            copies.append(mover.here(source, cut(block)))
        for slot, shard in enumerate((w_query, w_key, w_value)):
            source = shard.at[:, aligned(p.low * cols, cols)]
            target = cut(p.home).at[:, pl.ds(slot * cols, cols)]
            copies.append(mover.here(source, target))
        return copies

    def wait_all(copies):
        for copy in copies:
            copy.wait()

    @step
    def _():
        for chunk in chunks[:3]:
            chunk.finish()
        wait_all(
            load_three(
                lambda block: qkv_early.at[block // 4, aligned(lax.rem(block, 4) * TILE, TILE), :]
            )
        )
        for begin in range(0, length, TILE):
            rows = pl.ds(begin, TILE)
            three = contract(tokens[rows, pl.ds(0, units)], qkv_early[0], 1, 0) + contract(
                tokens[rows, pl.ds(units, units)], qkv_early[1], 1, 0
            )
            turned = [
                turn(three[:, start : start + cols], cosine[rows, :], sine_part[rows, :])
                for start in (0, cols)
            ]
            query_early[rows, :] = turned[0].astype(LOW)
            key_early[rows, :] = turned[1].astype(LOW)
            value_early[rows, :] = three[:, 2 * cols :].astype(LOW)

    @step
    def _():
        spot = block_of(grads_all, p.ctx, p.mp)
        own = out_grad.at[p.high, 0]
        made.cot_swap = mover.to(out_grad.at[1 - p.high, 0], spot, p.along(2))
        made.cot_own = GroupGather(p, mover, own_view(grads_all), own)

    @step
    def _():
        made.cot_swap.wait_recv()
        theirs = block_of(grads_all, p.along(2)[1], p.mp)
        made.cot_other = GroupGather(p, mover, other_view(grads_all), theirs)

    relays(lambda: made.cot_own)
    relays(lambda: made.cot_other)

    def attend(begin):
        rows = pl.ds(begin, TILE)
        keys = begin + TILE
        allowed = allowed_mask(seg_col, seg_row, begin, keys)
        for head in range(head_count):
            head_cols = pl.ds(head * HD, HD)
            scores = contract(query_early[rows, head_cols], key_early[pl.ds(0, keys), head_cols], 1, 1)
            scores = jnp.where(allowed, scores * score_scale, NEG_FILL)
            highest = jnp.max(scores, axis=-1, keepdims=True)
            exp_terms = jnp.exp(scores - highest)
            total_exp = jnp.sum(exp_terms, axis=-1, keepdims=True)
            probs_low = (exp_terms * (1.0 / total_exp)).astype(LOW)
            mixed_early[rows, head_cols] = contract(
                probs_low, value_early[pl.ds(0, keys), head_cols], 1, 0
            ).astype(LOW)
            log_total[rows, head_cols] = jnp.broadcast_to(
                highest + jnp.log(total_exp), (TILE, HD)
            )

    for block in range(blocks):
        step(functools.partial(attend, block * TILE))

    buffers = (core_send, core_recv, chip_send, chip_recv, along_send, along_recv, total_ref)

    def scatter_steps(terms, waits=True):
        scatter = GroupScatter(p, mover, buffers, terms)

        def stage(action, slot, part=None):
            def run():
                if waits and part != 1:
                    pl.semaphore_wait(credit.at[slot], 1)
                action() if part is None else action(part)

            return run

        step(stage(scatter.start_core, 0, 0))
        step(stage(scatter.start_core, 0, 1))
        step(stage(scatter.start_chip, 1))
        step(stage(scatter.start_along, 2))
        return scatter

    branch_sum = scatter_steps( lambda rows: contract(mixed_early[rows, :], out_here[...], 1, 0), False
    )
    back_sum = scatter_steps(
        lambda rows: contract(gate_back[rows, :], gate_here[...], 1, 1)
        + contract(up_back[rows, :], up_here[...], 1, 1),
    )
    feed_sum = scatter_steps( lambda rows: contract(hidden[rows, :], down_here[...], 1, 0)
    )
    input_sum = scatter_steps( lambda rows: contract(three_back[rows, :], qkv_here[...], 1, 1)
    )

    @step
    def _():
        chunks[3].finish()
        made.own_blocks[0].wait()
        made.saves = [mover.here(source, target) for source, (_, target) in zip(early, attended)]

    @step
    def _():
        branch = branch_sum.result()
        give_credit(p, credit)
        hidden_rows = residual[...] + branch
        residual[...] = hidden_rows
        normed_two, inverse = normalise(hidden_rows)
        inverse_two[...] = jnp.broadcast_to(inverse, inverse_two.shape)
        rows_low[...] = normed_two.astype(LOW)
        view = row_view(second)
        made.second_local = mover.here(rows_low, view(p.low, p.chip, p.core))
        made.second = GroupGather(p, mover, view, rows_low)

    relays(lambda: made.second)

    @step
    def _():
        for chunk in of_gate:
            chunk.finish()
        made.own_blocks[2].wait()

    @step
    def _():
        for copy in made.saves:
            copy.wait()
        for chunk in of_up:
            chunk.finish()
        made.own_blocks[3].wait()

    @step
    def _():
        made.second.finish()
        made.second_local.wait()

    @step
    def _():
        made.cot_own.finish()
        made.cot_other.finish()
        made.cot_swap.wait_send()
        made.normed.wait()
        made.cot_load = [mover.here(out_grad.at[p.high, 0], block_of(grads, p.ctx, p.mp))]
        for turn_by in range(1, 16):
            which = lax.rem(p.ctx * 4 + p.mp + turn_by, 16)
            made.cot_load.append(
                mover.here(
                    block_of(grads_all, which // 4, lax.rem(which, 4)),
                    block_of(grads, which // 4, lax.rem(which, 4)),
                )
            )

    def hidden_block(block):
        rows = pl.ds(block * TILE, TILE)
        for begin in range(0, units, TILE):
            part = pl.ds(begin, TILE)
            gate = contract(second[rows, :], gate_here[:, part], 1, 0)
            up = contract(second[rows, :], up_here[:, part], 1, 0)
            share = jax.nn.sigmoid(gate)
            silu = gate * share
            hidden[rows, part] = (silu * up).astype(LOW)
            gate_back[rows, part] = (up * share * (1.0 + gate * (1.0 - share))).astype(LOW)
            up_back[rows, part] = silu.astype(LOW)

    for block in range(blocks):
        step(functools.partial(hidden_block, block))

    def back_block(begin, index):
        rows, part = pl.ds(index * TILE, TILE), pl.ds(begin, TILE)
        back = contract(grads[rows, :], down_here[part, :], 1, 1)
        gate_back[rows, part] = (back * gate_back[rows, part].astype(FULL)).astype(LOW)
        up_back[rows, part] = (back * up_back[rows, part].astype(FULL)).astype(LOW)

    waited = set()

    def back_piece(which):
        piece = units // PIECES
        of_down[which].finish()
        if "down" not in waited:
            waited.add("down")
            made.own_blocks[1].wait()
        for begin in range(which * piece, (which + 1) * piece, TILE):
            for index in range(blocks):
                back_block(begin, index)

    for which in range(PIECES):
        step(functools.partial(back_piece, which))

    def narrow(ref):
        part = pl.ds(0, 3 * cols)
        return ref.at[:, part] if len(ref.shape) == 2 else ref.at[:, :, part]

    def short(ref):
        part = pl.ds(0, cols)
        return ref.at[part, :] if len(ref.shape) == 2 else ref.at[:, part, :]

    def left_terms(left, right):
        def terms(block, part):
            span = aligned(block * TILE + part.start, part.size, 128)
            return contract(left[:, span], right[...], 0, 0)

        return terms

    def right_terms(left, right):
        return lambda block, part: contract(left[:, part], block_cols(right, block), 0, 0)

    wide_staging, tall_staging = Staging(), Staging()
    wide_sends, tall_sends = (wide_far, wide_mid, wide_near), (tall_far, tall_mid, tall_near)
    return_down = GradReturn(
        p, mover, 0, right_terms(hidden, grads), tall_sends, (down_far, down_mid, down_near), tall_loads,
        (tall_staging, tall_stage), down_own,
    )
    return_gate = GradReturn(
        p, mover, 1, left_terms(second, gate_back), wide_sends, (gate_far, gate_mid, gate_near), wide_loads,
        (wide_staging, wide_stage), gate_own,
    )
    return_up = GradReturn(
        p, mover, 1, left_terms(second, up_back), wide_sends, (up_far, up_mid, up_near), wide_loads,
        (wide_staging, wide_stage), up_own, return_gate,
    )
    return_out = GradReturn(
        p, mover, 0, right_terms(mixed, down_here), [short(ref) for ref in tall_sends],
        (out_far, out_mid, out_near), short(tall_loads), (tall_staging, short(tall_stage)), out_own, return_down,
    )
    return_three = GradReturn(
        p, mover, 1, left_terms(grads, three_back), [narrow(ref) for ref in wide_sends],
        (three_far, three_mid, three_near), narrow(wide_loads), (wide_staging, narrow(wide_stage)), three_own,
        return_up,
    )
    returns = [return_down, return_gate, return_up, return_out, return_three]
    for part in returns:
        for which in range(4):
            step(functools.partial(part.across, which))
        for which in range(2):
            for half in range(2):
                step(functools.partial(part.along, which, half))
        for half in range(2):
            step(functools.partial(part.beside, half))
        step(part.own)

    @step
    def _():
        wait_all(made.cot_load)

    @step
    def _():
        normed_grad = back_sum.result()
        give_credit(p, credit)
        inverse = inverse_two[:, :1]
        centred = residual[...] - jnp.mean(residual[...], axis=-1, keepdims=True)
        back_value = grads[my_rows, :].astype(FULL) + norm_backward(
            normed_grad, centred * inverse, inverse
        )
        back_rows[...] = back_value
        rows_low[...] = back_value.astype(LOW)
        view = row_view(back_all)
        made.back_local = mover.here(rows_low, view(p.low, p.chip, p.core))
        made.back = GroupGather(p, mover, view, rows_low)

    relays(lambda: made.back)

    @step
    def _():
        for chunk in chunks:
            chunk.drain()
        made.refill = [mover.here(source, target) for target, source in attended]
        made.refill += load_three(lambda block: qkv_here.at[aligned(block * TILE, TILE), :])

    @step
    def _():
        made.norm_load = mover.here(normed_all, grads)

    @step
    def _():
        made.norm_load.wait()

    @step
    def _():
        made.back.finish()
        made.back_local.wait()
        made.back_load = mover.here(back_all, down_here)

    @step
    def _():
        rows_low[...] = (residual[...] + feed_sum.result()).astype(LOW)
        give_credit(p, credit)
        feed_return.start(rows_low, tokens_out)

    @step
    def _():
        made.back_load.wait()
        wait_all(made.refill)
        for begin in range(0, length, TILE):
            rows = pl.ds(begin, TILE)
            mixed_back[rows, :] = contract(down_here[rows, :], out_here[...], 1, 1).astype(LOW)

    def attend_back(begin):
        rows = pl.ds(begin, TILE)
        keys = begin + TILE
        key_rows = pl.ds(0, keys)
        allowed = allowed_mask(seg_col, seg_row, begin, keys)
        query_parts = []
        for head in range(head_count):
            head_cols = pl.ds(head * HD, HD)
            query_head, key_head = query[rows, head_cols], key[key_rows, head_cols]
            mixed_head = mixed_back[rows, head_cols]
            scores = contract(query_head, key_head, 1, 1) * score_scale
            scores = jnp.where(allowed, scores, NEG_FILL)
            probs = jnp.exp(scores - log_total[rows, pl.ds(head * HD, 1)])
            value_terms = contract(probs.astype(LOW), mixed_head, 0, 0)
            probs_back = contract(mixed_head, value[key_rows, head_cols], 1, 1)
            row_dot = jnp.sum(probs * probs_back, axis=-1, keepdims=True)
            scores_back = (probs * (probs_back - row_dot)).astype(LOW)
            query_parts.append(contract(scores_back, key_head, 1, 0) * score_scale)
            key_terms = contract(scores_back, query_head, 0, 0)
            if keys == length:
                key_sum[key_rows, head_cols] = key_terms
                value_sum[key_rows, head_cols] = value_terms
            else:
                key_sum[key_rows, head_cols] += key_terms
                value_sum[key_rows, head_cols] += value_terms
        three_back[rows, pl.ds(0, cols)] = turn(
            jnp.concatenate(query_parts, axis=1), cosine[rows, :], -sine_part[rows, :]
        ).astype(LOW)

    for block in range(blocks):
        step(functools.partial(attend_back, block * TILE))

    @step
    def _():
        for begin in range(0, length, TILE):
            rows = pl.ds(begin, TILE)
            three_back[rows, pl.ds(cols, cols)] = turn(
                key_sum[rows, :] * score_scale, cosine[rows, :], -sine_part[rows, :]
            ).astype(LOW)
            three_back[rows, pl.ds(2 * cols, cols)] = value_sum[rows, :].astype(LOW)

    @step
    def _():
        kept_normed, inverse = normalise(kept[...].astype(FULL))
        summed = input_sum.result()
        feed_return.finish()
        rows_low[...] = (back_rows[...] + norm_backward(summed, kept_normed, inverse)).astype(LOW)
        row_return.start(rows_low, grad_rows)

    @step
    def _():
        row_return.finish()
        for part in returns:
            part.drain()
        wide_staging.free()
        tall_staging.free()

    run_steps(steps, ORDER)


def whole_layer(tokens_in, out_grad, segment, weights, freqs):
    span, feats = tokens_in.shape[2:]
    length, width = 4 * span, 4 * feats
    cols, units = weights[0].shape[1] // 2, weights[4].shape[1] // 2

    def low(*shape):
        return jax.ShapeDtypeStruct(shape, LOW)

    def full(*shape):
        return jax.ShapeDtypeStruct(shape, FULL)

    wide, tall = (TILE, units), (units, TILE)
    in_hbm = [low(2, 1, span, feats), low(2, 1, span, feats)]
    for block in (tall, wide, wide, (cols, TILE), (TILE, 3 * cols)):
        in_hbm += [full(*block), low(*block)]
    in_hbm += [low(width, 3 * cols)] + [low(length, width)] * 3 + [low(length, cols)] * 4
    for block in (wide, wide, tall, (TILE, 3 * cols), (cols, TILE)):
        in_hbm += [low(4, *block), low(2, *block)]
    vmem = pl.BlockSpec(memory_space=pltpu.VMEM)

    def sending(block):
        return [
            pltpu.VMEM((4, *block), LOW),
            pltpu.VMEM((2, *block), LOW),
            pltpu.VMEM(block, LOW),
            pltpu.VMEM((2, *block), LOW),
            pltpu.VMEM(block, FULL),
        ]

    row_semaphores = [
        pltpu.SemaphoreType.DMA((4,)),
        pltpu.SemaphoreType.DMA((4,)),
        pltpu.SemaphoreType.DMA,
    ]
    outs = pl.pallas_call(
        layer_kernel,
        out_shape=in_hbm,
        in_specs=[HBM] * 9 + [vmem] * 2,
        out_specs=[HBM] * len(in_hbm),
        scratch_shapes=[
            pltpu.VMEM((length, width), LOW),
            pltpu.VMEM((length, width), LOW),
            pltpu.VMEM((width, units), LOW),
            pltpu.VMEM((width, units), LOW),
            pltpu.VMEM((units, width), LOW),
            pltpu.VMEM((2, length, units), LOW),
            pltpu.VMEM((length, units), LOW),
            pltpu.VMEM((cols, width), LOW),
            pltpu.VMEM((length, cols), FULL),
            pltpu.VMEM((length, cols), FULL),
            *sending(wide),
            *sending(tall),
            *scatter_buffers(width),
            pltpu.VMEM((length // 8, width), LOW),
            pltpu.VMEM((length // 8, width), FULL),
            pltpu.VMEM((length // 8, width), FULL),
            pltpu.VMEM((length // 8, HD), FULL),
            pltpu.VMEM((length, cols), FULL),
            *[pltpu.VMEM((length, HD), FULL)] * 3,
            pltpu.VMEM((8, length), FULL),
            pltpu.VMEM((2, 8, span), FULL),
            pltpu.VMEM((length // 8, width), LOW),
            pltpu.SemaphoreType.REGULAR((3,)),
            pltpu.SemaphoreType.DMA((288,)),
            pltpu.SemaphoreType.DMA((288,)),
            pltpu.SemaphoreType.DMA((256,)),
            *row_semaphores,
            *row_semaphores,
        ],
        compiler_params=pltpu.CompilerParams(
            collective_id=1, has_side_effects=True, vmem_limit_bytes=VMEM_BYTES
        ),
    )(tokens_in, out_grad, *weights, segment, freqs)
    return outs[:12]


def hand_over_kernel(*refs):
    tokens_in, grad_in, *halves = refs[:12]
    tokens_out, grad_out, down, gate, up, out, query, key, value = refs[12:21]
    held, own_held, far_held, wide_held = refs[21:23], refs[23:28], refs[28:33], refs[33:39]
    load, save = refs[39:]
    low = lax.axis_index("ctx") % 2
    started, saves = [], []

    def copy(source, target, semaphores, which):
        made = pltpu.make_async_copy(source, target, semaphores.at[len(which)])
        made.start()
        which.append(made)
        return made

    owns = [copy(halves[2 * slot], own_held[slot], load, started) for slot in range(5)]
    fars = [copy(halves[2 * slot + 1], far_held[slot], load, started) for slot in range(5)]
    rows = [copy(ref, here, load, started) for ref, here in zip((tokens_in, grad_in), held)]

    def place(source, targets, axis, which):
        begin = 0
        for target in targets:
            size = target.shape[axis] // 2
            spot, part = aligned(which * size, size), pl.ds(begin, size)
            begin += size
            if axis == 1:
                copy(source.at[:, part], target.at[:, spot], save, saves)
            else:
                copy(source.at[part, :], target.at[spot, :], save, saves)

    goals = (((down,), 0), ((gate,), 1), ((up,), 1), ((out,), 0), ((query, key, value), 1))
    for slot, (targets, axis) in enumerate(goals):
        owns[slot].wait()
        place(own_held[slot], targets, axis, low)
    for slot, (targets, axis) in enumerate(goals):
        fars[slot].wait()
        wide_held[slot][...] = far_held[slot][...].astype(FULL)
        place(wide_held[slot], targets, axis, 1 - low)
    for made in rows:
        made.wait()
    copy(held[0], tokens_out, save, saves)
    wide_held[5][...] = held[1][...].astype(FULL)
    copy(wide_held[5], grad_out, save, saves)
    for made in saves:
        made.wait()


def hand_over(arrays, shapes):
    tokens_out, grad_in, *halves = arrays
    held = [tokens_out, grad_in, *halves[::2], *halves[1::2]]
    return pl.pallas_call(
        hand_over_kernel,
        out_shape=[jax.ShapeDtypeStruct(shape, kind) for shape, kind in shapes],
        in_specs=[HBM] * 12,
        out_specs=[HBM] * len(shapes),
        scratch_shapes=[
            *[pltpu.VMEM(array.shape, array.dtype) for array in held],
            *[pltpu.VMEM(array.shape, FULL) for array in (*halves[1::2], grad_in)],
            pltpu.SemaphoreType.DMA((16,)),
            pltpu.SemaphoreType.DMA((24,)),
        ],
        compiler_params=pltpu.CompilerParams(vmem_limit_bytes=VMEM_BYTES),
    )(tokens_out, grad_in, *halves)


def per_device_grouped(
    tokens_in, out_grad, segment_ids, w_query, w_key, w_value, w_out, w_gate, w_up, w_down
):
    freq_half = np.power(10000.0, -2.0 * np.arange(HD // 2) / HD)
    freqs = np.tile(np.concatenate([freq_half, freq_half]), (8, 1)).astype(np.float32)
    results = whole_layer(
        tokens_in, out_grad, segment_ids, (w_query, w_key, w_value, w_out, w_gate, w_up, w_down), jnp.asarray(freqs)
    )
    full = jnp.float32
    (
        tokens_out, grad_in, grad_down, grad_gate, grad_up, grad_out, grad_query, grad_key, grad_value,
    ) = hand_over(
        results,
        [
            (tokens_in.shape, jnp.bfloat16),
            (tokens_in.shape, full),
            *[
                (weight.shape, full)
                for weight in (w_down, w_gate, w_up, w_out, w_query, w_key, w_value)
            ],
        ],
    )
    return (
        tokens_out,
        grad_in,
        grad_query,
        grad_key,
        grad_value,
        grad_out,
        grad_gate,
        grad_up,
        grad_down,
    )


def solution(mesh):
    in_specs = (
        P(None, "dp", "ctx", "mp"),
        P(None, "dp", "ctx", "mp"),
        P(None, "dp", "ctx"),
        P(("dp", "ctx"), "mp"),
        P(("dp", "ctx"), "mp"),
        P(("dp", "ctx"), "mp"),
        P("mp", ("dp", "ctx")),
        P(("dp", "ctx"), "mp"),
        P(("dp", "ctx"), "mp"),
        P("mp", ("dp", "ctx")),
    )
    out_specs = (
        P(None, "dp", "ctx", "mp"),
        P(None, "dp", "ctx", "mp"),
        P(("dp", "ctx"), "mp"),
        P(("dp", "ctx"), "mp"),
        P(("dp", "ctx"), "mp"),
        P("mp", ("dp", "ctx")),
        P(("dp", "ctx"), "mp"),
        P(("dp", "ctx"), "mp"),
        P("mp", ("dp", "ctx")),
    )
    grouped = mesh.shape["ctx"] == 4 and mesh.shape["mp"] == 4 and mesh.shape["dp"] == 2
    per_device = per_device_grouped if grouped else per_device_general
    return jax.shard_map(
        per_device, mesh=mesh, in_specs=in_specs, out_specs=out_specs, check_vma=False
    )
```

```python
import functools
import math
import types

import jax
import jax.numpy as jnp
import numpy as np
from jax import lax
from jax.experimental import pallas as pl
from jax.experimental.pallas import tpu as pltpu
from jax.sharding import PartitionSpec as P

HD = 128


EPSILON = 1e-05
NEG_FILL = -1e30


def layer_norm(values):
    centred = values - jnp.mean(values, axis=-1, keepdims=True)
    inverse = lax.rsqrt(jnp.mean(centred * centred, axis=-1, keepdims=True) + EPSILON)
    return (centred * inverse, inverse)


def norm_backward(upstream, normed, inverse):
    plain_mean = jnp.mean(upstream, axis=-1, keepdims=True)
    cross_mean = jnp.mean(upstream * normed, axis=-1, keepdims=True)
    return inverse * (upstream - plain_mean - normed * cross_mean)


def doc_positions(segment):
    length = segment.shape[-1]
    places = jnp.arange(length, dtype=jnp.int32)
    opening = jnp.ones(segment.shape[:-1] + (1,), dtype=bool)
    change = jnp.concatenate([opening, segment[..., 1:] != segment[..., :-1]], axis=-1)
    starts = lax.cummax(jnp.where(change, places, jnp.int32(0)), axis=segment.ndim - 1)
    return places - starts


def rope_angles(positions):
    freq_table = jnp.power(10000.0, -2.0 * jnp.arange(HD // 2, dtype=jnp.float32) / HD)
    turned = positions.astype(jnp.float32)[..., None] * freq_table
    return (jnp.cos(turned), jnp.sin(turned))


def rope_turn(values, cosine, sine_part):
    half_size = values.shape[-1] // 2
    leading = values[..., :half_size]
    trailing = values[..., half_size:]
    return jnp.concatenate(
        [leading * cosine - trailing * sine_part, trailing * cosine + leading * sine_part], axis=-1
    )


def dot_rows(left_mat, right_mat):
    return lax.dot_general(
        left_mat, right_mat, (((1,), (1,)), ((), ())), preferred_element_type=jnp.float32
    )


def dot_cols(left_mat, right_mat):
    return lax.dot_general(
        left_mat, right_mat, (((0,), (0,)), ((), ())), preferred_element_type=jnp.float32
    )


def fetch_weights(w_query, w_key, w_value, w_gate, w_up, w_out, w_down):
    return (
        lax.all_gather(w_query, ("dp", "ctx"), axis=0, tiled=True),
        lax.all_gather(w_key, ("dp", "ctx"), axis=0, tiled=True),
        lax.all_gather(w_value, ("dp", "ctx"), axis=0, tiled=True),
        lax.all_gather(w_gate, ("dp", "ctx"), axis=0, tiled=True),
        lax.all_gather(w_up, ("dp", "ctx"), axis=0, tiled=True),
        lax.all_gather(w_out, ("dp", "ctx"), axis=1, tiled=True),
        lax.all_gather(w_down, ("dp", "ctx"), axis=1, tiled=True),
    )


def per_device_general(
    tokens_in, out_grad, segment_ids, w_query, w_key, w_value, w_out, w_gate, w_up, w_down
):
    micro_count = tokens_in.shape[0]
    seq_local = tokens_in.shape[1]
    span_len = tokens_in.shape[2]
    local_width = tokens_in.shape[3]
    ctx_index = lax.axis_index("ctx")
    model_index = lax.axis_index("mp")
    tokens_all, grads_all = (
        lax.all_gather(tokens_in, "mp", axis=3, tiled=True),
        lax.all_gather(out_grad, "mp", axis=3, tiled=True),
    )
    segments_all = lax.all_gather(segment_ids, "ctx", axis=2, tiled=True)
    feature_width = tokens_all.shape[3]
    seq_length = segments_all.shape[2]
    row_count = seq_local * span_len
    score_scale = 1.0 / math.sqrt(HD)
    positions = doc_positions(segments_all)
    query_places = ctx_index * span_len + jnp.arange(span_len, dtype=jnp.int32)
    key_places = jnp.arange(seq_length, dtype=jnp.int32)
    causal = key_places[None, :] <= query_places[:, None]
    outputs = []
    input_grads = []
    totals = None
    for micro_step in range(micro_count):
        full_weights = fetch_weights(w_query, w_key, w_value, w_gate, w_up, w_out, w_down)
        query_full, key_full, value_full, gate_full, up_full, out_full, down_full = full_weights
        head_count = query_full.shape[1] // HD
        segment_seq = segments_all[micro_step]
        segment_own = lax.dynamic_slice_in_dim(segment_seq, ctx_index * span_len, span_len, 1)
        position_own = lax.dynamic_slice_in_dim(
            positions[micro_step], ctx_index * span_len, span_len, 1
        )
        allowed = (segment_own[:, :, None] == segment_seq[:, None, :]) & causal[None]
        cosine, sine_part = rope_angles(position_own)
        cosine = cosine[:, :, None, :]
        sine_part = sine_part[:, :, None, :]
        inputs = tokens_all[micro_step].astype(jnp.float32)
        normed, inverse_one = layer_norm(inputs)
        normed_low = normed.astype(jnp.bfloat16).reshape(row_count, feature_width)

        def project(matrix):
            product = jnp.dot(normed_low, matrix, preferred_element_type=jnp.float32)
            return product.reshape(seq_local, span_len, head_count, HD)

        query_low = (
            rope_turn(project(query_full), cosine, sine_part)
            .astype(jnp.bfloat16)
            .reshape(seq_local, span_len, head_count * HD)
        )
        key_low = (
            rope_turn(project(key_full), cosine, sine_part)
            .astype(jnp.bfloat16)
            .reshape(seq_local, span_len, head_count * HD)
        )
        value_low = (
            project(value_full).astype(jnp.bfloat16).reshape(seq_local, span_len, head_count * HD)
        )
        key_seq, value_seq = (
            lax.all_gather(key_low, "ctx", axis=1, tiled=True),
            lax.all_gather(value_low, "ctx", axis=1, tiled=True),
        )
        mixed_parts = []
        log_totals = []
        for head_index in range(head_count):
            head_cols = slice(head_index * HD, (head_index + 1) * HD)
            scores = (
                jnp.einsum(
                    "sqd,skd->sqk",
                    query_low[..., head_cols],
                    key_seq[..., head_cols],
                    preferred_element_type=jnp.float32,
                )
                * score_scale
            )
            scores = jnp.where(allowed, scores, NEG_FILL)
            highest = jnp.max(scores, axis=-1, keepdims=True)
            exp_terms = jnp.exp(scores - highest)
            total_exp = jnp.sum(exp_terms, axis=-1, keepdims=True)
            probs_low = (exp_terms / total_exp).astype(jnp.bfloat16)
            mixed_parts.append(
                jnp.einsum(
                    "sqk,skd->sqd",
                    probs_low,
                    value_seq[..., head_cols],
                    preferred_element_type=jnp.float32,
                )
            )
            log_totals.append(highest + jnp.log(total_exp))
        mixed_low = (
            jnp.concatenate(mixed_parts, axis=-1)
            .astype(jnp.bfloat16)
            .reshape(row_count, head_count * HD)
        )
        branch = jnp.dot(mixed_low, out_full, preferred_element_type=jnp.float32)
        branch = lax.psum(branch, "mp")
        residual = inputs + branch.reshape(seq_local, span_len, feature_width)
        normed_two, inverse_two = layer_norm(residual)
        second_low = normed_two.astype(jnp.bfloat16).reshape(row_count, feature_width)
        gate_lin = jnp.dot(second_low, gate_full, preferred_element_type=jnp.float32)
        up_lin = jnp.dot(second_low, up_full, preferred_element_type=jnp.float32)
        sigmoid_gate = jax.nn.sigmoid(gate_lin)
        hidden_low = (gate_lin * sigmoid_gate * up_lin).astype(jnp.bfloat16)
        feed_terms = jnp.dot(hidden_low, down_full, preferred_element_type=jnp.float32).reshape(
            seq_local, span_len, feature_width
        )
        feed_own = lax.psum_scatter(
            feed_terms.astype(jnp.bfloat16), "mp", scatter_dimension=2, tiled=True
        ).astype(jnp.float32)
        residual_own = lax.dynamic_slice_in_dim(residual, model_index * local_width, local_width, 2)
        outputs.append((residual_own + feed_own).astype(jnp.bfloat16))
        back_weights = (
            lax.all_gather(w_query, ("dp", "ctx"), axis=0, tiled=True),
            lax.all_gather(w_key, ("dp", "ctx"), axis=0, tiled=True),
            lax.all_gather(w_value, ("dp", "ctx"), axis=0, tiled=True),
            lax.all_gather(w_gate, ("dp", "ctx"), axis=0, tiled=True),
            lax.all_gather(w_up, ("dp", "ctx"), axis=0, tiled=True),
            lax.all_gather(w_out, ("dp", "ctx"), axis=1, tiled=True),
            lax.all_gather(w_down, ("dp", "ctx"), axis=1, tiled=True),
        )
        key_back, value_back = (
            lax.all_gather(key_low, "ctx", axis=1, tiled=True),
            lax.all_gather(value_low, "ctx", axis=1, tiled=True),
        )
        query_back, key_mat, value_mat, gate_back, up_back, out_back, down_back = back_weights
        grad_low = grads_all[micro_step].reshape(row_count, feature_width)
        grad_float = grads_all[micro_step].astype(jnp.float32)
        hidden_grad = dot_rows(grad_low, down_back)
        gate_grad = (
            hidden_grad * up_lin * sigmoid_gate * (1.0 + gate_lin * (1.0 - sigmoid_gate))
        ).astype(jnp.bfloat16)
        up_grad = (hidden_grad * gate_lin * sigmoid_gate).astype(jnp.bfloat16)
        normed_grad = dot_rows(gate_grad, gate_back) + dot_rows(up_grad, up_back)
        normed_grad = lax.psum(normed_grad, "mp").reshape(seq_local, span_len, feature_width)
        residual_grad = grad_float + norm_backward(normed_grad, normed_two, inverse_two)
        residual_low = residual_grad.astype(jnp.bfloat16).reshape(row_count, feature_width)
        mixed_grad = (
            dot_rows(residual_low, out_back)
            .astype(jnp.bfloat16)
            .reshape(seq_local, span_len, head_count * HD)
        )
        query_parts = []
        key_parts = []
        value_parts = []
        for head_index in range(head_count):
            head_cols = slice(head_index * HD, (head_index + 1) * HD)
            query_head = query_low[..., head_cols]
            key_head = key_back[..., head_cols]
            mixed_head = mixed_grad[..., head_cols]
            scores = (
                jnp.einsum("sqd,skd->sqk", query_head, key_head, preferred_element_type=jnp.float32)
                * score_scale
            )
            scores = jnp.where(allowed, scores, NEG_FILL)
            probs = jnp.exp(scores - log_totals[head_index])
            probs_low = probs.astype(jnp.bfloat16)
            value_parts.append(
                jnp.einsum(
                    "sqk,sqd->skd", probs_low, mixed_head, preferred_element_type=jnp.float32
                )
            )
            probs_grad = jnp.einsum(
                "sqd,skd->sqk",
                mixed_head,
                value_back[..., head_cols],
                preferred_element_type=jnp.float32,
            )
            row_dot = jnp.sum(probs * probs_grad, axis=-1, keepdims=True)
            scores_grad = (probs * (probs_grad - row_dot)).astype(jnp.bfloat16)
            query_parts.append(
                jnp.einsum(
                    "sqk,skd->sqd", scores_grad, key_head, preferred_element_type=jnp.float32
                )
                * score_scale
            )
            key_parts.append(
                jnp.einsum(
                    "sqk,sqd->skd", scores_grad, query_head, preferred_element_type=jnp.float32
                )
                * score_scale
            )
        key_terms = jnp.concatenate(key_parts, axis=-1)
        value_terms = jnp.concatenate(value_parts, axis=-1)
        key_grad_own, value_grad_own = (
            lax.psum_scatter(key_terms, "ctx", scatter_dimension=1, tiled=True),
            lax.psum_scatter(value_terms, "ctx", scatter_dimension=1, tiled=True),
        )
        query_sum = jnp.concatenate(query_parts, axis=-1).reshape(
            seq_local, span_len, head_count, HD
        )
        query_grad = (
            rope_turn(query_sum, cosine, -sine_part)
            .astype(jnp.bfloat16)
            .reshape(row_count, head_count * HD)
        )
        key_grad = (
            rope_turn(key_grad_own.reshape(seq_local, span_len, head_count, HD), cosine, -sine_part)
            .astype(jnp.bfloat16)
            .reshape(row_count, head_count * HD)
        )
        value_grad = value_grad_own.astype(jnp.bfloat16).reshape(row_count, head_count * HD)
        input_terms = (
            dot_rows(query_grad, query_back)
            + dot_rows(key_grad, key_mat)
            + dot_rows(value_grad, value_mat)
        )
        input_sum = (
            lax.psum(input_terms.astype(jnp.bfloat16), "mp")
            .astype(jnp.float32)
            .reshape(seq_local, span_len, feature_width)
        )
        grad_whole = residual_grad + norm_backward(input_sum, normed, inverse_one)
        input_grads.append(
            lax.dynamic_slice_in_dim(grad_whole, model_index * local_width, local_width, 2)
        )
        new_terms = (
            dot_cols(normed_low, query_grad),
            dot_cols(normed_low, key_grad),
            dot_cols(normed_low, value_grad),
            dot_cols(second_low, gate_grad),
            dot_cols(second_low, up_grad),
            dot_cols(mixed_low, residual_low),
            dot_cols(hidden_low, grad_low),
        )
        if totals is None:
            totals = new_terms
        else:
            totals = tuple((older + newer for older, newer in zip(totals, new_terms)))
    grads_total = (
        lax.psum_scatter(
            totals[0].astype(jnp.bfloat16), ("dp", "ctx"), scatter_dimension=0, tiled=True
        ).astype(jnp.float32),
        lax.psum_scatter(
            totals[1].astype(jnp.bfloat16), ("dp", "ctx"), scatter_dimension=0, tiled=True
        ).astype(jnp.float32),
        lax.psum_scatter(
            totals[2].astype(jnp.bfloat16), ("dp", "ctx"), scatter_dimension=0, tiled=True
        ).astype(jnp.float32),
        lax.psum_scatter(
            totals[3].astype(jnp.bfloat16), ("dp", "ctx"), scatter_dimension=0, tiled=True
        ).astype(jnp.float32),
        lax.psum_scatter(
            totals[4].astype(jnp.bfloat16), ("dp", "ctx"), scatter_dimension=0, tiled=True
        ).astype(jnp.float32),
        lax.psum_scatter(
            totals[5].astype(jnp.bfloat16), ("dp", "ctx"), scatter_dimension=1, tiled=True
        ).astype(jnp.float32),
        lax.psum_scatter(
            totals[6].astype(jnp.bfloat16), ("dp", "ctx"), scatter_dimension=1, tiled=True
        ).astype(jnp.float32),
    )
    return (
        jnp.stack(outputs, axis=0),
        jnp.stack(input_grads, axis=0),
        grads_total[0],
        grads_total[1],
        grads_total[2],
        grads_total[5],
        grads_total[3],
        grads_total[4],
        grads_total[6],
    )


MESH = pl.DeviceIdType.MESH
HBM = pl.BlockSpec(memory_space=pl.ANY)
LOW = jnp.bfloat16
FULL = jnp.float32
TILE = 256
PIECES = 4
VMEM_BYTES = 63 * 1024 * 1024


def contract(left, right, left_dim, right_dim):
    return lax.dot_general(
        left, right, (((left_dim,), (right_dim,)), ((), ())), preferred_element_type=FULL
    )


def aligned(start, size, unit=None):
    return pl.ds(pl.multiple_of(start, size if unit is None else unit), size)


class Place:
    def __init__(self):
        self.dp = lax.axis_index("dp")
        self.ctx = lax.axis_index("ctx")
        self.mp = lax.axis_index("mp")
        self.high = self.ctx // 2
        self.low = self.ctx % 2
        self.chip = self.mp // 2
        self.core = self.mp % 2
        self.home = self.dp * 4 + self.ctx
        self.inner = self.high != self.low

    def along(self, mask):
        other = self.ctx + mask - 2 * (self.ctx & mask)
        return (self.dp, other, self.mp)

    def across(self):
        return (1 - self.dp, self.ctx, self.mp)

    def beside_chip(self):
        return (self.dp, self.ctx, (1 - self.chip) * 2 + self.core)

    def beside_core(self):
        return (self.dp, self.ctx, self.chip * 2 + 1 - self.core)

    def shard_rows(self, low, chip, core, size=128):
        return aligned((core * 4 + chip * 2 + low) * 128, size, 128)


class Mover:
    def __init__(self, send, receive, local):
        self.send, self.receive, self.local = send, receive, local
        self.remote_count = 0
        self.local_count = 0

    def to(self, source, target, device):
        slot = self.remote_count
        self.remote_count += 1
        copy = pltpu.make_async_remote_copy(
            src_ref=source,
            dst_ref=target,
            send_sem=self.send.at[slot],
            recv_sem=self.receive.at[slot],
            device_id=device,
            device_id_type=MESH,
        )
        copy.start()
        return copy

    def hold(self, source, target, device, receive_slot=None):
        slot = self.remote_count
        self.remote_count += 1
        copy = pltpu.make_async_remote_copy(
            src_ref=source,
            dst_ref=target,
            send_sem=self.send.at[slot],
            recv_sem=self.receive.at[slot if receive_slot is None else receive_slot],
            device_id=device,
            device_id_type=MESH,
        )
        return HeldCopy(copy, slot)

    def here(self, source, target):
        slot = self.local_count
        self.local_count += 1
        copy = pltpu.make_async_copy(source, target, self.local.at[slot])
        copy.start()
        return copy


class HeldCopy:
    def __init__(self, copy, slot):
        self.copy, self.slot = copy, slot

    def start_if(self, wanted):
        @pl.when(wanted)
        def _():
            self.copy.start()

    def wait_send_if(self, wanted):
        @pl.when(wanted)
        def _():
            self.copy.wait_send()

    def wait_recv(self):
        self.copy.wait_recv()


def greet(partners):
    barrier = pltpu.get_barrier_semaphore()
    for partner in partners:
        pl.semaphore_signal(barrier, inc=1, device_id=partner, device_id_type=MESH)
    pl.semaphore_wait(barrier, len(partners))


class GroupGather:
    def __init__(self, place, mover, view, own):
        self.place, self.mover, self.view = place, mover, view
        p = place
        landing = view(p.low, p.chip, p.core)
        self.along = mover.to(own, landing, p.along(1))
        self.chip = mover.to(own, landing, p.beside_chip())
        self.core = mover.to(own, landing, p.beside_core())
        self.sent = [self.along, self.chip, self.core]

    def relay_along(self):
        p = self.place
        self.along.wait_recv()
        piece = self.view(1 - p.low, p.chip, p.core)
        self.corner = self.mover.to(piece, piece, p.beside_chip())
        self.along_core = self.mover.to(piece, piece, p.beside_core())
        self.sent += [self.corner, self.along_core]

    def relay_chip(self):
        p = self.place
        self.chip.wait_recv()
        piece = self.view(p.low, 1 - p.chip, p.core)
        self.chip_core = self.mover.to(piece, piece, p.beside_core())
        self.sent.append(self.chip_core)

    def relay_corner(self):
        p = self.place
        self.corner.wait_recv()
        piece = self.view(1 - p.low, 1 - p.chip, p.core)
        self.corner_core = self.mover.to(piece, piece, p.beside_core())
        self.sent.append(self.corner_core)

    def finish(self):
        for copy in (self.core, self.along_core, self.chip_core, self.corner_core):
            copy.wait_recv()
        for copy in self.sent:
            copy.wait_send()


class GroupScatter:
    def __init__(self, place, mover, buffers, terms):
        self.place, self.mover, self.buffers, self.terms = place, mover, buffers, terms
        self.sent = []

    def half(self, part):
        return pl.ds(part * TILE, TILE)

    def rows(self, chip, core):
        return self.place.shard_rows(0, chip, core, TILE)

    def start_core(self, part):
        p = self.place
        core_send, core_recv = self.buffers[:2]
        chip = 1 - p.chip if part == 0 else p.chip
        core_send[self.half(part), :] = self.terms(self.rows(chip, 1 - p.core)).astype(LOW)
        copy = self.mover.to(
            core_send.at[self.half(part)], core_recv.at[self.half(part)], p.beside_core()
        )
        self.sent.append(copy)
        if part == 0:
            self.core_first = copy
        else:
            self.core_second = copy

    def start_chip(self):
        p = self.place
        core_recv, chip_send, chip_recv = self.buffers[1:4]
        total = self.terms(self.rows(1 - p.chip, p.core))
        self.core_first.wait_recv()
        chip_send[...] = (total + core_recv[self.half(0), :].astype(FULL)).astype(LOW)
        self.chip_copies = []
        for which in (1 - p.low, p.low):
            rows = aligned(which * 128, 128)
            self.chip_copies.append(
                self.mover.to(chip_send.at[rows], chip_recv.at[rows], p.beside_chip())
            )
        self.sent += self.chip_copies

    def start_along(self):
        p = self.place
        core_recv, _, chip_recv, along_send, along_recv, total_ref = self.buffers[1:]
        total = self.terms(self.rows(p.chip, p.core))
        self.core_second.wait_recv()
        total_ref[...] = total + core_recv[self.half(1), :].astype(FULL)
        self.chip_copies[0].wait_recv()
        rows = aligned((1 - p.low) * 128, 128)
        along_send[...] = (total_ref[rows, :] + chip_recv[rows, :].astype(FULL)).astype(LOW)
        self.along = self.mover.to(along_send, along_recv, p.along(1))
        self.sent.append(self.along)

    def result(self):
        p = self.place
        chip_recv, _, along_recv, total_ref = self.buffers[3:]
        self.chip_copies[1].wait_recv()
        rows = aligned(p.low * 128, 128)
        total = total_ref[rows, :] + chip_recv[rows, :].astype(FULL)
        self.along.wait_recv()
        total = total + along_recv[...].astype(FULL)
        for copy in self.sent:
            copy.wait_send()
        return total


def scatter_buffers(width):
    return [
        pltpu.VMEM((2 * TILE, width), LOW),
        pltpu.VMEM((2 * TILE, width), LOW),
        pltpu.VMEM((TILE, width), LOW),
        pltpu.VMEM((TILE, width), LOW),
        pltpu.VMEM((TILE // 2, width), LOW),
        pltpu.VMEM((TILE // 2, width), LOW),
        pltpu.VMEM((TILE, width), FULL),
    ]


class WeightFetch:
    def __init__(self, place, mover, shard, whole, axis, start, size, landing):
        self.place, self.mover = place, mover
        half = shard.shape[axis] // 2
        block = shard.shape[1 - axis]

        def source(which):
            part = aligned(which * half + start, size, 128)
            return shard.at[:, part] if axis == 1 else shard.at[part, :]

        def target(ctx):
            span = aligned((place.dp * 4 + ctx) * block, block, 128)
            part = pl.ds(landing, size)
            return whole.at[span, part] if axis == 1 else whole.at[part, span]

        self.source, self.target = source, target

    def start(self):
        p = self.place
        mine = self.source(p.low)
        other = self.source(1 - p.low)
        spot = self.target(p.ctx)
        self.beside = self.mover.to(other, spot, p.along(1))
        self.corner = self.mover.hold(other, spot, p.along(3))
        self.corner.start_if(p.inner)
        self.ahead = self.mover.to(mine, spot, p.along(2))
        self.far = []

    def start_own(self):
        p = self.place
        mine, spot = self.source(p.low), self.target(p.ctx)
        self.own_far = self.mover.to(mine, spot, p.across())

    def send_across(self, mask):
        p = self.place
        block = self.target(p.along(mask)[1])
        self.far.append(self.mover.to(block, block, p.across()))

    def forward(self):
        p = self.place
        self.beside.wait_recv()
        block = self.target(p.along(1)[1])
        self.passed = self.mover.hold(block, block, p.along(2), self.corner.slot)
        self.passed.start_if(p.inner)
        self.send_across(1)

    def cross(self):
        self.ahead.wait_recv()
        self.send_across(2)
        self.corner.wait_recv()
        self.send_across(3)

    def finish(self):
        for copy in self.far + [self.own_far]:
            copy.wait_recv()

    def drain(self):
        for copy in self.far + [self.own_far, self.beside, self.ahead]:
            copy.wait_send()
        for copy in (self.corner, self.passed):
            copy.wait_send_if(self.place.inner)


def normalise(values):
    centred = values - jnp.mean(values, axis=-1, keepdims=True)
    inverse = lax.rsqrt(jnp.mean(centred * centred, axis=-1, keepdims=True) + EPSILON)
    return centred * inverse, inverse


def allowed_mask(seg_col, seg_row, start, keys):
    rows = seg_col[pl.ds(start, TILE), :][:, :1]
    cols = seg_row[0:1, pl.ds(0, keys)]
    row_place = start + lax.broadcasted_iota(jnp.int32, (TILE, keys), 0)
    col_place = lax.broadcasted_iota(jnp.int32, (TILE, keys), 1)
    return (rows == cols) & (col_place <= row_place)


def turn(values, cosine, sine_part):
    parts = []
    for start in range(0, values.shape[1], HD):
        head = values[:, start : start + HD]
        parts.append(head * cosine + pltpu.roll(head, HD // 2, 1) * sine_part)
    return jnp.concatenate(parts, axis=1)


class Staging:
    def __init__(self):
        self.last = None

    def free(self):
        if self.last is not None:
            self.last.wait()
            self.last = None


class GradReturn:
    def __init__(self, place, mover, axis, terms, sends, receives, loads, stage, own_out, before=None):
        self.place, self.mover, self.axis, self.terms = place, mover, axis, terms
        self.across_send, self.along_send, self.beside_send = sends
        self.across_recv, self.along_recv, self.beside_recv = receives
        self.loads, (self.stage, self.stage_ref), self.own_out = loads, stage, own_out
        self.before = before
        self.blocks = [place.along(3)[1], place.along(2)[1], place.along(1)[1], place.ctx]
        self.size = own_out.shape[0]
        self.arriving, self.leaving, self.here = {}, {}, set()

    def send(self, key, source, target, device):
        copy = self.mover.to(source, target, device)
        self.arriving[key] = self.leaving[key] = copy

    def arrived(self, key):
        if key not in self.here:
            self.here.add(key)
            self.arriving[key].wait_recv()

    def free(self, key):
        if self.before is not None:
            self.before.leaving.pop(key).wait_send()

    def part(self, half):
        count = self.size // 2
        return pl.ds(0, self.size) if half is None else pl.ds(half * count, count)

    def across(self, step):
        p = self.place
        value = self.terms((1 - p.dp) * 4 + self.blocks[step], self.part(None)).astype(LOW)
        self.free((0, step))
        self.across_send[step] = value
        self.send((0, step), self.across_send.at[step], self.across_recv.at[step], p.across())

    def summed(self, step, half, others):
        part = self.part(half)
        self.arrived((0, step))
        copies = [
            self.mover.here(self.across_recv.at[step, part, :], self.loads.at[0, part, :])
        ]
        for along_half in others:
            self.arrived((1, step - 2, along_half))
            spot = self.part(along_half)
            copies.append(
                self.mover.here(self.along_recv.at[step - 2, spot, :], self.loads.at[1, spot, :])
            )
        value = self.terms(self.place.dp * 4 + self.blocks[step], part)
        for copy in copies:
            copy.wait()
        value = value + self.loads[0, part, :].astype(FULL)
        if others:
            value = value + self.loads[1, part, :].astype(FULL)
        return value

    def along(self, step, half):
        part = self.part(half)
        value = self.summed(step, half, ()).astype(LOW)
        self.free((1, step, half))
        self.along_send[step, part, :] = value
        source = self.along_send.at[step, part, :]
        target = self.along_recv.at[step, part, :]
        self.send((1, step, half), source, target, self.place.along(2))

    def beside(self, half):
        part = self.part(half)
        value = self.summed(2, half, (half,)).astype(LOW)
        self.free((2, half))
        self.beside_send[part, :] = value
        source, target = self.beside_send.at[part, :], self.beside_recv.at[part, :]
        self.send((2, half), source, target, self.place.along(1))

    def own(self):
        value = self.summed(3, None, (0, 1))
        self.stage.free()
        self.stage_ref[...] = value
        self.stage.last = self.mover.here(self.stage_ref, self.own_out)

    def drain(self):
        for half in range(2):
            self.arrived((2, half))
        for copy in self.leaving.values():
            copy.wait_send()


def give_credit(place, credit):
    for slot, partner in enumerate((place.beside_core(), place.beside_chip(), place.along(1))):
        pl.semaphore_signal(credit.at[slot], inc=1, device_id=partner, device_id_type=MESH)


def block_cols(ref, block):
    return ref[:, aligned(block * TILE, TILE)]


class RowReturn:
    def __init__(self, place, send, receive, local):
        self.place, self.send, self.receive, self.local = place, send, receive, local
        self.goal = place.core * 2 + place.chip
        self.stays = place.ctx == self.goal

    def partners(self):
        p = self.place
        targets = [(p.dp, self.goal, model) for model in range(4)]
        sources = [(p.dp, ctx, p.low * 2 + p.high) for ctx in range(4)]
        return targets, sources

    def greet(self, others):
        p = self.place
        barrier = pltpu.get_barrier_semaphore()
        for other in others:
            pl.semaphore_signal(barrier, inc=1, device_id=other, device_id_type=MESH)
        targets, sources = self.partners()
        for model, target in enumerate(targets):

            @pl.when(jnp.logical_not(self.stays & (p.mp == model)))
            def _(target=target):
                pl.semaphore_signal(barrier, inc=1, device_id=target, device_id_type=MESH)

        for ctx, source in enumerate(sources):

            @pl.when(jnp.logical_not(self.stays & (p.ctx == ctx)))
            def _(source=source):
                pl.semaphore_signal(barrier, inc=1, device_id=source, device_id_type=MESH)

        @pl.when(self.stays)
        def _():
            pl.semaphore_wait(barrier, len(others) + 6)

        @pl.when(jnp.logical_not(self.stays))
        def _():
            pl.semaphore_wait(barrier, len(others) + 8)

    def copy(self, model):
        size = self.rows.shape[1] // 4
        return pltpu.make_async_remote_copy(
            src_ref=self.rows.at[:, pl.ds(model * size, size)],
            dst_ref=self.landing,
            send_sem=self.send.at[model],
            recv_sem=self.receive.at[self.place.ctx],
            device_id=(self.place.dp, self.goal, model),
            device_id_type=MESH,
        )

    def own_copy(self):
        size = self.rows.shape[1] // 4
        source = self.rows.at[:, aligned(self.place.mp * size, size)]
        return pltpu.make_async_copy(source, self.landing, self.local)

    def start(self, rows, whole):
        p = self.place
        self.rows, self.whole = rows, whole
        count = rows.shape[0]
        self.landing = whole.at[p.high, 0, aligned(p.low * count, count), :]
        for model in range(4):

            @pl.when(jnp.logical_not(self.stays & (p.mp == model)))
            def _(model=model):
                self.copy(model).start()

        @pl.when(self.stays)
        def _():
            self.own_copy().start()

    def finish(self):
        p = self.place
        for model in range(4):

            @pl.when(jnp.logical_not(self.stays & (p.mp == model)))
            def _(model=model):
                self.copy(model).wait_send()

        for ctx in range(4):

            @pl.when(jnp.logical_not(self.stays & (p.ctx == ctx)))
            def _(ctx=ctx):
                count = self.rows.shape[0]
                spot = self.whole.at[ctx // 2, 0, pl.ds((ctx % 2) * count, count), :]
                pltpu.make_async_remote_copy(
                    src_ref=spot,
                    dst_ref=spot,
                    send_sem=self.send.at[0],
                    recv_sem=self.receive.at[ctx],
                    device_id=(p.dp, ctx, p.low * 2 + p.high),
                    device_id_type=MESH,
                ).wait_recv()

        @pl.when(self.stays)
        def _():
            self.own_copy().wait()


ORDER = (
    64, 33, 5, 0, 8, 65, 9, 2, 1, 3, 44, 10, 4, 69, 66, 11, 45, 13, 53, 21,
    75, 46, 12, 67, 25, 47, 6, 40, 72, 70, 68, 32, 7, 77, 76, 71, 73, 42, 14, 49,
    20, 15, 28, 17, 29, 79, 61, 74, 86, 41, 43, 84, 85, 83, 103, 16, 37, 36, 78, 87,
    88, 89, 90, 80, 22, 30, 34, 81, 31, 18, 38, 23, 104, 24, 82, 57, 19, 35, 106, 60,
    105, 111, 26, 48, 39, 27, 62, 107, 109, 50, 56, 108, 110, 63, 112, 52, 51, 113, 114, 58,
    115, 175, 120, 59, 54, 119, 55, 124, 116, 121, 125, 118, 122, 117, 91, 92, 93, 127, 131, 126,
    94, 132, 135, 136, 142, 143, 134, 128, 176, 146, 147, 95, 133, 138, 96, 97, 145, 123, 137, 177,
    144, 98, 180, 140, 179, 139, 178, 183, 185, 154, 189, 149, 148, 188, 130, 184, 156, 141, 129, 181,
    187, 186, 190, 99, 182, 164, 151, 100, 165, 153, 150, 170, 169, 157, 101, 166, 168, 159, 155, 102,
    173, 172, 158, 160, 171, 191, 167, 163, 161, 152, 162, 174, 192,
)


def run_steps(steps, order):
    for place in order:
        steps[place]()


def layer_kernel(
    tokens_in, out_grad, w_query, w_key, w_value, w_out, w_gate, w_up, w_down,
    segment, freqs,
    tokens_out, grad_rows, down_own, down_near, gate_own, gate_near, up_own, up_near, out_own, out_near, three_own, three_near,
    qkv_all, grads_all, normed_all, back_all,
    query_all, key_all, value_all, mixed_all,
    gate_far, gate_mid, up_far, up_mid, down_far, down_mid, three_far, three_mid, out_far, out_mid,
    second, grads, gate_here, up_here, down_here, pair, up_back, out_here, key_sum, value_sum,
    wide_far, wide_mid, wide_near, wide_loads, wide_stage, tall_far, tall_mid, tall_near, tall_loads, tall_stage,
    core_send, core_recv, chip_send, chip_recv, along_send, along_recv, total_ref, rows_low, back_rows,
    residual, inverse_two, log_total, cosine, sine_part, seg_col, seg_row, seg_mine, kept,
    credit, send, receive, local, feed_send, feed_receive, feed_local, row_send, row_receive, row_local,
):
    p = Place()
    mover = Mover(send, receive, local)
    feed_return = RowReturn(p, feed_send, feed_receive, feed_local)
    row_return = RowReturn(p, row_send, row_receive, row_local)
    row_return.greet(
        [p.along(1), p.along(2), p.along(3), p.across(), p.beside_chip(), p.beside_core()]
    )
    hidden, gate_back = pair.at[0], pair.at[1]
    length = grads.shape[0]
    units = hidden.shape[1]
    span, feats = tokens_in.shape[2:]
    cols = out_here.shape[0]
    head_count = cols // HD
    blocks = length // TILE
    score_scale = 1.0 / math.sqrt(HD)
    tokens = grads
    first, later = pl.ds(0, length), pl.ds(length, length)
    query, key, value, mixed = [up_here.at[first, pl.ds(slot * cols, cols)] for slot in range(4)]
    three_back = up_here.at[later, pl.ds(0, 3 * cols)]
    mixed_back = up_here.at[later, pl.ds(3 * cols, cols)]
    qkv_here = gate_here.at[:, pl.ds(0, 3 * cols)]
    qkv_early = pair.at[:, :, pl.ds(0, 3 * cols)]
    attended = ((query, query_all), (key, key_all), (value, value_all), (mixed, mixed_all))
    early = [up_back.at[:, pl.ds(slot * cols, cols)] for slot in range(4)]
    query_early, key_early, value_early, mixed_early = early
    my_rows = p.shard_rows(p.low, p.chip, p.core)
    steps = []
    step = steps.append
    made = types.SimpleNamespace()

    def block_of(whole, ctx, model):
        return whole.at[aligned(ctx * span, span), aligned(model * feats, feats)]

    def own_view(whole):
        return lambda low, chip, core: block_of(whole, p.high * 2 + low, chip * 2 + core)

    def other_view(whole):
        return lambda low, chip, core: block_of(whole, (1 - p.high) * 2 + low, chip * 2 + core)

    def row_view(whole):
        return lambda low, chip, core: whole.at[p.shard_rows(low, chip, core)]

    def relays(gather):
        step(lambda: gather().relay_along())
        step(lambda: gather().relay_chip())
        step(lambda: gather().relay_corner())

    def fetch(shard, whole, axis, landing=0, pieces=1):
        size = shard.shape[axis] // 2 // pieces
        for piece in range(pieces):
            chunk = WeightFetch(
                p, mover, shard, whole, axis, piece * size, size, landing + piece * size
            )
            chunks.append(chunk)
            for action in (chunk.start, chunk.start_own, chunk.forward, chunk.cross):
                step(action)

    chunks = []
    fetch(w_query, qkv_all, 1, 0)
    fetch(w_key, qkv_all, 1, cols)
    fetch(w_value, qkv_all, 1, 2 * cols)
    fetch(w_out, out_here, 0)
    fetch(w_gate, gate_here, 1, 0, PIECES)
    fetch(w_up, up_here, 1, 0, PIECES)
    fetch(w_down, down_here, 0, 0, PIECES)
    of_gate, of_up, of_down = [chunks[4 + slot * PIECES :][:PIECES] for slot in range(3)]

    @step
    def _():
        spot = aligned(p.home * TILE, TILE)
        made.own_blocks = []
        for shard, whole in ((w_out, out_here), (w_down, down_here)):
            half = shard.shape[0] // 2
            source = shard.at[aligned(p.low * half, half), :]
            made.own_blocks.append(mover.here(source, whole.at[:, spot]))
        for shard, whole in ((w_gate, gate_here), (w_up, up_here)):
            half = shard.shape[1] // 2
            source = shard.at[:, aligned(p.low * half, half)]
            made.own_blocks.append(mover.here(source, whole.at[spot, :]))
        made.seg = []
        for which in range(2):
            numbers = segment[which].astype(FULL)
            seg_mine[which] = jnp.broadcast_to(numbers, seg_mine.shape[1:])
        spot = aligned(p.ctx * span, span)
        for mask in (1, 2, 3):
            goal = p.high if mask == 1 else 1 - p.high
            made.seg.append(
                mover.to(seg_mine.at[goal], seg_row.at[:, spot], p.along(mask))
            )
        made.seg.append(mover.here(seg_mine.at[p.high], seg_row.at[:, spot]))
        here = block_of(tokens, p.ctx, p.mp)
        made.swap = mover.to(tokens_in.at[1 - p.high, 0], here, p.along(2))
        own_tokens = tokens_in.at[p.high, 0]
        made.tokens = mover.here(own_tokens, here)
        made.own = GroupGather(p, mover, own_view(tokens), own_tokens)

    @step
    def _():
        made.swap.wait_recv()
        theirs = block_of(tokens, p.along(2)[1], p.mp)
        made.other = GroupGather(p, mover, other_view(tokens), theirs)

    relays(lambda: made.own)
    relays(lambda: made.other)

    @step
    def _():
        for copy in made.seg:
            copy.wait()
        for begin in range(0, length, TILE):
            rows = pl.ds(begin, TILE)
            numbers = jnp.broadcast_to(seg_row[0:1, rows], (HD, TILE))
            seg_col[rows, :] = numbers.T
            allowed = allowed_mask(seg_col, seg_row, begin, begin + TILE)
            position = jnp.sum(jnp.where(allowed, 1.0, 0.0), axis=1, keepdims=True) - 1.0
            angle = position * freqs[0:1, :]
            cosine[rows, :] = jnp.cos(angle)
            lane = lax.broadcasted_iota(jnp.int32, (TILE, HD), 1)
            sine = jnp.sin(angle)
            sine_part[rows, :] = jnp.where(lane < HD // 2, -sine, sine)

    @step
    def _():
        made.tokens.wait()
        made.swap.wait_send()
        made.own.finish()
        made.other.finish()
        kept[...] = tokens[my_rows, :]
        residual[...] = kept[...].astype(FULL)
        for begin in range(0, length, 128):
            rows = pl.ds(begin, 128)
            tokens[rows, :] = normalise(tokens[rows, :].astype(FULL))[0].astype(LOW)
        made.normed = mover.here(tokens, normed_all)

    def load_three(cut):
        copies = []
        for turn_by in range(1, 8):
            block = lax.rem(p.home + turn_by, 8)
            source = qkv_all.at[aligned(block * TILE, TILE), :]
            copies.append(mover.here(source, cut(block)))
        for slot, shard in enumerate((w_query, w_key, w_value)):
            source = shard.at[:, aligned(p.low * cols, cols)]
            target = cut(p.home).at[:, pl.ds(slot * cols, cols)]
            copies.append(mover.here(source, target))
        return copies

    def wait_all(copies):
        for copy in copies:
            copy.wait()

    @step
    def _():
        for chunk in chunks[:3]:
            chunk.finish()
        wait_all(
            load_three(
                lambda block: qkv_early.at[block // 4, aligned(lax.rem(block, 4) * TILE, TILE), :]
            )
        )
        for begin in range(0, length, TILE):
            rows = pl.ds(begin, TILE)
            three = contract(tokens[rows, pl.ds(0, units)], qkv_early[0], 1, 0) + contract(
                tokens[rows, pl.ds(units, units)], qkv_early[1], 1, 0
            )
            turned = [
                turn(three[:, start : start + cols], cosine[rows, :], sine_part[rows, :])
                for start in (0, cols)
            ]
            query_early[rows, :] = turned[0].astype(LOW)
            key_early[rows, :] = turned[1].astype(LOW)
            value_early[rows, :] = three[:, 2 * cols :].astype(LOW)

    @step
    def _():
        spot = block_of(grads_all, p.ctx, p.mp)
        own = out_grad.at[p.high, 0]
        made.cot_swap = mover.to(out_grad.at[1 - p.high, 0], spot, p.along(2))
        made.cot_own = GroupGather(p, mover, own_view(grads_all), own)

    @step
    def _():
        made.cot_swap.wait_recv()
        theirs = block_of(grads_all, p.along(2)[1], p.mp)
        made.cot_other = GroupGather(p, mover, other_view(grads_all), theirs)

    relays(lambda: made.cot_own)
    relays(lambda: made.cot_other)

    def attend(begin):
        rows = pl.ds(begin, TILE)
        keys = begin + TILE
        allowed = allowed_mask(seg_col, seg_row, begin, keys)
        for head in range(head_count):
            head_cols = pl.ds(head * HD, HD)
            scores = contract(query_early[rows, head_cols], key_early[pl.ds(0, keys), head_cols], 1, 1)
            scores = jnp.where(allowed, scores * score_scale, NEG_FILL)
            highest = jnp.max(scores, axis=-1, keepdims=True)
            exp_terms = jnp.exp(scores - highest)
            total_exp = jnp.sum(exp_terms, axis=-1, keepdims=True)
            probs_low = (exp_terms * (1.0 / total_exp)).astype(LOW)
            mixed_early[rows, head_cols] = contract(
                probs_low, value_early[pl.ds(0, keys), head_cols], 1, 0
            ).astype(LOW)
            log_total[rows, head_cols] = jnp.broadcast_to(
                highest + jnp.log(total_exp), (TILE, HD)
            )

    for block in range(blocks):
        step(functools.partial(attend, block * TILE))

    buffers = (core_send, core_recv, chip_send, chip_recv, along_send, along_recv, total_ref)

    def scatter_steps(terms, waits=True):
        scatter = GroupScatter(p, mover, buffers, terms)

        def stage(action, slot, part=None):
            def run():
                if waits and part != 1:
                    pl.semaphore_wait(credit.at[slot], 1)
                action() if part is None else action(part)

            return run

        step(stage(scatter.start_core, 0, 0))
        step(stage(scatter.start_core, 0, 1))
        step(stage(scatter.start_chip, 1))
        step(stage(scatter.start_along, 2))
        return scatter

    branch_sum = scatter_steps( lambda rows: contract(mixed_early[rows, :], out_here[...], 1, 0), False
    )
    back_sum = scatter_steps(
        lambda rows: contract(gate_back[rows, :], gate_here[...], 1, 1)
        + contract(up_back[rows, :], up_here[...], 1, 1),
    )
    feed_sum = scatter_steps( lambda rows: contract(hidden[rows, :], down_here[...], 1, 0)
    )
    input_sum = scatter_steps( lambda rows: contract(three_back[rows, :], qkv_here[...], 1, 1)
    )

    @step
    def _():
        chunks[3].finish()
        made.own_blocks[0].wait()
        made.saves = [mover.here(source, target) for source, (_, target) in zip(early, attended)]

    @step
    def _():
        branch = branch_sum.result()
        give_credit(p, credit)
        hidden_rows = residual[...] + branch
        residual[...] = hidden_rows
        normed_two, inverse = normalise(hidden_rows)
        inverse_two[...] = jnp.broadcast_to(inverse, inverse_two.shape)
        rows_low[...] = normed_two.astype(LOW)
        view = row_view(second)
        made.second_local = mover.here(rows_low, view(p.low, p.chip, p.core))
        made.second = GroupGather(p, mover, view, rows_low)

    relays(lambda: made.second)

    @step
    def _():
        for chunk in of_gate:
            chunk.finish()
        made.own_blocks[2].wait()

    @step
    def _():
        for copy in made.saves:
            copy.wait()
        for chunk in of_up:
            chunk.finish()
        made.own_blocks[3].wait()

    @step
    def _():
        made.second.finish()
        made.second_local.wait()

    @step
    def _():
        made.cot_own.finish()
        made.cot_other.finish()
        made.cot_swap.wait_send()
        made.normed.wait()
        made.cot_load = [mover.here(out_grad.at[p.high, 0], block_of(grads, p.ctx, p.mp))]
        for turn_by in range(1, 16):
            which = lax.rem(p.ctx * 4 + p.mp + turn_by, 16)
            made.cot_load.append(
                mover.here(
                    block_of(grads_all, which // 4, lax.rem(which, 4)),
                    block_of(grads, which // 4, lax.rem(which, 4)),
                )
            )

    def hidden_block(block):
        rows = pl.ds(block * TILE, TILE)
        for begin in range(0, units, TILE):
            part = pl.ds(begin, TILE)
            gate = contract(second[rows, :], gate_here[:, part], 1, 0)
            up = contract(second[rows, :], up_here[:, part], 1, 0)
            share = jax.nn.sigmoid(gate)
            silu = gate * share
            hidden[rows, part] = (silu * up).astype(LOW)
            gate_back[rows, part] = (up * share * (1.0 + gate * (1.0 - share))).astype(LOW)
            up_back[rows, part] = silu.astype(LOW)

    for block in range(blocks):
        step(functools.partial(hidden_block, block))

    def back_block(begin, index):
        rows, part = pl.ds(index * TILE, TILE), pl.ds(begin, TILE)
        back = contract(grads[rows, :], down_here[part, :], 1, 1)
        gate_back[rows, part] = (back * gate_back[rows, part].astype(FULL)).astype(LOW)
        up_back[rows, part] = (back * up_back[rows, part].astype(FULL)).astype(LOW)

    waited = set()

    def back_piece(which):
        piece = units // PIECES
        of_down[which].finish()
        if "down" not in waited:
            waited.add("down")
            made.own_blocks[1].wait()
        for begin in range(which * piece, (which + 1) * piece, TILE):
            for index in range(blocks):
                back_block(begin, index)

    for which in range(PIECES):
        step(functools.partial(back_piece, which))

    def narrow(ref):
        part = pl.ds(0, 3 * cols)
        return ref.at[:, part] if len(ref.shape) == 2 else ref.at[:, :, part]

    def short(ref):
        part = pl.ds(0, cols)
        return ref.at[part, :] if len(ref.shape) == 2 else ref.at[:, part, :]

    def left_terms(left, right):
        def terms(block, part):
            span = aligned(block * TILE + part.start, part.size, 128)
            return contract(left[:, span], right[...], 0, 0)

        return terms

    def right_terms(left, right):
        return lambda block, part: contract(left[:, part], block_cols(right, block), 0, 0)

    wide_staging, tall_staging = Staging(), Staging()
    wide_sends, tall_sends = (wide_far, wide_mid, wide_near), (tall_far, tall_mid, tall_near)
    return_down = GradReturn(
        p, mover, 0, right_terms(hidden, grads), tall_sends, (down_far, down_mid, down_near), tall_loads,
        (tall_staging, tall_stage), down_own,
    )
    return_gate = GradReturn(
        p, mover, 1, left_terms(second, gate_back), wide_sends, (gate_far, gate_mid, gate_near), wide_loads,
        (wide_staging, wide_stage), gate_own,
    )
    return_up = GradReturn(
        p, mover, 1, left_terms(second, up_back), wide_sends, (up_far, up_mid, up_near), wide_loads,
        (wide_staging, wide_stage), up_own, return_gate,
    )
    return_out = GradReturn(
        p, mover, 0, right_terms(mixed, down_here), [short(ref) for ref in tall_sends],
        (out_far, out_mid, out_near), short(tall_loads), (tall_staging, short(tall_stage)), out_own, return_down,
    )
    return_three = GradReturn(
        p, mover, 1, left_terms(grads, three_back), [narrow(ref) for ref in wide_sends],
        (three_far, three_mid, three_near), narrow(wide_loads), (wide_staging, narrow(wide_stage)), three_own,
        return_up,
    )
    returns = [return_down, return_gate, return_up, return_out, return_three]
    for part in returns:
        for which in range(4):
            step(functools.partial(part.across, which))
        for which in range(2):
            for half in range(2):
                step(functools.partial(part.along, which, half))
        for half in range(2):
            step(functools.partial(part.beside, half))
        step(part.own)

    @step
    def _():
        wait_all(made.cot_load)

    @step
    def _():
        normed_grad = back_sum.result()
        give_credit(p, credit)
        inverse = inverse_two[:, :1]
        centred = residual[...] - jnp.mean(residual[...], axis=-1, keepdims=True)
        back_value = grads[my_rows, :].astype(FULL) + norm_backward(
            normed_grad, centred * inverse, inverse
        )
        back_rows[...] = back_value
        rows_low[...] = back_value.astype(LOW)
        view = row_view(back_all)
        made.back_local = mover.here(rows_low, view(p.low, p.chip, p.core))
        made.back = GroupGather(p, mover, view, rows_low)

    relays(lambda: made.back)

    @step
    def _():
        for chunk in chunks:
            chunk.drain()
        made.refill = [mover.here(source, target) for target, source in attended]
        made.refill += load_three(lambda block: qkv_here.at[aligned(block * TILE, TILE), :])

    @step
    def _():
        made.norm_load = mover.here(normed_all, grads)

    @step
    def _():
        made.norm_load.wait()

    @step
    def _():
        made.back.finish()
        made.back_local.wait()
        made.back_load = mover.here(back_all, down_here)

    @step
    def _():
        rows_low[...] = (residual[...] + feed_sum.result()).astype(LOW)
        give_credit(p, credit)
        feed_return.start(rows_low, tokens_out)

    @step
    def _():
        made.back_load.wait()
        wait_all(made.refill)
        for begin in range(0, length, TILE):
            rows = pl.ds(begin, TILE)
            mixed_back[rows, :] = contract(down_here[rows, :], out_here[...], 1, 1).astype(LOW)

    def attend_back(begin):
        rows = pl.ds(begin, TILE)
        keys = begin + TILE
        key_rows = pl.ds(0, keys)
        allowed = allowed_mask(seg_col, seg_row, begin, keys)
        query_parts = []
        for head in range(head_count):
            head_cols = pl.ds(head * HD, HD)
            query_head, key_head = query[rows, head_cols], key[key_rows, head_cols]
            mixed_head = mixed_back[rows, head_cols]
            scores = contract(query_head, key_head, 1, 1) * score_scale
            scores = jnp.where(allowed, scores, NEG_FILL)
            probs = jnp.exp(scores - log_total[rows, pl.ds(head * HD, 1)])
            value_terms = contract(probs.astype(LOW), mixed_head, 0, 0)
            probs_back = contract(mixed_head, value[key_rows, head_cols], 1, 1)
            row_dot = jnp.sum(probs * probs_back, axis=-1, keepdims=True)
            scores_back = (probs * (probs_back - row_dot)).astype(LOW)
            query_parts.append(contract(scores_back, key_head, 1, 0) * score_scale)
            key_terms = contract(scores_back, query_head, 0, 0)
            if keys == length:
                key_sum[key_rows, head_cols] = key_terms
                value_sum[key_rows, head_cols] = value_terms
            else:
                key_sum[key_rows, head_cols] += key_terms
                value_sum[key_rows, head_cols] += value_terms
        three_back[rows, pl.ds(0, cols)] = turn(
            jnp.concatenate(query_parts, axis=1), cosine[rows, :], -sine_part[rows, :]
        ).astype(LOW)

    for block in range(blocks):
        step(functools.partial(attend_back, block * TILE))

    @step
    def _():
        for begin in range(0, length, TILE):
            rows = pl.ds(begin, TILE)
            three_back[rows, pl.ds(cols, cols)] = turn(
                key_sum[rows, :] * score_scale, cosine[rows, :], -sine_part[rows, :]
            ).astype(LOW)
            three_back[rows, pl.ds(2 * cols, cols)] = value_sum[rows, :].astype(LOW)

    @step
    def _():
        kept_normed, inverse = normalise(kept[...].astype(FULL))
        summed = input_sum.result()
        feed_return.finish()
        rows_low[...] = (back_rows[...] + norm_backward(summed, kept_normed, inverse)).astype(LOW)
        row_return.start(rows_low, grad_rows)

    @step
    def _():
        row_return.finish()
        for part in returns:
            part.drain()
        wide_staging.free()
        tall_staging.free()

    run_steps(steps, ORDER)


def whole_layer(tokens_in, out_grad, segment, weights, freqs):
    span, feats = tokens_in.shape[2:]
    length, width = 4 * span, 4 * feats
    cols, units = weights[0].shape[1] // 2, weights[4].shape[1] // 2

    def low(*shape):
        return jax.ShapeDtypeStruct(shape, LOW)

    def full(*shape):
        return jax.ShapeDtypeStruct(shape, FULL)

    wide, tall = (TILE, units), (units, TILE)
    in_hbm = [low(2, 1, span, feats), low(2, 1, span, feats)]
    for block in (tall, wide, wide, (cols, TILE), (TILE, 3 * cols)):
        in_hbm += [full(*block), low(*block)]
    in_hbm += [low(width, 3 * cols)] + [low(length, width)] * 3 + [low(length, cols)] * 4
    for block in (wide, wide, tall, (TILE, 3 * cols), (cols, TILE)):
        in_hbm += [low(4, *block), low(2, *block)]
    vmem = pl.BlockSpec(memory_space=pltpu.VMEM)

    def sending(block):
        return [
            pltpu.VMEM((4, *block), LOW),
            pltpu.VMEM((2, *block), LOW),
            pltpu.VMEM(block, LOW),
            pltpu.VMEM((2, *block), LOW),
            pltpu.VMEM(block, FULL),
        ]

    row_semaphores = [
        pltpu.SemaphoreType.DMA((4,)),
        pltpu.SemaphoreType.DMA((4,)),
        pltpu.SemaphoreType.DMA,
    ]
    outs = pl.pallas_call(
        layer_kernel,
        out_shape=in_hbm,
        in_specs=[HBM] * 9 + [vmem] * 2,
        out_specs=[HBM] * len(in_hbm),
        scratch_shapes=[
            pltpu.VMEM((length, width), LOW),
            pltpu.VMEM((length, width), LOW),
            pltpu.VMEM((width, units), LOW),
            pltpu.VMEM((width, units), LOW),
            pltpu.VMEM((units, width), LOW),
            pltpu.VMEM((2, length, units), LOW),
            pltpu.VMEM((length, units), LOW),
            pltpu.VMEM((cols, width), LOW),
            pltpu.VMEM((length, cols), FULL),
            pltpu.VMEM((length, cols), FULL),
            *sending(wide),
            *sending(tall),
            *scatter_buffers(width),
            pltpu.VMEM((length // 8, width), LOW),
            pltpu.VMEM((length // 8, width), FULL),
            pltpu.VMEM((length // 8, width), FULL),
            pltpu.VMEM((length // 8, HD), FULL),
            pltpu.VMEM((length, cols), FULL),
            *[pltpu.VMEM((length, HD), FULL)] * 3,
            pltpu.VMEM((8, length), FULL),
            pltpu.VMEM((2, 8, span), FULL),
            pltpu.VMEM((length // 8, width), LOW),
            pltpu.SemaphoreType.REGULAR((3,)),
            pltpu.SemaphoreType.DMA((288,)),
            pltpu.SemaphoreType.DMA((288,)),
            pltpu.SemaphoreType.DMA((256,)),
            *row_semaphores,
            *row_semaphores,
        ],
        compiler_params=pltpu.CompilerParams(
            collective_id=1, has_side_effects=True, vmem_limit_bytes=VMEM_BYTES
        ),
    )(tokens_in, out_grad, *weights, segment, freqs)
    return outs[:12]


def hand_over_kernel(*refs):
    tokens_in, grad_in, *halves = refs[:12]
    tokens_out, grad_out, down, gate, up, out, query, key, value = refs[12:21]
    held, own_held, far_held, wide_held = refs[21:23], refs[23:28], refs[28:33], refs[33:39]
    load, save = refs[39:]
    low = lax.axis_index("ctx") % 2
    started, saves = [], []

    def copy(source, target, semaphores, which):
        made = pltpu.make_async_copy(source, target, semaphores.at[len(which)])
        made.start()
        which.append(made)
        return made

    owns = [copy(halves[2 * slot], own_held[slot], load, started) for slot in range(5)]
    fars = [copy(halves[2 * slot + 1], far_held[slot], load, started) for slot in range(5)]
    rows = [copy(ref, here, load, started) for ref, here in zip((tokens_in, grad_in), held)]

    def place(source, targets, axis, which):
        begin = 0
        for target in targets:
            size = target.shape[axis] // 2
            spot, part = aligned(which * size, size), pl.ds(begin, size)
            begin += size
            if axis == 1:
                copy(source.at[:, part], target.at[:, spot], save, saves)
            else:
                copy(source.at[part, :], target.at[spot, :], save, saves)

    goals = (((down,), 0), ((gate,), 1), ((up,), 1), ((out,), 0), ((query, key, value), 1))
    for slot, (targets, axis) in enumerate(goals):
        owns[slot].wait()
        place(own_held[slot], targets, axis, low)
    for slot, (targets, axis) in enumerate(goals):
        fars[slot].wait()
        wide_held[slot][...] = far_held[slot][...].astype(FULL)
        place(wide_held[slot], targets, axis, 1 - low)
    for made in rows:
        made.wait()
    copy(held[0], tokens_out, save, saves)
    wide_held[5][...] = held[1][...].astype(FULL)
    copy(wide_held[5], grad_out, save, saves)
    for made in saves:
        made.wait()


def hand_over(arrays, shapes):
    tokens_out, grad_in, *halves = arrays
    held = [tokens_out, grad_in, *halves[::2], *halves[1::2]]
    return pl.pallas_call(
        hand_over_kernel,
        out_shape=[jax.ShapeDtypeStruct(shape, kind) for shape, kind in shapes],
        in_specs=[HBM] * 12,
        out_specs=[HBM] * len(shapes),
        scratch_shapes=[
            *[pltpu.VMEM(array.shape, array.dtype) for array in held],
            *[pltpu.VMEM(array.shape, FULL) for array in (*halves[1::2], grad_in)],
            pltpu.SemaphoreType.DMA((16,)),
            pltpu.SemaphoreType.DMA((24,)),
        ],
        compiler_params=pltpu.CompilerParams(vmem_limit_bytes=VMEM_BYTES),
    )(tokens_out, grad_in, *halves)


def per_device_grouped(
    tokens_in, out_grad, segment_ids, w_query, w_key, w_value, w_out, w_gate, w_up, w_down
):
    freq_half = np.power(10000.0, -2.0 * np.arange(HD // 2) / HD)
    freqs = np.tile(np.concatenate([freq_half, freq_half]), (8, 1)).astype(np.float32)
    results = whole_layer(
        tokens_in, out_grad, segment_ids, (w_query, w_key, w_value, w_out, w_gate, w_up, w_down), jnp.asarray(freqs)
    )
    full = jnp.float32
    (
        tokens_out, grad_in, grad_down, grad_gate, grad_up, grad_out, grad_query, grad_key, grad_value,
    ) = hand_over(
        results,
        [
            (tokens_in.shape, jnp.bfloat16),
            (tokens_in.shape, full),
            *[
                (weight.shape, full)
                for weight in (w_down, w_gate, w_up, w_out, w_query, w_key, w_value)
            ],
        ],
    )
    return (
        tokens_out,
        grad_in,
        grad_query,
        grad_key,
        grad_value,
        grad_out,
        grad_gate,
        grad_up,
        grad_down,
    )


def solution(mesh):
    in_specs = (
        P(None, "dp", "ctx", "mp"),
        P(None, "dp", "ctx", "mp"),
        P(None, "dp", "ctx"),
        P(("dp", "ctx"), "mp"),
        P(("dp", "ctx"), "mp"),
        P(("dp", "ctx"), "mp"),
        P("mp", ("dp", "ctx")),
        P(("dp", "ctx"), "mp"),
        P(("dp", "ctx"), "mp"),
        P("mp", ("dp", "ctx")),
    )
    out_specs = (
        P(None, "dp", "ctx", "mp"),
        P(None, "dp", "ctx", "mp"),
        P(("dp", "ctx"), "mp"),
        P(("dp", "ctx"), "mp"),
        P(("dp", "ctx"), "mp"),
        P("mp", ("dp", "ctx")),
        P(("dp", "ctx"), "mp"),
        P(("dp", "ctx"), "mp"),
        P("mp", ("dp", "ctx")),
    )
    grouped = mesh.shape["ctx"] == 4 and mesh.shape["mp"] == 4 and mesh.shape["dp"] == 2
    per_device = per_device_grouped if grouped else per_device_general
    return jax.shard_map(
        per_device, mesh=mesh, in_specs=in_specs, out_specs=out_specs, check_vma=False
    )
```
